32 devices in a mesh: dom: 4 (over y, core), feat: 8 (over z, x).
Axes of the slice: x: 2, y: 2, z: 4, core: 2. Of those that a mesh axis runs over, the one named last changes fastest.
Arguments:
- node_feats: bfloat16 [1024, 16384], P('feat', 'dom'), may hold values from -6 to 6
- send_rows: int32 [2048], P('dom'), may hold values from 0 to 4095
- hub_rows: int32 [512], P('dom'), may hold values from 0 to 4095
- tile_dst: int32 [2048], P('dom'), may hold values from 0 to 7
- tile_src: int32 [2048], P('dom'), may hold values from 0 to 39
- tile_count: int32 [4], P('dom'), may hold values from 128 to 512, as said below
- tile_vals: bfloat16 [2048, 128, 128], P('dom'), may hold values from -0.0625 to 0.0625
- w_self: bfloat16 [1024, 1024], P('feat'), may hold values from -0.1875 to 0.1875
- w_neigh: bfloat16 [1024, 1024], P('feat'), may hold values from -0.1875 to 0.1875
- bias_vec: float32 [1024], P('feat'), may hold values from -3 to 3
- cotangent: bfloat16 [1024, 4096], P('feat', 'dom'), may hold values from -6 to 6
Outputs:
- activations: bfloat16 [1024, 4096], P('feat', 'dom')
- grad_feats: float32 [1024, 16384], P('feat', 'dom')
- grad_w_self: float32 [1024, 1024], P('feat')
- grad_w_neigh: float32 [1024, 1024], P('feat')
- grad_bias: float32 [1024], P('feat')
The draws below stay inside these ranges and needn't reach their ends.
Inputs may be any that keep to these rules, and one draw needn't show every extreme that they name: `tile_count`: every partition has at least 128 live slots, and some partition has all 512 live; slots at or past the count are not edges: their tile_vals may hold any values and must be ignored.
All inputs are finite; a program needn't handle non-finite values.
Results may differ from the reference program's by a relative error of at most 0.0075.
Values may be sent and summed in bfloat16 or wider, within the bound.
No kernel may reach another device: no remote copies, remote signals or barrier semaphores. Data moves between devices by JAX's collectives and lax.ppermute only.
A program may use at most 128 MiB of HBM per device.

```python
import jax
import jax.numpy as jnp
from jax import lax

D = 1024
LOC_DEV = 4096
DST_DEV = 1024
BND = 128
HUB_DEV = 128
TILES = 512
TABLE = 5120
SRC = 16384
DST_ALL = 4096
N_DOM = 4


def draw_tile_count(key, part):
    first_key, second_key = jax.random.split(key)
    counts = jax.random.randint(first_key, (N_DOM,), TILES // 4, TILES + 1)
    busiest = jax.random.randint(second_key, (), 0, N_DOM)
    return jnp.where(jnp.arange(N_DOM) == busiest, TILES, counts).astype(jnp.int32)


def touch_ends(result, key, least, high):
    place = [jax.random.randint(jax.random.fold_in(key, axis), (), 0, length) for axis, length in enumerate(result.shape)]
    longest = result.shape.index(max(result.shape))
    beside = place[:longest] + [(place[longest] + 1) % result.shape[longest]] + place[longest + 1:]
    return result.at[tuple(place)].set(least).at[tuple(beside)].set(high)


def levels(rng, shape, shards, low, top_value):
    gain = 1.0
    for axis_at, blocks in shards:
        steps = jax.random.uniform(jax.random.fold_in(jax.random.fold_in(rng, 6), axis_at), (blocks,), jnp.float32, low / len(shards), top_value / len(shards))
        gain = gain * jnp.repeat(jnp.exp(steps), shape[axis_at] // blocks).reshape((-1,) + (1,) * (len(shape) - 1 - axis_at))
    return gain


def bell_draw(own_key, shape, deviation, reach, shards=(), kind=jnp.bfloat16):
    drawn = deviation * jax.random.normal(own_key, shape, jnp.float32)
    if shards:
        drawn = drawn * levels(own_key, shape, shards, -0.22, 0.18)
    return jnp.clip(drawn, -reach, reach).astype(kind)


def setup_inputs(seed: int = 0) -> dict:
    seeds = jax.random.split(jax.random.key(seed), 12)
    node_feats = bell_draw(seeds[0], (D, SRC), 1.0, 6.0, ((0, 8), (1, 4)))
    send_rows = touch_ends(jax.random.randint(seeds[1], (N_DOM * N_DOM * BND,), 0, LOC_DEV), jax.random.fold_in(seeds[1], 1), 0, LOC_DEV - 1).astype(jnp.int32)
    hub_rows = touch_ends(jax.random.randint(seeds[2], (N_DOM * HUB_DEV,), 0, LOC_DEV), jax.random.fold_in(seeds[2], 1), 0, LOC_DEV - 1).astype(jnp.int32)
    tile_dst = touch_ends(jax.random.randint(seeds[3], (N_DOM * TILES,), 0, DST_DEV // 128), jax.random.fold_in(seeds[3], 1), 0, (DST_DEV // 128) - 1).astype(jnp.int32)
    tile_src = touch_ends(jax.random.randint(seeds[4], (N_DOM * TILES,), 0, TABLE // 128), jax.random.fold_in(seeds[4], 1), 0, (TABLE // 128) - 1).astype(jnp.int32)
    tile_count = draw_tile_count(jax.random.fold_in(seeds[11], 71), 0)
    tile_vals = bell_draw(seeds[6], (N_DOM * TILES, 128, 128), (128 * TILES * 128 // DST_DEV) ** -0.5, 0.0625, ((0, 4),))
    w_self = bell_draw(seeds[7], (D, D), D ** -0.5, 0.1875, ((0, 8),))
    w_neigh = bell_draw(seeds[8], (D, D), D ** -0.5, 0.1875, ((0, 8),))
    bias_vec = bell_draw(seeds[9], (D,), 0.5, 3.0, ((0, 8),), jnp.float32)
    cotangent = bell_draw(seeds[10], (D, DST_ALL), 1.0, 6.0, ((0, 8), (1, 4)))
    return {"node_feats": node_feats, "send_rows": send_rows, "hub_rows": hub_rows, "tile_dst": tile_dst, "tile_src": tile_src, "tile_count": tile_count, "tile_vals": tile_vals, "w_self": w_self, "w_neigh": w_neigh, "bias_vec": bias_vec, "cotangent": cotangent}


def take_cols(columns, indices):
    return jnp.take(columns, indices, axis=1)


def add_cols(grads, indices, values):
    return grads.at[:, indices].add(values)


def reference(node_feats, send_rows, hub_rows, tile_dst, tile_src, tile_count, tile_vals, w_self, w_neigh, bias_vec, cotangent):
    tile_total = TABLE // 128
    dst_tiles = DST_DEV // 128
    parts = node_feats.reshape(D, N_DOM, LOC_DEV).transpose(1, 0, 2)
    sends = send_rows.reshape(N_DOM, N_DOM * BND)
    hubs = hub_rows.reshape(N_DOM, HUB_DEV)
    sent_cols = jax.vmap(take_cols)(parts, sends)
    halo_in = sent_cols.reshape(N_DOM, D, N_DOM, BND).transpose(2, 1, 0, 3).reshape(N_DOM, D, N_DOM * BND)
    hub_cols = jax.vmap(take_cols)(parts, hubs).transpose(1, 0, 2).reshape(D, N_DOM * HUB_DEV)
    dsts = tile_dst.reshape(N_DOM, TILES)
    srcs = tile_src.reshape(N_DOM, TILES)
    vals = tile_vals.reshape(N_DOM, TILES, 128, 128)

    def forward_part(items):
        owned, halo, dst_ids, src_ids, count, values = items
        source_table = jnp.concatenate([owned, halo, hub_cols], axis=1)
        live_mask = (jnp.arange(TILES) < count).astype(jnp.float32)
        dst_hot = (dst_ids[:, None] == jnp.arange(dst_tiles)[None, :]).astype(jnp.float32) * live_mask[:, None]
        picked = source_table.reshape(D, tile_total, 128)[:, src_ids, :]
        products = jnp.einsum("fkj,kij->fki", picked.astype(jnp.float32), values.astype(jnp.float32), precision=lax.Precision.HIGHEST)
        summed = jnp.einsum("fki,ku->fui", products, dst_hot, precision=lax.Precision.HIGHEST)
        return summed.reshape(D, DST_DEV).astype(jnp.bfloat16)

    aggs = lax.map(forward_part, (parts, halo_in, dsts, srcs, tile_count, vals))
    agg_whole = aggs.transpose(1, 0, 2).reshape(D, DST_ALL)
    dst_feats = parts[:, :, :DST_DEV].transpose(1, 0, 2).reshape(D, DST_ALL)
    pre_act = jnp.dot(w_self, dst_feats, preferred_element_type=jnp.float32) + jnp.dot(w_neigh, agg_whole, preferred_element_type=jnp.float32) + bias_vec[:, None]
    sig_val = jax.nn.sigmoid(pre_act)
    activations = (pre_act * sig_val).astype(jnp.bfloat16)
    grad_pre = (cotangent.astype(jnp.float32) * sig_val * (1.0 + pre_act * (1.0 - sig_val))).astype(jnp.bfloat16)
    grad_w_self = jnp.dot(grad_pre, dst_feats.T, preferred_element_type=jnp.float32)
    grad_w_neigh = jnp.dot(grad_pre, agg_whole.T, preferred_element_type=jnp.float32)
    grad_bias = jnp.sum(grad_pre.astype(jnp.float32), axis=1)
    grad_self_in = jnp.dot(w_self.T, grad_pre, preferred_element_type=jnp.float32)
    grad_agg = jnp.dot(w_neigh.T, grad_pre, preferred_element_type=jnp.float32).astype(jnp.bfloat16)
    grad_aggs = grad_agg.reshape(D, N_DOM, DST_DEV).transpose(1, 0, 2)

    def backward_part(items):
        upstream_all, dst_ids, src_ids, count, values = items
        live_mask = (jnp.arange(TILES) < count).astype(jnp.float32)
        src_hot = (src_ids[:, None] == jnp.arange(tile_total)[None, :]).astype(jnp.float32) * live_mask[:, None]
        upstream = upstream_all.reshape(D, dst_tiles, 128)[:, dst_ids, :]
        back_terms = jnp.einsum("fki,kij->fkj", upstream.astype(jnp.float32), values.astype(jnp.float32), precision=lax.Precision.HIGHEST)
        placed = jnp.einsum("fkj,kt->ftj", back_terms, src_hot, precision=lax.Precision.HIGHEST)
        return placed.reshape(D, TABLE)

    grad_tables = lax.map(backward_part, (grad_aggs, dsts, srcs, tile_count, vals))
    owned_grad = grad_tables[:, :, :LOC_DEV]
    halo_grad = grad_tables[:, :, LOC_DEV:LOC_DEV + N_DOM * BND].reshape(N_DOM, D, N_DOM, BND)
    halo_back = halo_grad.transpose(2, 1, 0, 3).reshape(N_DOM, D, N_DOM * BND)
    hub_grad = grad_tables[:, :, LOC_DEV + N_DOM * BND:].reshape(N_DOM, D, N_DOM, HUB_DEV)
    hub_back = jnp.sum(hub_grad, axis=0).transpose(1, 0, 2)
    grads = jax.vmap(add_cols)(owned_grad, sends, halo_back)
    grads = jax.vmap(add_cols)(grads, hubs, hub_back)
    grads = grads.at[:, :, :DST_DEV].add(grad_self_in.reshape(D, N_DOM, DST_DEV).transpose(1, 0, 2))
    grad_feats = grads.transpose(1, 0, 2).reshape(D, SRC)
    return (activations, grad_feats, grad_w_self, grad_w_neigh, grad_bias)
```

```python
import functools

import jax
import jax.numpy as jnp
from jax import lax
from jax.experimental import pallas as pl
from jax.experimental.pallas import tpu as pltpu
from jax.sharding import Mesh, PartitionSpec as P

T = 128
BF = jnp.bfloat16
F32 = jnp.float32
MIB = 1 << 20


def dot(left, right, dims):
    return lax.dot_general(left, right, (dims, ((), ())), preferred_element_type=F32)


def params(mib):
    return pltpu.CompilerParams(vmem_limit_bytes=mib * MIB)


def gather_kernel(x_ref, idx_ref, out_ref):
    readers = out_ref.shape[0]
    x = x_ref[...]
    rows = lax.broadcasted_iota(jnp.int32, (x.shape[1], T), 0)
    for q in range(readers + 1):
        hot = (rows == idx_ref[q : q + 1, :]).astype(F32).astype(BF)
        got = dot(x, hot, ((1,), (0,))).astype(BF)
        if q < readers:
            out_ref[q, :, :T] = got
        else:
            for r in range(readers):
                out_ref[r, :, T:] = got


def gather_cols(x, idx):
    readers = idx.shape[0] - 1
    return pl.pallas_call(
        gather_kernel,
        out_shape=jax.ShapeDtypeStruct((readers, x.shape[0], 2 * T), BF),
        in_specs=[pl.BlockSpec(memory_space=pltpu.VMEM)] * 2,
        out_specs=pl.BlockSpec(memory_space=pltpu.VMEM),
        compiler_params=params(40),
        name="gather_cols",
    )(x, idx)


def build_kernel(per, n_src, n_own, pos_ref, count_ref, vals_ref, own_ref, ext_ref, acc_ref):
    step = pl.program_id(0)
    blocks = pos_ref.shape[0] // per

    @pl.when(step == 0)
    def _():
        def clear(i, c):
            acc_ref[i] = jnp.zeros((T, T), F32)
            return c

        lax.fori_loop(0, acc_ref.shape[0], clear, 0, unroll=4)

    @pl.when(step < blocks)
    def _():
        live = jnp.clip(count_ref[0] - step * per, 0, per)

        def add(i, c):
            at = pos_ref[step * per + i]
            acc_ref[at] += vals_ref[i].astype(F32)
            return c

        lax.fori_loop(0, live, add, 0)

    @pl.when(step >= blocks)
    def _():
        u = step - blocks
        for s in range(n_src):
            tile = acc_ref[u * n_src + s].astype(BF)
            if s < n_own:
                own_ref[:, s * T : (s + 1) * T] = tile
            else:
                ext_ref[:, (s - n_own) * T : (s - n_own + 1) * T] = tile


def build_dense(vals, pos, count, n_dst, n_src, n_own):
    per = 32
    slots = vals.shape[0]
    blocks = slots // per

    def vals_map(i, pos, count):
        return (jnp.minimum(i, (count[0] - 1) // per), 0, 0)

    def out_map(i, pos, count):
        return (jnp.maximum(i - blocks, 0), 0)

    return pl.pallas_call(
        functools.partial(build_kernel, per, n_src, n_own),
        out_shape=(
            jax.ShapeDtypeStruct((n_dst * T, n_own * T), BF),
            jax.ShapeDtypeStruct((n_dst * T, (n_src - n_own) * T), BF),
        ),
        grid_spec=pltpu.PrefetchScalarGridSpec(
            num_scalar_prefetch=2,
            grid=(blocks + n_dst,),
            in_specs=[pl.BlockSpec((per, T, T), vals_map)],
            out_specs=[
                pl.BlockSpec((T, n_own * T), out_map),
                pl.BlockSpec((T, (n_src - n_own) * T), out_map),
            ],
            scratch_shapes=[pltpu.VMEM((n_dst * n_src, T, T), F32)],
        ),
        compiler_params=params(48),
        cost_estimate=pl.CostEstimate(flops=0, bytes_accessed=slots * T * T * 2 * 2, transcendentals=0),
        name="build_dense",
    )(pos, count, vals)


def middle_kernel(w_ref, xc_ref, agg_ref, bias_ref, act_ref, g_ref, gagg_ref, gself_ref):
    groups, sub = w_ref.shape[0], w_ref.shape[1] // 2
    width = w_ref.shape[2]
    rows = groups * sub
    w_self = w_ref[:, :sub, :].reshape(rows, width)
    w_neigh = w_ref[:, sub:, :].reshape(rows, width)
    bias = bias_ref[...]
    for p in range(agg_ref.shape[0]):
        pre = dot(w_self, xc_ref[p, :width, :], ((1,), (0,)))
        pre += dot(w_neigh, agg_ref[p], ((1,), (0,)))
        pre += bias
        sig = 1.0 / (1.0 + jnp.exp(-pre))
        act_ref[p] = (pre * sig).astype(BF)
        cot = xc_ref[p, width:, :].astype(F32)
        grad = (cot * sig * (1.0 + pre * (1.0 - sig))).astype(BF)
        g_ref[p] = grad
        gagg_ref[p] = dot(w_neigh, grad, ((0,), (0,))).astype(BF)
        gself_ref[p] = dot(w_self, grad, ((0,), (0,))).astype(BF)


def middle(w, xc, agg, bias):
    parts, width, n = agg.shape
    rows = w.shape[0] * w.shape[1] // 2
    small = jax.ShapeDtypeStruct((parts, rows, n), BF)
    large = jax.ShapeDtypeStruct((parts, width, n), BF)
    return pl.pallas_call(
        middle_kernel,
        out_shape=(small, small, large, large),
        in_specs=[pl.BlockSpec(memory_space=pltpu.VMEM)] * 4,
        out_specs=[pl.BlockSpec(memory_space=pltpu.VMEM)] * 4,
        compiler_params=params(48),
        name="middle",
    )(w, xc, agg, bias)


def wgrad_kernel(g_ref, xc_ref, agg_ref, out_ref):
    parts, rows, _ = g_ref.shape
    width = agg_ref.shape[1]
    groups, sub, _ = out_ref.shape
    own = jnp.zeros((rows, width), F32)
    neigh = jnp.zeros((rows, width), F32)
    total = jnp.zeros((rows, 1), F32)
    for p in range(parts):
        grad = g_ref[p]
        own += dot(grad, xc_ref[p, :width, :], ((1,), (1,)))
        neigh += dot(grad, agg_ref[p], ((1,), (1,)))
        total += jnp.sum(grad.astype(F32), axis=1, keepdims=True)
    out_ref[:, :, :width] = own.astype(BF).reshape(groups, sub, width)
    out_ref[:, :, width : 2 * width] = neigh.astype(BF).reshape(groups, sub, width)
    high = total.astype(BF).astype(F32)
    lane = lax.broadcasted_iota(jnp.int32, (rows, T), 1)
    both = jnp.where(lane == 0, high, jnp.where(lane == 1, total - high, 0.0))
    out_ref[:, :, 2 * width :] = both.astype(BF).reshape(groups, sub, T)


def wgrad(g, xc, agg, groups):
    rows, width = g.shape[1], agg.shape[1]
    return pl.pallas_call(
        wgrad_kernel,
        out_shape=jax.ShapeDtypeStruct((groups, rows // groups, 2 * width + T), BF),
        in_specs=[pl.BlockSpec(memory_space=pltpu.VMEM)] * 3,
        out_specs=pl.BlockSpec(memory_space=pltpu.VMEM),
        compiler_params=params(48),
        name="wgrad",
    )(g, xc, agg)


def finish_kernel(dst_blocks, base_ref, ret_ref, idx_ref, gself_ref, out_ref):
    step = pl.program_id(0)
    readers, _, k = ret_ref.shape
    width = out_ref.shape[1]
    cols = lax.broadcasted_iota(jnp.int32, (k, width), 1) + step * width
    total = base_ref[...]
    for q in range(readers):
        hot = (cols == idx_ref[q]).astype(F32).astype(BF)
        total += dot(ret_ref[q], hot, ((1,), (0,)))
    own = gself_ref[...].astype(F32)
    out_ref[...] = total + jnp.where(step < dst_blocks, own, 0.0)


def finish(base, ret, idx, gself):
    rows, n = base.shape
    width = 512
    dst_blocks = gself.shape[1] // width
    return pl.pallas_call(
        functools.partial(finish_kernel, dst_blocks),
        out_shape=jax.ShapeDtypeStruct((rows, n), F32),
        grid=(n // width,),
        in_specs=[
            pl.BlockSpec((rows, width), lambda i: (0, i)),
            pl.BlockSpec(ret.shape, lambda i: (0, 0, 0)),
            pl.BlockSpec(idx.shape, lambda i: (0, 0, 0)),
            pl.BlockSpec((rows, width), lambda i: (0, jnp.minimum(i, dst_blocks - 1))),
        ],
        out_specs=pl.BlockSpec((rows, width), lambda i: (0, i)),
        compiler_params=params(40),
        name="finish",
    )(base, ret, idx, gself)


def body(
    node_feats,
    send_rows,
    hub_rows,
    tile_dst,
    tile_src,
    tile_count,
    tile_vals,
    w_self,
    w_neigh,
    bias_vec,
    cotangent,
):
    dom = ("c", "y")
    n_dom = lax.axis_size("y") * lax.axis_size("c")
    n_feat = lax.axis_size("feat")
    rows = node_feats.shape[0]
    own_rows = node_feats.shape[1]
    dst_rows = cotangent.shape[1]
    width = w_self.shape[1]
    n_own, n_dst = own_rows // T, dst_rows // T
    n_src = n_own + 2 * n_dom
    piece = dst_rows // n_feat
    sub = w_self.shape[0] // n_dom
    d = lax.axis_index(dom)

    halo_tile = n_own + 2 * (tile_src - n_own)
    hub_tile = n_own + 2 * (tile_src - n_own - n_dom) + 1
    place = jnp.where(
        tile_src < n_own, tile_src, jnp.where(tile_src < n_own + n_dom, halo_tile, hub_tile)
    )
    pos = tile_dst * n_src + place
    idx = jnp.concatenate([send_rows.reshape(n_dom, T), hub_rows[None, :]], axis=0)
    outgoing = gather_cols(node_feats, idx)
    incoming = lax.all_to_all(outgoing, ("y", "c"), 0, 0, tiled=True)

    high = bias_vec.astype(BF)
    low = (bias_vec - high.astype(F32)).astype(BF)
    bias_rows = jnp.pad(jnp.stack([high, low]), ((0, 14), (0, 0)))

    def by_piece(x):
        return x.reshape(rows, n_feat, piece).transpose(1, 0, 2)

    xc = jnp.concatenate(
        [
            by_piece(node_feats[:, :dst_rows]),
            by_piece(cotangent),
            jnp.broadcast_to(bias_rows[None], (n_feat, 16, rows)),
        ],
        axis=1,
    )
    xc = lax.all_to_all(xc, "feat", 0, 0, tiled=True)

    mine = jnp.concatenate(
        [
            lax.dynamic_slice_in_dim(w_self, d * sub, sub, axis=0),
            lax.dynamic_slice_in_dim(w_neigh, d * sub, sub, axis=0),
        ],
        axis=0,
    )
    w_part = lax.all_to_all(
        jnp.broadcast_to(mine[None], (n_feat, 2 * sub, width)), "feat", 0, 0, tiled=True
    )

    a_own, a_ext = build_dense(tile_vals, pos, tile_count, n_dst, n_src, n_own)
    agg_own = dot(node_feats, a_own, ((1,), (1,)))

    x_all = xc[:, :rows, :].reshape(1, width, piece)
    cot = xc[:, rows : 2 * rows, :].reshape(n_feat, n_dom, sub, piece).transpose(1, 0, 2, 3)
    xc_dom = jnp.concatenate(
        [
            jnp.broadcast_to(x_all, (n_dom, width, piece)),
            cot.reshape(n_dom, n_feat * sub, piece),
        ],
        axis=1,
    )
    xc_dom = lax.all_to_all(xc_dom, dom, 0, 0, tiled=True)
    bias = xc[:, 2 * rows, :].astype(F32) + xc[:, 2 * rows + 1, :].astype(F32)
    bias = lax.dynamic_slice_in_dim(bias, d * sub, sub, axis=1).reshape(n_feat * sub, 1)

    halo = incoming.transpose(1, 0, 2).reshape(rows, 2 * n_dom * T)
    agg = (agg_own + dot(halo, a_ext, ((1,), (1,)))).astype(BF)
    agg = lax.all_to_all(by_piece(agg), "feat", 0, 0, tiled=True)
    agg = agg.reshape(1, width, piece)
    agg = lax.all_gather(agg, "y", axis=0, tiled=True)
    agg = lax.all_gather(agg, "c", axis=0, tiled=True)

    act, grad, gagg, gself = middle(w_part, xc_dom, agg, bias)

    gagg = lax.all_to_all(gagg, dom, 0, 0, tiled=True)
    gagg = jnp.sum(gagg.astype(F32), axis=0).astype(BF)
    gagg = lax.all_to_all(gagg.reshape(n_feat, rows, piece), "feat", 0, 0, tiled=True)
    gagg = gagg.transpose(1, 0, 2).reshape(rows, dst_rows)

    halo_grad = dot(gagg, a_ext, ((1,), (0,))).astype(BF)
    halo_grad = halo_grad.reshape(rows, n_dom, 2 * T).transpose(1, 0, 2)
    returned = lax.all_to_all(halo_grad, ("y", "c"), 0, 0, tiled=True)
    base = dot(gagg, a_own, ((1,), (0,)))

    parts = wgrad(grad, xc_dom, agg, n_feat)
    parts = lax.all_to_all(parts, "feat", 0, 0, tiled=True)
    parts = jnp.sum(parts.astype(F32), axis=0)

    back = lax.all_to_all(jnp.concatenate([gself, act], axis=1), dom, 0, 0, tiled=True)
    own = jnp.sum(back[:, :width, :].astype(F32), axis=0).astype(BF).reshape(n_feat, rows, piece)
    act = back[:, width:, :].reshape(n_dom, n_feat, sub, piece).transpose(1, 0, 2, 3)
    back = jnp.concatenate([own, act.reshape(n_feat, rows, piece)], axis=1)
    back = lax.all_to_all(back, "feat", 0, 0, tiled=True)
    gself = back[:, :rows, :].transpose(1, 0, 2).reshape(rows, dst_rows)
    activations = back[:, rows:, :].transpose(1, 0, 2).reshape(rows, dst_rows)

    ret_idx = jnp.concatenate(
        [send_rows.reshape(n_dom, T), jnp.broadcast_to(hub_rows[None], (n_dom, T))], axis=1
    )
    grad_feats = finish(base, returned, ret_idx[:, :, None], gself)

    bias_grad = parts[:, 2 * width] + parts[:, 2 * width + 1]
    bias_high = bias_grad.astype(BF).astype(F32)
    tail = jnp.stack([bias_high, bias_grad - bias_high], axis=1)
    parts = jnp.concatenate([parts[:, : 2 * width], jnp.pad(tail, ((0, 0), (0, T - 2)))], axis=1)
    whole = lax.all_gather(parts.astype(BF), "y", axis=0, tiled=True)
    whole = lax.all_gather(whole, "c", axis=0, tiled=True).astype(F32)
    grad_bias = whole[:, 2 * width] + whole[:, 2 * width + 1]
    return (activations, grad_feats, whole[:, :width], whole[:, width : 2 * width], grad_bias)


def solution(mesh):
    n_dom, n_feat = mesh.devices.shape
    fine = Mesh(mesh.devices.reshape(n_dom // 2, 2, n_feat), ("y", "c", "feat"))
    dom = ("y", "c")
    return jax.shard_map(
        body,
        mesh=fine,
        in_specs=(
            P("feat", dom),
            P(dom),
            P(dom),
            P(dom),
            P(dom),
            P(dom),
            P(dom, None, None),
            P("feat", None),
            P("feat", None),
            P("feat"),
            P("feat", dom),
        ),
        out_specs=(P("feat", dom), P("feat", dom), P("feat", None), P("feat", None), P("feat")),
        check_vma=False,
    )
```

```python
import functools

import jax
import jax.numpy as jnp
from jax import lax
from jax.experimental import pallas as pl
from jax.experimental.pallas import tpu as pltpu
from jax.sharding import PartitionSpec as P

T = 128
BF = jnp.bfloat16
F32 = jnp.float32
MIB = 1 << 20
VMEM = pl.BlockSpec(memory_space=pltpu.VMEM)
SMEM = pl.BlockSpec(memory_space=pltpu.SMEM)


def dot(left, right, dims):
    return lax.dot_general(left, right, (dims, ((), ())), preferred_element_type=F32)


def params(mib):
    return pltpu.CompilerParams(vmem_limit_bytes=mib * MIB)


def cost(micros):
    return pl.CostEstimate(flops=0, bytes_accessed=int(micros * 3.0e6), transcendentals=0)


def shape(*dims, kind=BF):
    return jax.ShapeDtypeStruct(dims, kind)


def gather_kernel(x_ref, idx_ref, *out_refs):
    x = x_ref[...]
    rows = lax.broadcasted_iota(jnp.int32, (x.shape[1], T), 0)
    readers = len(out_refs)
    for q in range(readers + 1):
        hot = (rows == idx_ref[q : q + 1, :]).astype(F32).astype(BF)
        got = dot(x, hot, ((1,), (0,))).astype(BF)
        if q < readers:
            out_refs[q][:, :T] = got
        else:
            for r in range(readers):
                out_refs[r][:, T:] = got


def gather_cols(x, idx):
    readers = idx.shape[0] - 1
    return pl.pallas_call(
        gather_kernel,
        out_shape=[shape(x.shape[0], 2 * T)] * readers,
        in_specs=[VMEM] * 2,
        out_specs=[VMEM] * readers,
        compiler_params=params(40),
        cost_estimate=cost(2.5),
        name="gather_cols",
    )(x, idx)


def build_kernel(n_own, order_ref, start_ref, x_ref, vals_hbm, own_ref, ext_ref, agg_ref, vals, sems):
    u = pl.program_id(0)
    slots = vals_hbm.shape[0]
    n_src = n_own + ext_ref.shape[1] // T
    chunks = sems.shape[0]
    per = slots // chunks

    def piece(i):
        span = pl.ds(i * per, per)
        return pltpu.make_async_copy(vals_hbm.at[span], vals.at[span], sems.at[i])

    @pl.when(u == 0)
    def _():
        for i in range(chunks):
            piece(i).start()
        vals[slots] = jnp.zeros((T, T), BF)
        for i in range(chunks):
            piece(i).wait()

    for s in range(n_src):
        p = u * n_src + s
        first, last = start_ref[p], start_ref[p + 1]
        one = jnp.where(last > first, order_ref[first], slots)
        two = jnp.where(last > first + 1, order_ref[first + 1], slots)
        total = vals[one].astype(F32) + vals[two].astype(F32)

        def more(i, total):
            return total + vals[order_ref[i]].astype(F32)

        total = lax.fori_loop(first + 2, last, more, total).astype(BF)
        if s < n_own:
            own_ref[:, s * T : (s + 1) * T] = total
        else:
            ext_ref[:, (s - n_own) * T : (s - n_own + 1) * T] = total
    agg_ref[...] = dot(x_ref[...], own_ref[...], ((1,), (1,)))


def build_dense(vals, order, start, x, n_dst, n_src, n_own):
    slots = vals.shape[0]
    chunks = 8
    return pl.pallas_call(
        functools.partial(build_kernel, n_own),
        out_shape=(
            shape(n_dst * T, n_own * T),
            shape(n_dst * T, (n_src - n_own) * T),
            shape(x.shape[0], n_dst * T, kind=F32),
        ),
        grid_spec=pltpu.PrefetchScalarGridSpec(
            num_scalar_prefetch=2,
            grid=(n_dst,),
            in_specs=[
                pl.BlockSpec(x.shape, lambda u, *_: (0, 0)),
                pl.BlockSpec(memory_space=pl.ANY),
            ],
            out_specs=[
                pl.BlockSpec((T, n_own * T), lambda u, *_: (u, 0)),
                pl.BlockSpec((T, (n_src - n_own) * T), lambda u, *_: (u, 0)),
                pl.BlockSpec((x.shape[0], T), lambda u, *_: (0, u)),
            ],
            scratch_shapes=[
                pltpu.VMEM((slots + 1, T, T), BF),
                pltpu.SemaphoreType.DMA((chunks,)),
            ],
        ),
        compiler_params=params(40),
        cost_estimate=cost(14.0),
        name="build_dense",
    )(order, start, x, vals)


def halo_kernel(own_ref, ext_ref, *refs):
    *in_refs, out_ref = refs
    total = own_ref[...]
    halo = jnp.concatenate([r[...] for r in in_refs], axis=1)
    total = (total + dot(halo, ext_ref[...], ((1,), (1,)))).astype(BF)
    piece = out_ref.shape[2]
    for b in range(out_ref.shape[0]):
        out_ref[b] = total[:, b * piece : (b + 1) * piece]


def add_halo(own, ext, halos, n_feat):
    rows, n = own.shape
    return pl.pallas_call(
        halo_kernel,
        out_shape=shape(n_feat, rows, n // n_feat),
        in_specs=[VMEM] * (2 + len(halos)),
        out_specs=VMEM,
        compiler_params=params(40),
        cost_estimate=cost(2.0),
        name="add_halo",
    )(own, ext, *halos)


def middle_kernel(ny, small, w_ref, bias_ref, *refs):
    even, odd = refs[:ny], refs[ny : 2 * ny]
    agg = refs[2 * ny : 4 * ny]
    g_ref, gagg_even, gagg_odd, back_even, back_odd = refs[4 * ny :]
    width = w_ref.shape[2]
    w_self, w_neigh = w_ref[0], w_ref[1]
    bias = bias_ref[...]
    for k in range(2 * ny):
        j = k // 2
        if k % 2 == 0:
            cot, x = even[j][:small, :], even[j][small : small + width, :]
            gagg_ref, back_ref = gagg_even, back_even
        else:
            x, cot = odd[j][:width, :], odd[j][width:, :]
            gagg_ref, back_ref = gagg_odd, back_odd
        pre = dot(w_self, x, ((1,), (0,)))
        pre += dot(w_neigh, agg[k][...], ((1,), (0,)))
        pre += bias
        sig = 1.0 / (1.0 + jnp.exp(-pre))
        back_ref[j, width:, :] = (pre * sig).astype(BF)
        grad = (cot.astype(F32) * sig * (1.0 + pre * (1.0 - sig))).astype(BF)
        g_ref[k] = grad
        gagg_ref[j] = dot(w_neigh, grad, ((0,), (0,))).astype(BF)
        back_ref[j, :width, :] = dot(w_self, grad, ((0,), (0,))).astype(BF)


def middle(w, bias, even, odd, agg):
    ny, width, small = len(even), w.shape[2], w.shape[1]
    n = agg[0].shape[1]
    return pl.pallas_call(
        functools.partial(middle_kernel, ny, small),
        out_shape=[
            shape(2 * ny, small, n),
            shape(ny, width, n),
            shape(ny, width, n),
            shape(ny, width + small, n),
            shape(ny, width + small, n),
        ],
        in_specs=[VMEM] * (2 + 4 * ny),
        out_specs=[VMEM] * 5,
        compiler_params=params(40),
        cost_estimate=cost(3.0),
        name="middle",
    )(w, bias, *even, *odd, *agg)


def wgrad_kernel(ny, small, me_ref, g_ref, *refs):
    even, odd = refs[:ny], refs[ny : 2 * ny]
    agg = refs[2 * ny : 4 * ny]
    out_ref = refs[4 * ny]
    width = agg[0].shape[0]
    sub = out_ref.shape[2]
    xs = []
    for k in range(2 * ny):
        ref = odd[k // 2] if k % 2 else even[k // 2]
        xs.append(ref[:width, :] if k % 2 else ref[small : small + width, :])
    grad = jnp.concatenate([g_ref[k] for k in range(2 * ny)], axis=1)
    own = dot(grad, jnp.concatenate(xs, axis=1), ((1,), (1,))).astype(BF)
    neigh = dot(grad, jnp.concatenate([r[...] for r in agg], axis=1), ((1,), (1,))).astype(BF)
    total = jnp.sum(grad.astype(F32), axis=1, keepdims=True)
    high = total.astype(BF).astype(F32)
    lane = lax.broadcasted_iota(jnp.int32, (small, T), 1)
    both = jnp.where(lane == 0, high, jnp.where(lane == 1, total - high, 0.0)).astype(BF)
    for i in range(small // sub):
        k = me_ref[0] ^ i
        rows = slice(i * sub, (i + 1) * sub)
        out_ref[k % 2, k // 2, :, :width] = own[rows]
        out_ref[k % 2, k // 2, :, width : 2 * width] = neigh[rows]
        out_ref[k % 2, k // 2, :, 2 * width :] = both[rows]


def wgrad(me, g, even, odd, agg, groups):
    ny, width, small = len(even), agg[0].shape[0], g.shape[1]
    return pl.pallas_call(
        functools.partial(wgrad_kernel, ny, small),
        out_shape=shape(2, groups // 2, small // groups, 2 * width + T),
        in_specs=[SMEM] + [VMEM] * (1 + 4 * ny),
        out_specs=VMEM,
        compiler_params=params(40),
        cost_estimate=cost(2.5),
        name="wgrad",
    )(me, g, *even, *odd, *agg)


def halo_grad_kernel(ga_ref, ext_ref, flat_ref, *out_refs):
    ga = jnp.concatenate([ga_ref[b] for b in range(ga_ref.shape[0])], axis=1)
    flat_ref[...] = ga
    for k, out_ref in enumerate(out_refs):
        span = slice(k * 2 * T, (k + 1) * 2 * T)
        out_ref[...] = dot(ga, ext_ref[:, span], ((1,), (0,))).astype(BF)


def halo_grads(ga, ext, n_dom):
    groups, rows, piece = ga.shape
    return pl.pallas_call(
        halo_grad_kernel,
        out_shape=[shape(rows, groups * piece)] + [shape(rows, 2 * T)] * n_dom,
        in_specs=[VMEM] * 2,
        out_specs=[VMEM] * (1 + n_dom),
        compiler_params=params(40),
        cost_estimate=cost(2.0),
        name="halo_grads",
    )(ga, ext)


def finish_kernel(dst_blocks, base_ref, idx_ref, gself_ref, *refs):
    *ret_refs, out_ref = refs
    step = pl.program_id(0)
    width = out_ref.shape[1]
    total = base_ref[...]
    cols = lax.broadcasted_iota(jnp.int32, (2 * T, width), 1) + step * width
    for q, ret_ref in enumerate(ret_refs):
        hot = (cols == idx_ref[q]).astype(F32).astype(BF)
        total += dot(ret_ref[...], hot, ((1,), (0,)))
    own = gself_ref[...].astype(F32)
    out_ref[...] = total + jnp.where(step < dst_blocks, own, 0.0)


def finish(base, ret, idx, gself):
    rows, n = base.shape
    width = 512
    dst_blocks = gself.shape[1] // width
    return pl.pallas_call(
        functools.partial(finish_kernel, dst_blocks),
        out_shape=shape(rows, n, kind=F32),
        grid=(n // width,),
        in_specs=[
            pl.BlockSpec((rows, width), lambda i: (0, i)),
            pl.BlockSpec(idx.shape, lambda i: (0, 0, 0)),
            pl.BlockSpec((rows, width), lambda i: (0, jnp.minimum(i, dst_blocks - 1))),
        ]
        + [pl.BlockSpec((rows, 2 * T), lambda i: (0, 0))] * len(ret),
        out_specs=pl.BlockSpec((rows, width), lambda i: (0, i)),
        compiler_params=params(40),
        cost_estimate=cost(5.0),
        name="finish",
    )(base, idx, gself, *ret)


def body(
    node_feats,
    send_rows,
    hub_rows,
    tile_dst,
    tile_src,
    tile_count,
    tile_vals,
    w_self,
    w_neigh,
    bias_vec,
    cotangent,
):
    n_dom = lax.axis_size("dom")
    n_feat = lax.axis_size("feat")
    ny, nz = n_dom // 2, n_feat // 2
    rows = node_feats.shape[0]
    own_rows = node_feats.shape[1]
    dst_rows = cotangent.shape[1]
    width = w_self.shape[1]
    n_own, n_dst = own_rows // T, dst_rows // T
    n_src = n_own + 2 * n_dom
    piece = dst_rows // n_feat
    sub = w_self.shape[0] // n_dom
    small = n_feat * sub
    me = lax.axis_index("dom")
    block = lax.axis_index("feat")

    def over_dom(x, k):
        return lax.ppermute(x, "dom", [(i, i ^ k) for i in range(n_dom)])

    def over_feat(x, k):
        return lax.ppermute(x, "feat", [(i, i ^ k) for i in range(n_feat)])

    def relative(x, axis):
        parts = [lax.dynamic_slice_in_dim(x, me ^ k, 1, axis) for k in range(n_dom)]
        return jnp.concatenate(parts, axis=axis)

    def by_piece(x):
        return x.reshape(rows, n_feat, piece).transpose(1, 0, 2)

    mine = jnp.stack(
        [
            lax.dynamic_slice_in_dim(w_self, me * sub, sub, axis=0),
            lax.dynamic_slice_in_dim(w_neigh, me * sub, sub, axis=0),
        ]
    )
    mine = mine.reshape(2 * sub, width // piece, piece).transpose(1, 0, 2).reshape(-1, piece)
    high = bias_vec.astype(BF)
    low = (bias_vec - high.astype(F32)).astype(BF)
    bias_rows = jnp.pad(jnp.stack([high, low]), ((0, 14), (0, 0)))
    first = jnp.concatenate(
        [
            by_piece(node_feats[:, :dst_rows]),
            by_piece(cotangent),
            jnp.broadcast_to(bias_rows[None], (n_feat, 16, piece)),
            jnp.broadcast_to(mine[None], (n_feat,) + mine.shape),
        ],
        axis=1,
    )
    first = lax.all_to_all(first, "feat", 0, 0, tiled=True)

    sends = relative(send_rows.reshape(n_dom, T), 0)
    outgoing = gather_cols(node_feats, jnp.concatenate([sends, hub_rows[None, :]], axis=0))
    incoming = [outgoing[0]] + [over_dom(outgoing[k], k) for k in range(1, n_dom)]

    halo_tile = n_own + 2 * ((tile_src - n_own) ^ me)
    hub_tile = n_own + 2 * ((tile_src - n_own - n_dom) ^ me) + 1
    place = jnp.where(
        tile_src < n_own, tile_src, jnp.where(tile_src < n_own + n_dom, halo_tile, hub_tile)
    )
    n_pos = n_dst * n_src
    slot = jnp.arange(tile_dst.shape[0], dtype=jnp.int32)
    key = jnp.where(slot < tile_count[0], tile_dst * n_src + place, n_pos)
    before = (key[None, :] < key[:, None]) | (
        (key[None, :] == key[:, None]) & (slot[None, :] < slot[:, None])
    )
    rank = jnp.sum(before.astype(jnp.int32), axis=1)
    order = jnp.sum(jnp.where(rank[:, None] == slot[None, :], slot[:, None], 0), axis=0)
    order = jnp.concatenate([order, jnp.zeros((2,), jnp.int32)])
    ends = jnp.arange(n_pos + 1, dtype=jnp.int32)
    start = jnp.sum((key[None, :] < ends[:, None]).astype(jnp.int32), axis=1)
    a_own, a_ext, agg_own = build_dense(tile_vals, order, start, node_feats, n_dst, n_src, n_own)
    agg = add_halo(agg_own, a_ext, incoming, n_feat)

    agg, first = lax.optimization_barrier((agg, first))
    agg = lax.all_to_all(agg, "feat", 0, 0, tiled=True).reshape(width, piece)

    x = first[:, :rows, :].reshape(width, piece)
    cot = first[:, rows : 2 * rows, :].reshape(n_feat, n_dom, sub, piece)
    cot = relative(cot, 1).transpose(1, 0, 2, 3).reshape(n_dom, small, piece)
    even = [jnp.concatenate([cot[0], x, cot[1]], axis=0)]
    for j in range(1, ny):
        even.append(over_dom(jnp.concatenate([cot[2 * j], x, cot[2 * j + 1]], axis=0), 2 * j))
    odd = [over_dom(e[small:], 1) for e in even]
    bias = first[:, 2 * rows, :].astype(F32) + first[:, 2 * rows + 1, :].astype(F32)
    bias = lax.dynamic_slice_in_dim(bias, me * sub, sub, axis=1).reshape(small, 1)
    w = first[:, 2 * rows + 16 :, :].reshape(n_feat, width // piece, 2, sub, piece)
    w = w.transpose(2, 0, 3, 1, 4).reshape(2, small, width)

    agg_even = [agg] + [over_dom(agg, 2 * j) for j in range(1, ny)]
    agg_odd = [over_dom(a, 1) for a in agg_even]
    aggs = [a for pair in zip(agg_even, agg_odd) for a in pair]

    grad, gagg_even, gagg_odd, back_even, back_odd = middle(w, bias, even, odd, aggs)

    got = over_dom(gagg_odd, 1)
    pair = (gagg_even.astype(F32) + got.astype(F32)).astype(BF)
    gagg = pair[0].astype(F32)
    for j in range(1, ny):
        gagg += over_dom(pair[j], 2 * j).astype(F32)
    gagg = gagg.astype(BF).reshape(n_feat, rows, piece)
    gagg = lax.all_to_all(gagg, "feat", 0, 0, tiled=True)
    gagg, *halo_grad = halo_grads(gagg, a_ext, n_dom)
    returned = [halo_grad[0]] + [over_dom(halo_grad[k], k) for k in range(1, n_dom)]
    base = dot(gagg, a_own, ((1,), (0,)))

    parts = wgrad(block.reshape(1), grad, even, odd, aggs, n_feat)
    parts = (parts[0].astype(F32) + over_feat(parts[1], 1).astype(F32)).astype(BF)
    total = parts[0].astype(F32)
    for j in range(1, nz):
        total += over_feat(parts[j], 2 * j).astype(F32)
    bias_grad = total[:, 2 * width] + total[:, 2 * width + 1]
    bias_high = bias_grad.astype(BF).astype(F32)
    tail = jnp.stack([bias_high, bias_grad - bias_high], axis=1)
    total = jnp.concatenate([total[:, : 2 * width], jnp.pad(tail, ((0, 0), (0, T - 2)))], axis=1)
    total = total.astype(BF)
    whole = [total] + [over_dom(total, 2 * j) for j in range(1, ny)]
    whole = [t for e in whole for t in (e, over_dom(e, 1))]
    whole = relative(jnp.stack(whole), 0).reshape(n_dom * sub, -1).astype(F32)
    grad_bias = whole[:, 2 * width] + whole[:, 2 * width + 1]

    got = over_dom(back_odd, 1)
    self_pair = (back_even[:, :width].astype(F32) + got[:, :width].astype(F32)).astype(BF)
    gself = self_pair[0].astype(F32)
    acts = [back_even[0, width:], got[0, width:]]
    for j in range(1, ny):
        back = over_dom(
            jnp.concatenate([self_pair[j], back_even[j, width:], got[j, width:]], axis=0), 2 * j
        )
        gself += back[:width].astype(F32)
        acts += [back[width : width + small], back[width + small :]]
    acts = jnp.stack([a.reshape(n_feat, sub, piece) for a in acts], axis=1)
    acts = relative(acts, 1).reshape(n_feat, rows, piece)
    back = jnp.concatenate([gself.astype(BF).reshape(n_feat, rows, piece), acts], axis=1)
    back = lax.all_to_all(back, "feat", 0, 0, tiled=True)
    gself = back[:, :rows, :].transpose(1, 0, 2).reshape(rows, dst_rows)
    activations = back[:, rows:, :].transpose(1, 0, 2).reshape(rows, dst_rows)

    ret_idx = jnp.concatenate([sends, jnp.broadcast_to(hub_rows[None], (n_dom, T))], axis=1)
    grad_feats = finish(base, returned, ret_idx[:, :, None], gself)
    return (activations, grad_feats, whole[:, :width], whole[:, width : 2 * width], grad_bias)


def solution(mesh):
    return jax.shard_map(
        body,
        mesh=mesh,
        in_specs=(
            P("feat", "dom"),
            P("dom"),
            P("dom"),
            P("dom"),
            P("dom"),
            P("dom"),
            P("dom", None, None),
            P("feat", None),
            P("feat", None),
            P("feat"),
            P("feat", "dom"),
        ),
        out_specs=(P("feat", "dom"), P("feat", "dom"), P("feat", None), P("feat", None), P("feat")),
        check_vma=False,
    )
```

```python
import functools

import jax
import jax.numpy as jnp
from jax import lax
from jax.experimental import pallas as pl
from jax.experimental.pallas import tpu as pltpu
from jax.sharding import PartitionSpec as P

T = 128
BF = jnp.bfloat16
F32 = jnp.float32
MIB = 1 << 20
VMEM = pl.BlockSpec(memory_space=pltpu.VMEM)
SMEM = pl.BlockSpec(memory_space=pltpu.SMEM)


def dot(left, right, dims):
    return lax.dot_general(left, right, (dims, ((), ())), preferred_element_type=F32)


def shape(*dims, kind=BF):
    return jax.ShapeDtypeStruct(dims, kind)


def whole_call(kernel, name, micros, out_shape, *args, scalars=0, mib=24):
    many = isinstance(out_shape, (list, tuple))
    return pl.pallas_call(
        kernel,
        out_shape=out_shape,
        in_specs=[SMEM] * scalars + [VMEM] * (len(args) - scalars),
        out_specs=[VMEM] * len(out_shape) if many else VMEM,
        compiler_params=pltpu.CompilerParams(vmem_limit_bytes=mib * MIB),
        cost_estimate=pl.CostEstimate(
            flops=0, bytes_accessed=int(micros * 3.0e6), transcendentals=0
        ),
        name=name,
    )(*args)


def pack_kernel(sub, me_ref, x_ref, cot_ref, bias_ref, send_ref, hub_ref, first_ref, *out_refs):
    groups, chunks, _, piece = first_ref.shape
    n = x_ref.shape[0] // sub
    bias = bias_ref[...]
    high = bias.astype(BF).astype(F32)
    row = lax.broadcasted_iota(jnp.int32, (sub, piece), 0)
    tail = jnp.where(row == 0, high, jnp.where(row == 1, bias - high, 0.0)).astype(BF)
    for b in range(groups):
        cols = slice(b * piece, (b + 1) * piece)
        first_ref[b, :n] = x_ref[:, cols].reshape(n, sub, piece)
        first_ref[b, n : 2 * n] = cot_ref[:, cols].reshape(n, sub, piece)
        first_ref[b, 2 * n] = tail
    x = x_ref[...]
    rows = lax.broadcasted_iota(jnp.int32, (x.shape[1], T), 0)
    readers = len(out_refs)
    for q in range(readers + 1):
        idx = send_ref[pl.ds(me_ref[0] ^ q, 1), :] if q < readers else hub_ref[...]
        hot = (rows == idx).astype(F32).astype(BF)
        got = dot(x, hot, ((1,), (0,))).astype(BF)
        if q < readers:
            out_refs[q][:, :T] = got
        else:
            for r in range(readers):
                out_refs[r][:, T:] = got


def pack(me, x, cot, bias, sends, hubs, sub, n_feat):
    n_dom = sends.shape[0]
    rows = x.shape[0]
    args = (x, cot, bias, sends, hubs)
    outs = [shape(n_feat, 2 * n_dom + 1, sub, cot.shape[1] // n_feat)]
    outs += [shape(rows, 2 * T)] * n_dom
    return pl.pallas_call(
        functools.partial(pack_kernel, sub),
        out_shape=outs,
        grid=(1,),
        in_specs=[SMEM] + [pl.BlockSpec(a.shape, lambda i, n=a.ndim: (0,) * n) for a in args],
        out_specs=[pl.BlockSpec(o.shape, lambda i, n=len(o.shape): (0,) * n) for o in outs],
        compiler_params=pltpu.CompilerParams(vmem_limit_bytes=60 * MIB),
        cost_estimate=pl.CostEstimate(flops=0, bytes_accessed=12000000, transcendentals=0),
        name="pack",
    )(me, *args)


def build_kernel(n_own, order_ref, start_ref, x_ref, vals_hbm, *refs):
    *halo_refs, own_ref, ext_ref, agg_ref, vals, sems = refs
    step = pl.program_id(0)
    slots = vals_hbm.shape[0]
    n_src = n_own + ext_ref.shape[1] // T
    chunks = sems.shape[0]
    per = slots // chunks

    def piece(i):
        span = pl.ds(i * per, per)
        return pltpu.make_async_copy(vals_hbm.at[span], vals.at[span], sems.at[i])

    @pl.when(step == 0)
    def _():
        for i in range(chunks):
            piece(i).start()
        vals[slots] = jnp.zeros((T, T), BF)
        for i in range(chunks):
            piece(i).wait()

    for v in range(own_ref.shape[0] // T):
        rows = slice(v * T, (v + 1) * T)
        for s in range(n_src):
            p = (step * (own_ref.shape[0] // T) + v) * n_src + s
            first, last = start_ref[p], start_ref[p + 1]
            one = jnp.where(last > first, order_ref[first], slots)
            two = jnp.where(last > first + 1, order_ref[first + 1], slots)
            total = vals[one].astype(F32) + vals[two].astype(F32)

            def more(i, total):
                return total + vals[order_ref[i]].astype(F32)

            total = lax.fori_loop(first + 2, last, more, total).astype(BF)
            if s < n_own:
                own_ref[rows, s * T : (s + 1) * T] = total
            else:
                ext_ref[rows, (s - n_own) * T : (s - n_own + 1) * T] = total
    halo = jnp.concatenate([r[...] for r in halo_refs], axis=1)
    total = dot(x_ref[...], own_ref[...], ((1,), (1,)))
    total = (total + dot(halo, ext_ref[...], ((1,), (1,)))).astype(BF)
    piece_n = agg_ref.shape[2]
    for b in range(agg_ref.shape[0]):
        agg_ref[b] = total[:, b * piece_n : (b + 1) * piece_n]


def build_dense(vals, order, start, x, halos, n_dst, n_src, n_own, n_feat):
    rows = x.shape[0]
    piece = n_dst * T // n_feat
    ext = (n_src - n_own) * T
    return pl.pallas_call(
        functools.partial(build_kernel, n_own),
        out_shape=(
            shape(n_dst * T, n_own * T),
            shape(n_dst * T, ext),
            shape(n_feat, rows, piece),
        ),
        grid_spec=pltpu.PrefetchScalarGridSpec(
            num_scalar_prefetch=2,
            grid=(n_dst // 2,),
            in_specs=[VMEM, pl.BlockSpec(memory_space=pl.ANY)] + [VMEM] * len(halos),
            out_specs=[
                pl.BlockSpec((2 * T, n_own * T), lambda u, *_: (u, 0)),
                pl.BlockSpec((2 * T, ext), lambda u, *_: (u, 0)),
                pl.BlockSpec((2 * T // piece, rows, piece), lambda u, *_: (u, 0, 0)),
            ],
            scratch_shapes=[
                pltpu.VMEM((vals.shape[0] + 1, T, T), BF),
                pltpu.SemaphoreType.DMA((8,)),
            ],
        ),
        compiler_params=pltpu.CompilerParams(vmem_limit_bytes=58 * MIB),
        cost_estimate=pl.CostEstimate(flops=0, bytes_accessed=30000000, transcendentals=0),
        name="build_dense",
    )(order, start, x, vals, *halos)


def split_kernel(blocks, n_dom, me_ref, block_ref, first_ref, bias_ref, *out_refs):
    _, _, sub, piece = first_ref.shape
    n = (first_ref.shape[1] - 1) // 2
    small = len(blocks) * sub
    width = len(blocks) * n * sub
    x = first_ref[:, :n].reshape(width, piece)
    row = lax.broadcasted_iota(jnp.int32, (sub, piece), 0) + me_ref[0] * sub
    lane = lax.broadcasted_iota(jnp.int32, (sub, piece), 1)
    for i, k in enumerate(blocks):
        b = block_ref[0] ^ k
        both = first_ref[b, 2 * n, 0:1].astype(F32) + first_ref[b, 2 * n, 1:2].astype(F32)
        mine = jnp.sum(jnp.where(row == lane, both, 0.0), axis=1, keepdims=True)
        bias_ref[i * sub : (i + 1) * sub, :] = jnp.broadcast_to(mine, (sub, T))
    even, odd = out_refs[0], out_refs[1]
    even[small:] = x
    odd[:width] = x
    for i, k in enumerate(blocks):
        b = block_ref[0] ^ k
        even[i * sub : (i + 1) * sub] = first_ref[b, n + me_ref[0]]
        odd[width + i * sub : width + (i + 1) * sub] = first_ref[b, n + (me_ref[0] ^ 1)]
    for j in range(1, n_dom // 2):
        ref = out_refs[1 + j]
        ref[small : small + width] = x
        for i, k in enumerate(blocks):
            b = block_ref[0] ^ k
            at = small + width + i * sub
            ref[i * sub : (i + 1) * sub] = first_ref[b, n + (me_ref[0] ^ (2 * j))]
            ref[at : at + sub] = first_ref[b, n + (me_ref[0] ^ (2 * j + 1))]


def weights(refs):
    return [jnp.concatenate([r[g, m] for r in refs for g in range(r.shape[0])]) for m in (0, 1)]


def dense_kernel(ny, nw, bias_ref, *refs):
    w_refs, refs = refs[:nw], refs[nw:]
    even, odd, agg = refs[:ny], refs[ny : 2 * ny], refs[2 * ny : 4 * ny]
    g_ref, act_even, act_odd, gagg_even, gagg_odd = refs[4 * ny :]
    w_self, w_neigh = weights(w_refs)
    small, width = w_self.shape
    bias = bias_ref[:, :1]
    for k in range(2 * ny):
        j = k // 2
        if k % 2 == 0:
            cot, x = even[j][:small, :], even[j][small : small + width, :]
            act_ref, gagg_ref = act_even, gagg_even
        else:
            x, cot = odd[j][:width, :], odd[j][width:, :]
            act_ref, gagg_ref = act_odd, gagg_odd
        pre = dot(w_self, x, ((1,), (0,)))
        pre += dot(w_neigh, agg[k][...], ((1,), (0,)))
        pre += bias
        sig = 1.0 / (1.0 + jnp.exp(-pre))
        act_ref[j] = (pre * sig).astype(BF)
        grad = (cot.astype(F32) * sig * (1.0 + pre * (1.0 - sig))).astype(BF)
        g_ref[k] = grad
        gagg_ref[j] = dot(w_neigh, grad, ((0,), (0,))).astype(BF)


def grads_kernel(ny, nw, g_ref, act_even, act_odd, *refs):
    w_refs, refs = refs[:nw], refs[nw:]
    even, odd, agg = refs[:ny], refs[ny : 2 * ny], refs[2 * ny : 4 * ny]
    back_even, back_odd, out_ref = refs[4 * ny :]
    w_self, _ = weights(w_refs)
    small, width = w_self.shape
    sub = out_ref.shape[2]
    xs = []
    for k in range(2 * ny):
        j = k // 2
        act_ref, back_ref = (act_odd, back_odd) if k % 2 else (act_even, back_even)
        back_ref[j, :width] = dot(w_self, g_ref[k], ((0,), (0,))).astype(BF)
        back_ref[j, width:] = act_ref[j]
        xs.append(odd[j][:width, :] if k % 2 else even[j][small : small + width, :])
    grad = jnp.concatenate([g_ref[k] for k in range(2 * ny)], axis=1)
    own = dot(grad, jnp.concatenate(xs, axis=1), ((1,), (1,))).astype(BF)
    neigh = dot(grad, jnp.concatenate([r[...] for r in agg], axis=1), ((1,), (1,))).astype(BF)
    total = jnp.sum(grad.astype(F32), axis=1, keepdims=True)
    high = total.astype(BF).astype(F32)
    lane = lax.broadcasted_iota(jnp.int32, (small, T), 1)
    both = jnp.where(lane == 0, high, jnp.where(lane == 1, total - high, 0.0)).astype(BF)
    nz = out_ref.shape[1]
    for i in range(small // sub):
        rows = slice(i * sub, (i + 1) * sub)
        out_ref[i // nz, i % nz, :, :width] = own[rows]
        out_ref[i // nz, i % nz, :, width : 2 * width] = neigh[rows]
        out_ref[i // nz, i % nz, :, 2 * width :] = both[rows]


def pair_kernel(even_ref, got_ref, *out_refs):
    for j, out_ref in enumerate(out_refs):
        out_ref[...] = (even_ref[j].astype(F32) + got_ref[j].astype(F32)).astype(BF)


def back_pair_kernel(width, even_ref, got_ref, *out_refs):
    for j, out_ref in enumerate(out_refs):
        both = even_ref[j, :width].astype(F32) + got_ref[j, :width].astype(F32)
        small = even_ref.shape[1] - width
        out_ref[:width] = both.astype(BF)
        out_ref[width : width + small] = even_ref[j, width:]
        out_ref[width + small :] = got_ref[j, width:]


def back_pack_kernel(blocks, me_ref, block_ref, *refs):
    *in_refs, out_ref = refs
    groups, chunks, sub, piece = out_ref.shape
    n = chunks // 2
    width = groups * n * sub
    small = groups * sub
    total = in_refs[0][:width].astype(F32)
    for r in in_refs[1:]:
        total += r[:width].astype(F32)
    out_ref[:, :n] = total.astype(BF).reshape(groups, n, sub, piece)
    for k in range(2 * len(in_refs)):
        d = me_ref[0] ^ k
        for i, f in enumerate(blocks):
            at = width + (k % 2) * small + i * sub
            out_ref[block_ref[0] ^ f, n + d] = in_refs[k // 2][at : at + sub]


def wsum_kernel(width, *refs):
    *in_refs, out_ref = refs
    total = in_refs[0][...].astype(F32)
    for r in in_refs[1:]:
        total += r[...].astype(F32)
    out_ref[:, : 2 * width] = total[:, : 2 * width].astype(BF)
    bias = jnp.sum(total[:, 2 * width :], axis=1, keepdims=True)
    high = bias.astype(BF).astype(F32)
    lane = lax.broadcasted_iota(jnp.int32, (total.shape[0], T), 1)
    both = jnp.where(lane == 0, high, jnp.where(lane == 1, bias - high, 0.0))
    out_ref[:, 2 * width :] = both.astype(BF)


def wout_kernel(me_ref, *refs):
    *in_refs, self_ref, neigh_ref, bias_ref = refs
    width = self_ref.shape[2]
    for k, ref in enumerate(in_refs):
        d = me_ref[0] ^ k
        self_ref[d] = ref[:, :width].astype(F32)
        neigh_ref[d] = ref[:, width : 2 * width].astype(F32)
        total = jnp.sum(ref[:, 2 * width :].astype(F32), axis=1, keepdims=True)
        bias_ref[d] = jnp.broadcast_to(total, bias_ref.shape[1:])


def halo_grad_kernel(ga_ref, ext_ref, flat_ref, *out_refs):
    ga = jnp.concatenate([ga_ref[b] for b in range(ga_ref.shape[0])], axis=1)
    flat_ref[...] = ga
    for k, out_ref in enumerate(out_refs):
        span = slice(k * 2 * T, (k + 1) * 2 * T)
        out_ref[...] = dot(ga, ext_ref[:, span], ((1,), (0,))).astype(BF)


def add_returned(total, at, me_ref, send_ref, hub_ref, ret_refs):
    rows = lax.broadcasted_iota(jnp.int32, (total.shape[1], T), 0) + at
    hub = (rows == hub_ref[...]).astype(F32).astype(BF)
    for q, ret_ref in enumerate(ret_refs):
        idx = send_ref[pl.ds(me_ref[0] ^ q, 1), :]
        sent = (rows == idx).astype(F32).astype(BF)
        total += dot(ret_ref[:, :T], sent, ((1,), (1,)))
        total += dot(ret_ref[:, T:], hub, ((1,), (1,)))
    return total


def finish_rest_kernel(top, me_ref, base_ref, send_ref, hub_ref, *refs):
    *ret_refs, out_ref = refs
    at = (pl.program_id(0) + top) * out_ref.shape[1]
    out_ref[...] = add_returned(base_ref[...], at, me_ref, send_ref, hub_ref, ret_refs)


def finish_dst_kernel(me_ref, base_ref, send_ref, hub_ref, back_ref, grads_ref, *refs):
    *ret_refs, out_ref, act_ref = refs
    rows = base_ref.shape[0]
    groups = range(back_ref.shape[0])
    own = jnp.concatenate([back_ref[b, :rows] for b in groups], axis=1).astype(F32)
    act_ref[...] = jnp.concatenate([back_ref[b, rows:] for b in groups], axis=1)
    at = pl.program_id(0) * out_ref.shape[1]
    out_ref[...] = add_returned(base_ref[...] + own, at, me_ref, send_ref, hub_ref, ret_refs)


def finish(me, base, ret, sends, hubs, back):
    rows, n = base.shape
    width = 512
    groups, _, piece = back.shape
    n_dst = groups * piece
    per = width // piece
    top = n_dst // width

    def column(first):
        return pl.BlockSpec((rows, width), lambda i: (0, i + first))

    def fixed(x):
        return pl.BlockSpec(x.shape, lambda i: (0, 0))

    grads = pl.pallas_call(
        functools.partial(finish_rest_kernel, top),
        out_shape=shape(rows, n, kind=F32),
        grid=(n // width - top,),
        in_specs=[SMEM, column(top), fixed(sends), fixed(hubs)] + [fixed(r) for r in ret],
        out_specs=column(top),
        compiler_params=pltpu.CompilerParams(vmem_limit_bytes=24 * MIB),
        cost_estimate=pl.CostEstimate(flops=0, bytes_accessed=15000000, transcendentals=0),
        name="finish_rest",
    )(me, base, sends, hubs, *ret)
    return pl.pallas_call(
        finish_dst_kernel,
        out_shape=[shape(rows, n, kind=F32), shape(rows, n_dst)],
        grid=(top,),
        in_specs=[
            SMEM,
            column(0),
            fixed(sends),
            fixed(hubs),
            pl.BlockSpec((per, 2 * rows, piece), lambda i: (i, 0, 0)),
            pl.BlockSpec(memory_space=pl.ANY),
        ]
        + [fixed(r) for r in ret],
        out_specs=[column(0), column(0)],
        input_output_aliases={5: 0},
        compiler_params=pltpu.CompilerParams(vmem_limit_bytes=24 * MIB),
        cost_estimate=pl.CostEstimate(flops=0, bytes_accessed=5000000, transcendentals=0),
        name="finish_dst",
    )(me, base, sends, hubs, back, grads, *ret)


def body(
    node_feats,
    send_rows,
    hub_rows,
    tile_dst,
    tile_src,
    tile_count,
    tile_vals,
    w_self,
    w_neigh,
    bias_vec,
    cotangent,
):
    n_dom = lax.axis_size("dom")
    n_feat = lax.axis_size("feat")
    ny, nz = n_dom // 2, n_feat // 2
    rows = node_feats.shape[0]
    own_rows = node_feats.shape[1]
    dst_rows = cotangent.shape[1]
    width = w_self.shape[1]
    n_own, n_dst = own_rows // T, dst_rows // T
    n_src = n_own + 2 * n_dom
    piece = dst_rows // n_feat
    sub = w_self.shape[0] // n_dom
    small = n_feat * sub
    me = lax.axis_index("dom")
    block = lax.axis_index("feat")
    me_s, block_s = me.reshape(1), block.reshape(1)

    def over_dom(x, k):
        return lax.ppermute(x, "dom", [(i, i ^ k) for i in range(n_dom)])

    def over_feat(x, k):
        return lax.ppermute(x, "feat", [(i, i ^ k) for i in range(n_feat)])

    def after(x, *events):
        return lax.optimization_barrier((x, events))[0]

    mine = jnp.stack(
        [
            lax.dynamic_slice_in_dim(w_self, me * sub, sub, axis=0),
            lax.dynamic_slice_in_dim(w_neigh, me * sub, sub, axis=0),
        ]
    )
    w, blocks = [mine[None]], [0]
    for bit in [1 << i for i in range(1, n_feat.bit_length() - 1)]:
        send = w[0] if len(w) == 1 else jnp.concatenate(w, axis=0)
        w.append(over_feat(send, bit))
        blocks += [k ^ bit for k in blocks]
    blocks += [k ^ 1 for k in blocks]

    sends, hubs = send_rows.reshape(n_dom, T), hub_rows[None, :]
    first, *outgoing = pack(
        me_s, node_feats, cotangent, bias_vec[None, :], sends, hubs, sub, n_feat
    )
    first = after(first, w[1])
    first = lax.all_to_all(first, "feat", 0, 0, tiled=True)
    incoming = [outgoing[0]] + [over_dom(outgoing[k], k) for k in range(1, n_dom)]

    halo_tile = n_own + 2 * ((tile_src - n_own) ^ me)
    hub_tile = n_own + 2 * ((tile_src - n_own - n_dom) ^ me) + 1
    place = jnp.where(
        tile_src < n_own, tile_src, jnp.where(tile_src < n_own + n_dom, halo_tile, hub_tile)
    )
    n_pos = n_dst * n_src
    slot = jnp.arange(tile_dst.shape[0], dtype=jnp.int32)
    key = jnp.where(slot < tile_count[0], tile_dst * n_src + place, n_pos)
    before = (key[None, :] < key[:, None]) | (
        (key[None, :] == key[:, None]) & (slot[None, :] < slot[:, None])
    )
    rank = jnp.sum(before.astype(jnp.int32), axis=1)
    order = jnp.sum(jnp.where(rank[:, None] == slot[None, :], slot[:, None], 0), axis=0)
    order = jnp.concatenate([order, jnp.zeros((2,), jnp.int32)])
    ends = jnp.arange(n_pos + 1, dtype=jnp.int32)
    start = jnp.sum((key[None, :] < ends[:, None]).astype(jnp.int32), axis=1)
    a_own, a_ext, agg = build_dense(
        tile_vals, order, start, node_feats, incoming, n_dst, n_src, n_own, n_feat
    )

    w[-1] = after(w[-1], agg)
    w.append(over_feat(jnp.concatenate(w, axis=0), 1))
    agg = after(agg, first)
    agg = lax.all_to_all(agg, "feat", 0, 0, tiled=True).reshape(width, piece)

    bias, even, odd, *cross = whole_call(
        functools.partial(split_kernel, blocks, n_dom),
        "split",
        1.5,
        [
            shape(small, T, kind=F32),
            shape(small + width, piece),
            shape(small + width, piece),
        ]
        + [shape(2 * small + width, piece)] * (ny - 1),
        me_s,
        block_s,
        first,
        scalars=2,
    )
    cross = [over_dom(c, 2 * (j + 1)) for j, c in enumerate(cross)]
    evens = [even] + cross
    odds = [over_dom(odd, 1)] + [over_dom(c[small:], 1) for c in cross]
    agg_even = [agg] + [over_dom(agg, 2 * j) for j in range(1, ny)]
    agg_odd = [over_dom(a, 1) for a in agg_even]
    aggs = [a for pair in zip(agg_even, agg_odd) for a in pair]

    grad, act_even, act_odd, gagg_even, gagg_odd = whole_call(
        functools.partial(dense_kernel, ny, len(w)),
        "dense",
        3.0,
        [
            shape(n_dom, small, piece),
            shape(ny, small, piece),
            shape(ny, small, piece),
            shape(ny, width, piece),
            shape(ny, width, piece),
        ],
        bias,
        *w,
        *evens,
        *odds,
        *aggs,
    )

    got = over_dom(gagg_odd, 1)
    pair = whole_call(pair_kernel, "pair", 1.0, [shape(width, piece)] * ny, gagg_even, got)

    back_even, back_odd, parts = whole_call(
        functools.partial(grads_kernel, ny, len(w)),
        "grads",
        3.0,
        [
            shape(ny, width + small, piece),
            shape(ny, width + small, piece),
            shape(2, nz, sub, 2 * width + T),
        ],
        grad,
        act_even,
        act_odd,
        *w,
        *evens,
        *odds,
        *aggs,
    )
    parts, back_odd = after((parts, back_odd), pair)

    gagg = pair[0].astype(F32)
    for j in range(1, ny):
        gagg += over_dom(pair[j], 2 * j).astype(F32)
    gagg = gagg.astype(BF).reshape(n_feat, rows, piece)
    from_x = over_feat(parts[1], 1)
    from_core = over_dom(back_odd, 1)
    from_x, from_core = after(from_x, gagg), after(from_core, gagg)

    gagg = lax.all_to_all(gagg, "feat", 0, 0, tiled=True)
    back = whole_call(
        functools.partial(back_pair_kernel, width),
        "back_pair",
        1.0,
        [shape(width + 2 * small, piece)] * ny,
        back_even,
        from_core,
    )
    back = [back[0]] + [over_dom(back[j], 2 * j) for j in range(1, ny)]
    parts = whole_call(pair_kernel, "x_sum", 1.0, [shape(sub, 2 * width + T)] * nz, parts[0], from_x)
    parts = [parts[0]] + [over_feat(parts[j], 2 * j) for j in range(1, nz)]

    gagg, *halo_grad = whole_call(
        halo_grad_kernel,
        "halo_grads",
        1.0,
        [shape(rows, dst_rows)] + [shape(rows, 2 * T)] * n_dom,
        gagg,
        a_ext,
    )
    back, parts = after(back, halo_grad), after(parts, halo_grad)
    returned = [halo_grad[0]] + [over_dom(halo_grad[k], k) for k in range(1, n_dom)]
    parts = after(parts, returned)

    back = whole_call(
        functools.partial(back_pack_kernel, blocks),
        "back_pack",
        1.0,
        shape(n_feat, 2 * n_dom, sub, piece),
        me_s,
        block_s,
        *back,
        scalars=2,
    )
    back = lax.all_to_all(back, "feat", 0, 0, tiled=True).reshape(n_feat, 2 * rows, piece)
    total = whole_call(
        functools.partial(wsum_kernel, width), "w_sum", 1.0, shape(sub, 2 * width + T), *parts
    )
    whole = [total] + [over_dom(total, 2 * j) for j in range(1, ny)]
    whole = [t for e in whole for t in (e, over_dom(e, 1))]
    base = dot(gagg, a_own, ((1,), (0,)))
    grad_self, grad_neigh, grad_bias = whole_call(
        wout_kernel,
        "w_out",
        1.0,
        [
            shape(n_dom, sub, width, kind=F32),
            shape(n_dom, sub, width, kind=F32),
            shape(n_dom, sub, T, kind=F32),
        ],
        me_s,
        *whole,
        scalars=1,
    )

    grad_feats, activations = finish(me_s, base, returned, sends, hubs, back)
    return (
        activations,
        grad_feats,
        grad_self.reshape(n_dom * sub, width),
        grad_neigh.reshape(n_dom * sub, width),
        grad_bias[:, :, 0].reshape(n_dom * sub),
    )


def solution(mesh):
    return jax.shard_map(
        body,
        mesh=mesh,
        in_specs=(
            P("feat", "dom"),
            P("dom"),
            P("dom"),
            P("dom"),
            P("dom"),
            P("dom"),
            P("dom", None, None),
            P("feat", None),
            P("feat", None),
            P("feat"),
            P("feat", "dom"),
        ),
        out_specs=(P("feat", "dom"), P("feat", "dom"), P("feat", None), P("feat", None), P("feat")),
        check_vma=False,
    )
```

```python
import functools

import jax
import jax.numpy as jnp
from jax import lax
from jax.experimental import pallas as pl
from jax.experimental.pallas import tpu as pltpu
from jax.sharding import PartitionSpec as P

T = 128
BF = jnp.bfloat16
F32 = jnp.float32
MIB = 1 << 20
VMEM = pl.BlockSpec(memory_space=pltpu.VMEM)
SMEM = pl.BlockSpec(memory_space=pltpu.SMEM)


def dot(left, right, dims):
    return lax.dot_general(left, right, (dims, ((), ())), preferred_element_type=F32)


def shape(*dims, kind=BF):
    return jax.ShapeDtypeStruct(dims, kind)


def whole_call(kernel, name, micros, out_shape, *args, scalars=0, mib=24):
    many = isinstance(out_shape, (list, tuple))
    return pl.pallas_call(
        kernel,
        out_shape=out_shape,
        in_specs=[SMEM] * scalars + [VMEM] * (len(args) - scalars),
        out_specs=[VMEM] * len(out_shape) if many else VMEM,
        compiler_params=pltpu.CompilerParams(vmem_limit_bytes=mib * MIB),
        cost_estimate=pl.CostEstimate(
            flops=0, bytes_accessed=int(micros * 3.0e6), transcendentals=0
        ),
        name=name,
    )(*args)


def pack_kernel(sub, me_ref, x_ref, cot_ref, bias_ref, send_ref, hub_ref, first_ref, *out_refs):
    groups, chunks, _, piece = first_ref.shape
    n = x_ref.shape[0] // sub
    bias = bias_ref[...]
    high = bias.astype(BF).astype(F32)
    row = lax.broadcasted_iota(jnp.int32, (sub, piece), 0)
    tail = jnp.where(row == 0, high, jnp.where(row == 1, bias - high, 0.0)).astype(BF)
    for b in range(groups):
        cols = slice(b * piece, (b + 1) * piece)
        first_ref[b, :n] = x_ref[:, cols].reshape(n, sub, piece)
        first_ref[b, n : 2 * n] = cot_ref[:, cols].reshape(n, sub, piece)
        first_ref[b, 2 * n] = tail
    x = x_ref[...]
    rows = lax.broadcasted_iota(jnp.int32, (x.shape[1], T), 0)
    readers = len(out_refs)
    for q in range(readers + 1):
        idx = send_ref[pl.ds(me_ref[0] ^ q, 1), :] if q < readers else hub_ref[...]
        hot = (rows == idx).astype(F32).astype(BF)
        got = dot(x, hot, ((1,), (0,))).astype(BF)
        if q < readers:
            out_refs[q][:, :T] = got
        else:
            for r in range(readers):
                out_refs[r][:, T:] = got


def pack(me, x, cot, bias, sends, hubs, sub, n_feat):
    n_dom = sends.shape[0]
    rows = x.shape[0]
    args = (x, cot, bias, sends, hubs)
    outs = [shape(n_feat, 2 * n_dom + 1, sub, cot.shape[1] // n_feat)]
    outs += [shape(rows, 2 * T)] * n_dom
    return pl.pallas_call(
        functools.partial(pack_kernel, sub),
        out_shape=outs,
        grid=(1,),
        in_specs=[SMEM] + [pl.BlockSpec(a.shape, lambda i, n=a.ndim: (0,) * n) for a in args],
        out_specs=[pl.BlockSpec(o.shape, lambda i, n=len(o.shape): (0,) * n) for o in outs],
        compiler_params=pltpu.CompilerParams(vmem_limit_bytes=60 * MIB),
        cost_estimate=pl.CostEstimate(flops=0, bytes_accessed=12000000, transcendentals=0),
        name="pack",
    )(me, *args)


def build_kernel(n_own, order_ref, start_ref, x_ref, vals_hbm, *refs):
    *halo_refs, own_ref, ext_ref, agg_ref, vals, sems = refs
    step = pl.program_id(0)
    slots = vals_hbm.shape[0]
    n_src = n_own + ext_ref.shape[1] // T
    chunks = sems.shape[0]
    per = slots // chunks

    def piece(i):
        span = pl.ds(i * per, per)
        return pltpu.make_async_copy(vals_hbm.at[span], vals.at[span], sems.at[i])

    @pl.when(step == 0)
    def _():
        for i in range(chunks):
            piece(i).start()
        vals[slots] = jnp.zeros((T, T), BF)
        for i in range(chunks):
            piece(i).wait()

    for v in range(own_ref.shape[0] // T):
        rows = slice(v * T, (v + 1) * T)
        for s in range(n_src):
            p = (step * (own_ref.shape[0] // T) + v) * n_src + s
            first, last = start_ref[p], start_ref[p + 1]
            one = jnp.where(last > first, order_ref[first], slots)
            two = jnp.where(last > first + 1, order_ref[first + 1], slots)
            total = vals[one].astype(F32) + vals[two].astype(F32)

            def more(i, total):
                return total + vals[order_ref[i]].astype(F32)

            total = lax.fori_loop(first + 2, last, more, total).astype(BF)
            if s < n_own:
                own_ref[rows, s * T : (s + 1) * T] = total
            else:
                ext_ref[rows, (s - n_own) * T : (s - n_own + 1) * T] = total
    halo = jnp.concatenate([r[...] for r in halo_refs], axis=1)
    total = dot(x_ref[...], own_ref[...], ((1,), (1,)))
    total = (total + dot(halo, ext_ref[...], ((1,), (1,)))).astype(BF)
    piece_n = agg_ref.shape[2]
    for b in range(agg_ref.shape[0]):
        agg_ref[b] = total[:, b * piece_n : (b + 1) * piece_n]


def build_dense(vals, order, start, x, halos, n_dst, n_src, n_own, n_feat):
    rows = x.shape[0]
    piece = n_dst * T // n_feat
    ext = (n_src - n_own) * T
    return pl.pallas_call(
        functools.partial(build_kernel, n_own),
        out_shape=(
            shape(n_dst * T, n_own * T),
            shape(n_dst * T, ext),
            shape(n_feat, rows, piece),
        ),
        grid_spec=pltpu.PrefetchScalarGridSpec(
            num_scalar_prefetch=2,
            grid=(n_dst // 2,),
            in_specs=[VMEM, pl.BlockSpec(memory_space=pl.ANY)] + [VMEM] * len(halos),
            out_specs=[
                pl.BlockSpec((2 * T, n_own * T), lambda u, *_: (u, 0)),
                pl.BlockSpec((2 * T, ext), lambda u, *_: (u, 0)),
                pl.BlockSpec((2 * T // piece, rows, piece), lambda u, *_: (u, 0, 0)),
            ],
            scratch_shapes=[
                pltpu.VMEM((vals.shape[0] + 1, T, T), BF),
                pltpu.SemaphoreType.DMA((8,)),
            ],
        ),
        compiler_params=pltpu.CompilerParams(vmem_limit_bytes=58 * MIB),
        cost_estimate=pl.CostEstimate(flops=0, bytes_accessed=30000000, transcendentals=0),
        name="build_dense",
    )(order, start, x, vals, *halos)


def split_kernel(blocks, n_dom, me_ref, block_ref, first_ref, bias_ref, *out_refs):
    _, _, sub, piece = first_ref.shape
    n = (first_ref.shape[1] - 1) // 2
    small = len(blocks) * sub
    width = len(blocks) * n * sub
    x = first_ref[:, :n].reshape(width, piece)
    row = lax.broadcasted_iota(jnp.int32, (sub, piece), 0) + me_ref[0] * sub
    lane = lax.broadcasted_iota(jnp.int32, (sub, piece), 1)
    for i, k in enumerate(blocks):
        b = block_ref[0] ^ k
        both = first_ref[b, 2 * n, 0:1].astype(F32) + first_ref[b, 2 * n, 1:2].astype(F32)
        mine = jnp.sum(jnp.where(row == lane, both, 0.0), axis=1, keepdims=True)
        bias_ref[i * sub : (i + 1) * sub, :] = jnp.broadcast_to(mine, (sub, T))
    even, odd = out_refs[0], out_refs[1]
    even[small:] = x
    odd[:width] = x
    for i, k in enumerate(blocks):
        b = block_ref[0] ^ k
        even[i * sub : (i + 1) * sub] = first_ref[b, n + me_ref[0]]
        odd[width + i * sub : width + (i + 1) * sub] = first_ref[b, n + (me_ref[0] ^ 1)]
    for j in range(1, n_dom // 2):
        ref = out_refs[1 + j]
        ref[small : small + width] = x
        for i, k in enumerate(blocks):
            b = block_ref[0] ^ k
            at = small + width + i * sub
            ref[i * sub : (i + 1) * sub] = first_ref[b, n + (me_ref[0] ^ (2 * j))]
            ref[at : at + sub] = first_ref[b, n + (me_ref[0] ^ (2 * j + 1))]


def weights(refs):
    return [jnp.concatenate([r[g, m] for r in refs for g in range(r.shape[0])]) for m in (0, 1)]


def dense_kernel(ny, nw, bias_ref, *refs):
    w_refs, refs = refs[:nw], refs[nw:]
    even, odd, agg = refs[:ny], refs[ny : 2 * ny], refs[2 * ny : 4 * ny]
    g_ref, act_even, act_odd, gagg_even, gagg_odd = refs[4 * ny :]
    w_self, w_neigh = weights(w_refs)
    small, width = w_self.shape
    bias = bias_ref[:, :1]
    for k in range(2 * ny):
        j = k // 2
        if k % 2 == 0:
            cot, x = even[j][:small, :], even[j][small : small + width, :]
            act_ref, gagg_ref = act_even, gagg_even
        else:
            x, cot = odd[j][:width, :], odd[j][width:, :]
            act_ref, gagg_ref = act_odd, gagg_odd
        pre = dot(w_self, x, ((1,), (0,)))
        pre += dot(w_neigh, agg[k][...], ((1,), (0,)))
        pre += bias
        sig = 1.0 / (1.0 + jnp.exp(-pre))
        act_ref[j] = (pre * sig).astype(BF)
        grad = (cot.astype(F32) * sig * (1.0 + pre * (1.0 - sig))).astype(BF)
        g_ref[k] = grad
        gagg_ref[j] = dot(w_neigh, grad, ((0,), (0,))).astype(BF)


def grads_kernel(ny, nw, g_ref, act_even, act_odd, *refs):
    w_refs, refs = refs[:nw], refs[nw:]
    even, odd, agg = refs[:ny], refs[ny : 2 * ny], refs[2 * ny : 4 * ny]
    back_even, back_odd, *out_refs = refs[4 * ny :]
    w_self, _ = weights(w_refs)
    small, width = w_self.shape
    sub = out_refs[0].shape[1]
    xs = []
    for k in range(2 * ny):
        j = k // 2
        act_ref, back_ref = (act_odd, back_odd) if k % 2 else (act_even, back_even)
        back_ref[j, :width] = dot(w_self, g_ref[k], ((0,), (0,))).astype(BF)
        back_ref[j, width:] = act_ref[j]
        xs.append(odd[j][:width, :] if k % 2 else even[j][small : small + width, :])
    grad = jnp.concatenate([g_ref[k] for k in range(2 * ny)], axis=1)
    own = dot(grad, jnp.concatenate(xs, axis=1), ((1,), (1,))).astype(BF)
    neigh = dot(grad, jnp.concatenate([r[...] for r in agg], axis=1), ((1,), (1,))).astype(BF)
    total = jnp.sum(grad.astype(F32), axis=1, keepdims=True)
    high = total.astype(BF).astype(F32)
    lane = lax.broadcasted_iota(jnp.int32, (small, T), 1)
    both = jnp.where(lane == 0, high, jnp.where(lane == 1, total - high, 0.0)).astype(BF)
    nz = out_refs[0].shape[0]
    for i in range(small // sub):
        rows, out_ref = slice(i * sub, (i + 1) * sub), out_refs[i // nz]
        out_ref[i % nz, :, :width] = own[rows]
        out_ref[i % nz, :, width : 2 * width] = neigh[rows]
        out_ref[i % nz, :, 2 * width :] = both[rows]


def pair_kernel(even_ref, got_ref, *out_refs):
    for j, out_ref in enumerate(out_refs):
        out_ref[...] = (even_ref[j].astype(F32) + got_ref[j].astype(F32)).astype(BF)


def back_pair_kernel(width, even_ref, got_ref, *out_refs):
    for j, out_ref in enumerate(out_refs):
        both = even_ref[j, :width].astype(F32) + got_ref[j, :width].astype(F32)
        small = even_ref.shape[1] - width
        out_ref[:width] = both.astype(BF)
        out_ref[width : width + small] = even_ref[j, width:]
        out_ref[width + small :] = got_ref[j, width:]


def back_pack_kernel(blocks, me_ref, block_ref, *refs):
    *in_refs, out_ref = refs
    groups, chunks, sub, piece = out_ref.shape
    n = chunks // 2
    width = groups * n * sub
    small = groups * sub
    total = in_refs[0][:width].astype(F32)
    for r in in_refs[1:]:
        total += r[:width].astype(F32)
    out_ref[:, :n] = total.astype(BF).reshape(groups, n, sub, piece)
    for k in range(2 * len(in_refs)):
        d = me_ref[0] ^ k
        for i, f in enumerate(blocks):
            at = width + (k % 2) * small + i * sub
            out_ref[block_ref[0] ^ f, n + d] = in_refs[k // 2][at : at + sub]


def wsum_kernel(width, *refs):
    *in_refs, out_ref = refs
    total = in_refs[0][...].astype(F32)
    for r in in_refs[1:]:
        total += r[...].astype(F32)
    out_ref[:, : 2 * width] = total[:, : 2 * width].astype(BF)
    bias = jnp.sum(total[:, 2 * width :], axis=1, keepdims=True)
    high = bias.astype(BF).astype(F32)
    lane = lax.broadcasted_iota(jnp.int32, (total.shape[0], T), 1)
    both = jnp.where(lane == 0, high, jnp.where(lane == 1, bias - high, 0.0))
    out_ref[:, 2 * width :] = both.astype(BF)


def wout_kernel(me_ref, *refs):
    *in_refs, self_ref, neigh_ref, bias_ref = refs
    width = self_ref.shape[2]
    for k, ref in enumerate(in_refs):
        d = me_ref[0] ^ k
        self_ref[d] = ref[:, :width].astype(F32)
        neigh_ref[d] = ref[:, width : 2 * width].astype(F32)
        total = jnp.sum(ref[:, 2 * width :].astype(F32), axis=1, keepdims=True)
        bias_ref[d] = jnp.broadcast_to(total, bias_ref.shape[1:])


def halo_grad_kernel(ga_ref, ext_ref, flat_ref, *out_refs):
    ga = jnp.concatenate([ga_ref[b] for b in range(ga_ref.shape[0])], axis=1)
    flat_ref[...] = ga
    for k, out_ref in enumerate(out_refs):
        span = slice(k * 2 * T, (k + 1) * 2 * T)
        out_ref[...] = dot(ga, ext_ref[:, span], ((1,), (0,))).astype(BF)


def add_returned(total, at, me_ref, send_ref, hub_ref, ret_refs):
    rows = lax.broadcasted_iota(jnp.int32, (total.shape[1], T), 0) + at
    hub = (rows == hub_ref[...]).astype(F32).astype(BF)
    for q, ret_ref in enumerate(ret_refs):
        idx = send_ref[pl.ds(me_ref[0] ^ q, 1), :]
        sent = (rows == idx).astype(F32).astype(BF)
        total += dot(ret_ref[:, :T], sent, ((1,), (1,)))
        total += dot(ret_ref[:, T:], hub, ((1,), (1,)))
    return total


def finish_rest_kernel(top, me_ref, ga_ref, own_ref, send_ref, hub_ref, *refs):
    *ret_refs, out_ref = refs
    at = (pl.program_id(0) + top) * out_ref.shape[1]
    total = dot(ga_ref[...], own_ref[...], ((1,), (0,)))
    out_ref[...] = add_returned(total, at, me_ref, send_ref, hub_ref, ret_refs)


def finish_dst_kernel(me_ref, ga_ref, own_ref, send_ref, hub_ref, back_ref, grads_ref, *refs):
    *ret_refs, out_ref, act_ref = refs
    rows = ga_ref.shape[0]
    groups = range(back_ref.shape[0])
    own = jnp.concatenate([back_ref[b, :rows] for b in groups], axis=1).astype(F32)
    act_ref[...] = jnp.concatenate([back_ref[b, rows:] for b in groups], axis=1)
    at = pl.program_id(0) * out_ref.shape[1]
    total = dot(ga_ref[...], own_ref[...], ((1,), (0,))) + own
    out_ref[...] = add_returned(total, at, me_ref, send_ref, hub_ref, ret_refs)


WIDE = 512


def column(rows, first):
    return pl.BlockSpec((rows, WIDE), lambda i: (0, i + first))


def fixed(x):
    return pl.BlockSpec(x.shape, lambda i: (0, 0))


def finish_rest(me, ga, own, ret, sends, hubs, n_dst):
    rows, n, top = ga.shape[0], own.shape[1], n_dst // WIDE
    return pl.pallas_call(
        functools.partial(finish_rest_kernel, top),
        out_shape=shape(rows, n, kind=F32),
        grid=(n // WIDE - top,),
        in_specs=[SMEM, fixed(ga), column(n_dst, top), fixed(sends), fixed(hubs)]
        + [fixed(r) for r in ret],
        out_specs=column(rows, top),
        compiler_params=pltpu.CompilerParams(vmem_limit_bytes=24 * MIB),
        cost_estimate=pl.CostEstimate(flops=0, bytes_accessed=18000000, transcendentals=0),
        name="finish_rest",
    )(me, ga, own, sends, hubs, *ret)


def finish_dst(me, ga, own, ret, sends, hubs, back, grads):
    rows, n = grads.shape
    groups, _, piece = back.shape
    n_dst = groups * piece
    return pl.pallas_call(
        finish_dst_kernel,
        out_shape=[shape(rows, n, kind=F32), shape(rows, n_dst)],
        grid=(n_dst // WIDE,),
        in_specs=[
            SMEM,
            fixed(ga),
            column(n_dst, 0),
            fixed(sends),
            fixed(hubs),
            pl.BlockSpec((WIDE // piece, 2 * rows, piece), lambda i: (i, 0, 0)),
            pl.BlockSpec(memory_space=pl.ANY),
        ]
        + [fixed(r) for r in ret],
        out_specs=[column(rows, 0), column(rows, 0)],
        input_output_aliases={6: 0},
        compiler_params=pltpu.CompilerParams(vmem_limit_bytes=24 * MIB),
        cost_estimate=pl.CostEstimate(flops=0, bytes_accessed=6000000, transcendentals=0),
        name="finish_dst",
    )(me, ga, own, sends, hubs, back, grads, *ret)


def body(
    node_feats,
    send_rows,
    hub_rows,
    tile_dst,
    tile_src,
    tile_count,
    tile_vals,
    w_self,
    w_neigh,
    bias_vec,
    cotangent,
):
    n_dom = lax.axis_size("dom")
    n_feat = lax.axis_size("feat")
    ny, nz = n_dom // 2, n_feat // 2
    rows = node_feats.shape[0]
    own_rows = node_feats.shape[1]
    dst_rows = cotangent.shape[1]
    width = w_self.shape[1]
    n_own, n_dst = own_rows // T, dst_rows // T
    n_src = n_own + 2 * n_dom
    piece = dst_rows // n_feat
    sub = w_self.shape[0] // n_dom
    small = n_feat * sub
    me = lax.axis_index("dom")
    block = lax.axis_index("feat")
    me_s, block_s = me.reshape(1), block.reshape(1)

    def over_dom(x, k):
        return lax.ppermute(x, "dom", [(i, i ^ k) for i in range(n_dom)])

    def over_feat(x, k):
        return lax.ppermute(x, "feat", [(i, i ^ k) for i in range(n_feat)])

    def after(x, *events):
        return lax.optimization_barrier((x, events))[0]

    mine = jnp.stack(
        [
            lax.dynamic_slice_in_dim(w_self, me * sub, sub, axis=0),
            lax.dynamic_slice_in_dim(w_neigh, me * sub, sub, axis=0),
        ]
    )
    w, blocks = [mine[None]], [0]
    for bit in [1 << i for i in range(n_feat.bit_length() - 2, 0, -1)]:
        send = w[0] if len(w) == 1 else jnp.concatenate(w, axis=0)
        w.append(over_feat(send, bit))
        blocks += [k ^ bit for k in blocks]
    blocks += [k ^ 1 for k in blocks]

    sends, hubs = send_rows.reshape(n_dom, T), hub_rows[None, :]
    first, *outgoing = pack(
        me_s, node_feats, cotangent, bias_vec[None, :], sends, hubs, sub, n_feat
    )
    first = after(first, w[1])
    first = lax.all_to_all(first, "feat", 0, 0, tiled=True)
    incoming = [outgoing[0]] + [over_dom(outgoing[k], k) for k in range(1, n_dom)]

    halo_tile = n_own + 2 * ((tile_src - n_own) ^ me)
    hub_tile = n_own + 2 * ((tile_src - n_own - n_dom) ^ me) + 1
    place = jnp.where(
        tile_src < n_own, tile_src, jnp.where(tile_src < n_own + n_dom, halo_tile, hub_tile)
    )
    n_pos = n_dst * n_src
    slot = jnp.arange(tile_dst.shape[0], dtype=jnp.int32)
    key = jnp.where(slot < tile_count[0], tile_dst * n_src + place, n_pos)
    before = (key[None, :] < key[:, None]) | (
        (key[None, :] == key[:, None]) & (slot[None, :] < slot[:, None])
    )
    rank = jnp.sum(before.astype(jnp.int32), axis=1)
    order = jnp.sum(jnp.where(rank[:, None] == slot[None, :], slot[:, None], 0), axis=0)
    order = jnp.concatenate([order, jnp.zeros((2,), jnp.int32)])
    ends = jnp.arange(n_pos + 1, dtype=jnp.int32)
    start = jnp.sum((key[None, :] < ends[:, None]).astype(jnp.int32), axis=1)
    a_own, a_ext, agg = build_dense(
        tile_vals, order, start, node_feats, incoming, n_dst, n_src, n_own, n_feat
    )

    w[-1] = after(w[-1], agg)
    agg = after(agg, first)
    first = after(first, w[-1])
    w.append(over_feat(jnp.concatenate(w, axis=0), 1))
    agg = lax.all_to_all(agg, "feat", 0, 0, tiled=True).reshape(width, piece)

    bias, even, odd, *cross = whole_call(
        functools.partial(split_kernel, blocks, n_dom),
        "split",
        1.5,
        [
            shape(small, T, kind=F32),
            shape(small + width, piece),
            shape(small + width, piece),
        ]
        + [shape(2 * small + width, piece)] * (ny - 1),
        me_s,
        block_s,
        first,
        scalars=2,
    )
    cross = [over_dom(c, 2 * (j + 1)) for j, c in enumerate(cross)]
    evens = [even] + cross
    odds = [over_dom(odd, 1)] + [over_dom(c[small:], 1) for c in cross]
    agg_even = [agg] + [over_dom(agg, 2 * j) for j in range(1, ny)]
    agg_odd = [over_dom(a, 1) for a in agg_even]
    aggs = [a for pair in zip(agg_even, agg_odd) for a in pair]

    grad, act_even, act_odd, gagg_even, gagg_odd = whole_call(
        functools.partial(dense_kernel, ny, len(w)),
        "dense",
        3.0,
        [
            shape(n_dom, small, piece),
            shape(ny, small, piece),
            shape(ny, small, piece),
            shape(ny, width, piece),
            shape(ny, width, piece),
        ],
        bias,
        *w,
        *evens,
        *odds,
        *aggs,
    )

    got = over_dom(gagg_odd, 1)
    pair = whole_call(pair_kernel, "pair", 1.0, [shape(width, piece)] * ny, gagg_even, got)

    back_even, back_odd, parts, parts_odd = whole_call(
        functools.partial(grads_kernel, ny, len(w)),
        "grads",
        3.0,
        [
            shape(ny, width + small, piece),
            shape(ny, width + small, piece),
            shape(nz, sub, 2 * width + T),
            shape(nz, sub, 2 * width + T),
        ],
        grad,
        act_even,
        act_odd,
        *w,
        *evens,
        *odds,
        *aggs,
    )
    parts_odd, back_odd = after(parts_odd, pair), after(back_odd, pair)

    gagg = pair[0].astype(F32)
    for j in range(1, ny):
        gagg += over_dom(pair[j], 2 * j).astype(F32)
    gagg = gagg.astype(BF).reshape(n_feat, rows, piece)
    from_x = over_feat(parts_odd, 1)
    from_core = over_dom(back_odd, 1)
    from_x, from_core = after(from_x, gagg), after(from_core, gagg)

    gagg = lax.all_to_all(gagg, "feat", 0, 0, tiled=True)
    back = whole_call(
        functools.partial(back_pair_kernel, width),
        "back_pair",
        1.0,
        [shape(width + 2 * small, piece)] * ny,
        back_even,
        from_core,
    )
    back = [back[0]] + [over_dom(back[j], 2 * j) for j in range(1, ny)]
    parts = whole_call(pair_kernel, "x_sum", 1.0, [shape(sub, 2 * width + T)] * nz, parts, from_x)
    gagg = after(gagg, parts)
    parts = [parts[0]] + [over_feat(parts[j], blocks[j]) for j in range(1, nz)]

    gagg, *halo_grad = whole_call(
        halo_grad_kernel,
        "halo_grads",
        1.0,
        [shape(rows, dst_rows)] + [shape(rows, 2 * T)] * n_dom,
        gagg,
        a_ext,
    )
    back = after(back, halo_grad, parts)
    returned = [halo_grad[0]] + [over_dom(halo_grad[k], k) for k in range(1, n_dom)]

    back = whole_call(
        functools.partial(back_pack_kernel, blocks),
        "back_pack",
        1.0,
        shape(n_feat, 2 * n_dom, sub, piece),
        me_s,
        block_s,
        *back,
        scalars=2,
    )
    back = lax.all_to_all(back, "feat", 0, 0, tiled=True).reshape(n_feat, 2 * rows, piece)
    total = whole_call(
        functools.partial(wsum_kernel, width), "w_sum", 1.0, shape(sub, 2 * width + T), *parts
    )
    whole = [total] + [over_dom(total, 2 * j) for j in range(1, ny)]
    grads = finish_rest(me_s, gagg, a_own, returned, sends, hubs, dst_rows)
    whole[1:] = [after(e, grads) for e in whole[1:]]
    whole = [t for e in whole for t in (e, over_dom(e, 1))]
    grad_self, grad_neigh, grad_bias = whole_call(
        wout_kernel,
        "w_out",
        1.0,
        [
            shape(n_dom, sub, width, kind=F32),
            shape(n_dom, sub, width, kind=F32),
            shape(n_dom, sub, T, kind=F32),
        ],
        me_s,
        *whole,
        scalars=1,
    )

    grad_feats, activations = finish_dst(
        me_s, gagg, a_own, returned, sends, hubs, back, grads
    )
    return (
        activations,
        grad_feats,
        grad_self.reshape(n_dom * sub, width),
        grad_neigh.reshape(n_dom * sub, width),
        grad_bias[:, :, 0].reshape(n_dom * sub),
    )


def solution(mesh):
    return jax.shard_map(
        body,
        mesh=mesh,
        in_specs=(
            P("feat", "dom"),
            P("dom"),
            P("dom"),
            P("dom"),
            P("dom"),
            P("dom"),
            P("dom", None, None),
            P("feat", None),
            P("feat", None),
            P("feat"),
            P("feat", "dom"),
        ),
        out_specs=(P("feat", "dom"), P("feat", "dom"), P("feat", None), P("feat", None), P("feat")),
        check_vma=False,
    )
```

```python
import functools

import jax
import jax.numpy as jnp
from jax import lax
from jax.experimental import pallas as pl
from jax.experimental.pallas import tpu as pltpu
from jax.sharding import PartitionSpec as P

T = 128
BF = jnp.bfloat16
F32 = jnp.float32
MIB = 1 << 20
VMEM = pl.BlockSpec(memory_space=pltpu.VMEM)
SMEM = pl.BlockSpec(memory_space=pltpu.SMEM)


def dot(left, right, dims):
    return lax.dot_general(left, right, (dims, ((), ())), preferred_element_type=F32)


def shape(*dims, kind=BF):
    return jax.ShapeDtypeStruct(dims, kind)


def whole_call(kernel, name, micros, out_shape, *args, scalars=0, mib=24):
    many = isinstance(out_shape, (list, tuple))
    return pl.pallas_call(
        kernel,
        out_shape=out_shape,
        in_specs=[SMEM] * scalars + [VMEM] * (len(args) - scalars),
        out_specs=[VMEM] * len(out_shape) if many else VMEM,
        compiler_params=pltpu.CompilerParams(vmem_limit_bytes=mib * MIB),
        cost_estimate=pl.CostEstimate(
            flops=0, bytes_accessed=int(micros * 3.0e6), transcendentals=0
        ),
        name=name,
    )(*args)


def pack_kernel(sub, me_ref, x_ref, cot_ref, bias_ref, send_ref, hub_ref, first_ref, *out_refs):
    groups, chunks, _, piece = first_ref.shape
    n = x_ref.shape[0] // sub
    bias = bias_ref[...]
    high = bias.astype(BF).astype(F32)
    row = lax.broadcasted_iota(jnp.int32, (sub, piece), 0)
    tail = jnp.where(row == 0, high, jnp.where(row == 1, bias - high, 0.0)).astype(BF)
    for b in range(groups):
        cols = slice(b * piece, (b + 1) * piece)
        first_ref[b, :n] = x_ref[:, cols].reshape(n, sub, piece)
        first_ref[b, n : 2 * n] = cot_ref[:, cols].reshape(n, sub, piece)
        first_ref[b, 2 * n] = tail
    x = x_ref[...]
    rows = lax.broadcasted_iota(jnp.int32, (x.shape[1], T), 0)
    readers = len(out_refs)
    for q in range(readers + 1):
        idx = send_ref[pl.ds(me_ref[0] ^ q, 1), :] if q < readers else hub_ref[...]
        hot = (rows == idx).astype(F32).astype(BF)
        got = dot(x, hot, ((1,), (0,))).astype(BF)
        if q < readers:
            out_refs[q][:, :T] = got
        else:
            for r in range(readers):
                out_refs[r][:, T:] = got


def pack(me, x, cot, bias, sends, hubs, sub, n_feat):
    n_dom = sends.shape[0]
    rows = x.shape[0]
    args = (x, cot, bias, sends, hubs)
    outs = [shape(n_feat, 2 * n_dom + 1, sub, cot.shape[1] // n_feat)]
    outs += [shape(rows, 2 * T)] * n_dom
    return pl.pallas_call(
        functools.partial(pack_kernel, sub),
        out_shape=outs,
        grid=(1,),
        in_specs=[SMEM] + [pl.BlockSpec(a.shape, lambda i, n=a.ndim: (0,) * n) for a in args],
        out_specs=[pl.BlockSpec(o.shape, lambda i, n=len(o.shape): (0,) * n) for o in outs],
        compiler_params=pltpu.CompilerParams(vmem_limit_bytes=60 * MIB),
        cost_estimate=pl.CostEstimate(flops=0, bytes_accessed=12000000, transcendentals=0),
        name="pack",
    )(me, *args)


def build_kernel(n_own, order_ref, start_ref, x_ref, vals_hbm, *refs):
    *halo_refs, own_ref, ext_ref, agg_ref, vals, sems = refs
    step = pl.program_id(0)
    slots = vals_hbm.shape[0]
    n_src = n_own + ext_ref.shape[1] // T
    chunks = sems.shape[0]
    per = slots // chunks

    def piece(i):
        span = pl.ds(i * per, per)
        return pltpu.make_async_copy(vals_hbm.at[span], vals.at[span], sems.at[i])

    @pl.when(step == 0)
    def _():
        for i in range(chunks):
            piece(i).start()
        vals[slots] = jnp.zeros((T, T), BF)
        for i in range(chunks):
            piece(i).wait()

    for v in range(own_ref.shape[0] // T):
        rows = slice(v * T, (v + 1) * T)
        for s in range(n_src):
            p = (step * (own_ref.shape[0] // T) + v) * n_src + s
            first, last = start_ref[p], start_ref[p + 1]
            one = jnp.where(last > first, order_ref[first], slots)
            two = jnp.where(last > first + 1, order_ref[first + 1], slots)
            total = vals[one].astype(F32) + vals[two].astype(F32)

            def more(i, total):
                return total + vals[order_ref[i]].astype(F32)

            total = lax.fori_loop(first + 2, last, more, total).astype(BF)
            if s < n_own:
                own_ref[rows, s * T : (s + 1) * T] = total
            else:
                ext_ref[rows, (s - n_own) * T : (s - n_own + 1) * T] = total
    halo = jnp.concatenate([r[...] for r in halo_refs], axis=1)
    total = dot(x_ref[...], own_ref[...], ((1,), (1,)))
    total = (total + dot(halo, ext_ref[...], ((1,), (1,)))).astype(BF)
    piece_n = agg_ref.shape[2]
    for b in range(agg_ref.shape[0]):
        agg_ref[b] = total[:, b * piece_n : (b + 1) * piece_n]


def build_dense(vals, order, start, x, halos, n_dst, n_src, n_own, n_feat):
    rows = x.shape[0]
    piece = n_dst * T // n_feat
    ext = (n_src - n_own) * T
    return pl.pallas_call(
        functools.partial(build_kernel, n_own),
        out_shape=(
            shape(n_dst * T, n_own * T),
            shape(n_dst * T, ext),
            shape(n_feat, rows, piece),
        ),
        grid_spec=pltpu.PrefetchScalarGridSpec(
            num_scalar_prefetch=2,
            grid=(n_dst // 2,),
            in_specs=[VMEM, pl.BlockSpec(memory_space=pl.ANY)] + [VMEM] * len(halos),
            out_specs=[
                pl.BlockSpec((2 * T, n_own * T), lambda u, *_: (u, 0)),
                pl.BlockSpec((2 * T, ext), lambda u, *_: (u, 0)),
                pl.BlockSpec((2 * T // piece, rows, piece), lambda u, *_: (u, 0, 0)),
            ],
            scratch_shapes=[
                pltpu.VMEM((vals.shape[0] + 1, T, T), BF),
                pltpu.SemaphoreType.DMA((8,)),
            ],
        ),
        compiler_params=pltpu.CompilerParams(vmem_limit_bytes=58 * MIB),
        cost_estimate=pl.CostEstimate(flops=0, bytes_accessed=30000000, transcendentals=0),
        name="build_dense",
    )(order, start, x, vals, *halos)


def split_kernel(blocks, n_dom, me_ref, block_ref, first_ref, bias_ref, *out_refs):
    _, _, sub, piece = first_ref.shape
    n = (first_ref.shape[1] - 1) // 2
    small = len(blocks) * sub
    width = len(blocks) * n * sub
    x = first_ref[:, :n].reshape(width, piece)
    row = lax.broadcasted_iota(jnp.int32, (sub, piece), 0) + me_ref[0] * sub
    lane = lax.broadcasted_iota(jnp.int32, (sub, piece), 1)
    for i, k in enumerate(blocks):
        b = block_ref[0] ^ k
        both = first_ref[b, 2 * n, 0:1].astype(F32) + first_ref[b, 2 * n, 1:2].astype(F32)
        mine = jnp.sum(jnp.where(row == lane, both, 0.0), axis=1, keepdims=True)
        bias_ref[i * sub : (i + 1) * sub, :] = jnp.broadcast_to(mine, (sub, T))
    even, odd = out_refs[0], out_refs[1]
    even[small:] = x
    odd[:width] = x
    for i, k in enumerate(blocks):
        b = block_ref[0] ^ k
        even[i * sub : (i + 1) * sub] = first_ref[b, n + me_ref[0]]
        odd[width + i * sub : width + (i + 1) * sub] = first_ref[b, n + (me_ref[0] ^ 1)]
    for j in range(1, n_dom // 2):
        ref = out_refs[1 + j]
        ref[small : small + width] = x
        for i, k in enumerate(blocks):
            b = block_ref[0] ^ k
            at = small + width + i * sub
            ref[i * sub : (i + 1) * sub] = first_ref[b, n + (me_ref[0] ^ (2 * j))]
            ref[at : at + sub] = first_ref[b, n + (me_ref[0] ^ (2 * j + 1))]


def weights(refs):
    return [jnp.concatenate([r[g, m] for r in refs for g in range(r.shape[0])]) for m in (0, 1)]


def dense_kernel(ny, nw, bias_ref, *refs):
    w_refs, refs = refs[:nw], refs[nw:]
    even, odd, agg = refs[:ny], refs[ny : 2 * ny], refs[2 * ny : 4 * ny]
    g_ref, act_even, act_odd, gagg_even, gagg_odd = refs[4 * ny :]
    w_self, w_neigh = weights(w_refs)
    small, width = w_self.shape
    bias = bias_ref[:, :1]
    for k in range(2 * ny):
        j = k // 2
        if k % 2 == 0:
            cot, x = even[j][:small, :], even[j][small : small + width, :]
            act_ref, gagg_ref = act_even, gagg_even
        else:
            x, cot = odd[j][:width, :], odd[j][width:, :]
            act_ref, gagg_ref = act_odd, gagg_odd
        pre = dot(w_self, x, ((1,), (0,)))
        pre += dot(w_neigh, agg[k][...], ((1,), (0,)))
        pre += bias
        sig = 1.0 / (1.0 + jnp.exp(-pre))
        act_ref[j] = (pre * sig).astype(BF)
        grad = (cot.astype(F32) * sig * (1.0 + pre * (1.0 - sig))).astype(BF)
        g_ref[k] = grad
        gagg_ref[j] = dot(w_neigh, grad, ((0,), (0,))).astype(BF)


def grads_kernel(ny, nw, g_ref, act_even, act_odd, *refs):
    w_refs, refs = refs[:nw], refs[nw:]
    even, odd, agg = refs[:ny], refs[ny : 2 * ny], refs[2 * ny : 4 * ny]
    back_even, back_odd, *out_refs = refs[4 * ny :]
    w_self, _ = weights(w_refs)
    small, width = w_self.shape
    sub = out_refs[0].shape[1]
    xs = []
    for k in range(2 * ny):
        j = k // 2
        act_ref, back_ref = (act_odd, back_odd) if k % 2 else (act_even, back_even)
        back_ref[j, :width] = dot(w_self, g_ref[k], ((0,), (0,))).astype(BF)
        back_ref[j, width:] = act_ref[j]
        xs.append(odd[j][:width, :] if k % 2 else even[j][small : small + width, :])
    grad = jnp.concatenate([g_ref[k] for k in range(2 * ny)], axis=1)
    own = dot(grad, jnp.concatenate(xs, axis=1), ((1,), (1,))).astype(BF)
    neigh = dot(grad, jnp.concatenate([r[...] for r in agg], axis=1), ((1,), (1,))).astype(BF)
    total = jnp.sum(grad.astype(F32), axis=1, keepdims=True)
    high = total.astype(BF).astype(F32)
    lane = lax.broadcasted_iota(jnp.int32, (small, T), 1)
    both = jnp.where(lane == 0, high, jnp.where(lane == 1, total - high, 0.0)).astype(BF)
    nz = out_refs[0].shape[0]
    for i in range(small // sub):
        rows, out_ref = slice(i * sub, (i + 1) * sub), out_refs[i // nz]
        out_ref[i % nz, :, :width] = own[rows]
        out_ref[i % nz, :, width : 2 * width] = neigh[rows]
        out_ref[i % nz, :, 2 * width :] = both[rows]


def pair_kernel(even_ref, got_ref, *out_refs):
    for j, out_ref in enumerate(out_refs):
        out_ref[...] = (even_ref[j].astype(F32) + got_ref[j].astype(F32)).astype(BF)


def back_pair_kernel(width, even_ref, got_ref, *out_refs):
    for j, out_ref in enumerate(out_refs):
        both = even_ref[j, :width].astype(F32) + got_ref[j, :width].astype(F32)
        small = even_ref.shape[1] - width
        out_ref[:width] = both.astype(BF)
        out_ref[width : width + small] = even_ref[j, width:]
        out_ref[width + small :] = got_ref[j, width:]


def back_pack_kernel(blocks, ny, me_ref, block_ref, *refs):
    gagg_refs, in_refs, out_ref = refs[:ny], refs[ny:-1], refs[-1]
    groups, chunks, sub, piece = out_ref.shape
    n = chunks // 3
    width = groups * n * sub
    small = groups * sub
    total = gagg_refs[0][...].astype(F32)
    own = in_refs[0][:width].astype(F32)
    for j in range(1, ny):
        total += gagg_refs[j][...].astype(F32)
        own += in_refs[j][:width].astype(F32)
    out_ref[:, :n] = total.astype(BF).reshape(groups, n, sub, piece)
    out_ref[:, n : 2 * n] = own.astype(BF).reshape(groups, n, sub, piece)
    for k in range(2 * ny):
        d = me_ref[0] ^ k
        for i, f in enumerate(blocks):
            at = width + (k % 2) * small + i * sub
            out_ref[block_ref[0] ^ f, 2 * n + d] = in_refs[k // 2][at : at + sub]


def wsum_kernel(width, *refs):
    *in_refs, out_ref = refs
    total = in_refs[0][...].astype(F32)
    for r in in_refs[1:]:
        total += r[...].astype(F32)
    out_ref[:, : 2 * width] = total[:, : 2 * width].astype(BF)
    bias = jnp.sum(total[:, 2 * width :], axis=1, keepdims=True)
    high = bias.astype(BF).astype(F32)
    lane = lax.broadcasted_iota(jnp.int32, (total.shape[0], T), 1)
    both = jnp.where(lane == 0, high, jnp.where(lane == 1, bias - high, 0.0))
    out_ref[:, 2 * width :] = both.astype(BF)


def wout_kernel(me_ref, *refs):
    *in_refs, self_ref, neigh_ref, bias_ref = refs
    width = self_ref.shape[2]
    for k, ref in enumerate(in_refs):
        d = me_ref[0] ^ k
        self_ref[d] = ref[:, :width].astype(F32)
        neigh_ref[d] = ref[:, width : 2 * width].astype(F32)
        total = jnp.sum(ref[:, 2 * width :].astype(F32), axis=1, keepdims=True)
        bias_ref[d] = jnp.broadcast_to(total, bias_ref.shape[1:])


def halo_grad_kernel(ga_ref, ext_ref, flat_ref, *out_refs):
    rows = flat_ref.shape[0]
    ga = jnp.concatenate([ga_ref[b, :rows] for b in range(ga_ref.shape[0])], axis=1)
    flat_ref[...] = ga
    for k, out_ref in enumerate(out_refs):
        span = slice(k * 2 * T, (k + 1) * 2 * T)
        out_ref[...] = dot(ga, ext_ref[:, span], ((1,), (0,))).astype(BF)


def add_returned(total, at, me_ref, send_ref, hub_ref, ret_refs):
    rows = lax.broadcasted_iota(jnp.int32, (total.shape[1], T), 0) + at
    hub = (rows == hub_ref[...]).astype(F32).astype(BF)
    for q, ret_ref in enumerate(ret_refs):
        idx = send_ref[pl.ds(me_ref[0] ^ q, 1), :]
        sent = (rows == idx).astype(F32).astype(BF)
        total += dot(ret_ref[:, :T], sent, ((1,), (1,)))
        total += dot(ret_ref[:, T:], hub, ((1,), (1,)))
    return total


def finish_kernel(top, me_ref, ga_ref, own_ref, send_ref, hub_ref, back_ref, *refs):
    *ret_refs, out_ref, act_ref = refs
    step = pl.program_id(0)
    rows, width = out_ref.shape
    total = dot(ga_ref[...], own_ref[...], ((1,), (0,)))
    total = add_returned(total, step * width, me_ref, send_ref, hub_ref, ret_refs)
    out_ref[...] = total

    @pl.when(step < top)
    def _():
        groups = range(back_ref.shape[0])
        own = jnp.concatenate([back_ref[b, rows : 2 * rows] for b in groups], axis=1)
        act_ref[...] = jnp.concatenate([back_ref[b, 2 * rows :] for b in groups], axis=1)
        out_ref[...] = total + own.astype(F32)


def finish(me, ga, own, ret, sends, hubs, back):
    rows, n = ga.shape[0], own.shape[1]
    groups, _, piece = back.shape
    n_dst, wide = groups * piece, 512
    top = n_dst // wide

    def fixed(x):
        return pl.BlockSpec(x.shape, lambda i: (0, 0))

    return pl.pallas_call(
        functools.partial(finish_kernel, top),
        out_shape=[shape(rows, n, kind=F32), shape(rows, n_dst)],
        grid=(n // wide,),
        in_specs=[
            SMEM,
            fixed(ga),
            pl.BlockSpec((n_dst, wide), lambda i: (0, i)),
            fixed(sends),
            fixed(hubs),
            pl.BlockSpec(
                (wide // piece, 3 * rows, piece), lambda i: (jnp.minimum(i, top - 1), 0, 0)
            ),
        ]
        + [fixed(r) for r in ret],
        out_specs=[
            pl.BlockSpec((rows, wide), lambda i: (0, i)),
            pl.BlockSpec((rows, wide), lambda i: (0, jnp.minimum(i, top - 1))),
        ],
        compiler_params=pltpu.CompilerParams(vmem_limit_bytes=56 * MIB),
        cost_estimate=pl.CostEstimate(flops=0, bytes_accessed=24000000, transcendentals=0),
        name="finish",
    )(me, ga, own, sends, hubs, back, *ret)


def body(
    node_feats,
    send_rows,
    hub_rows,
    tile_dst,
    tile_src,
    tile_count,
    tile_vals,
    w_self,
    w_neigh,
    bias_vec,
    cotangent,
):
    n_dom = lax.axis_size("dom")
    n_feat = lax.axis_size("feat")
    ny, nz = n_dom // 2, n_feat // 2
    rows = node_feats.shape[0]
    own_rows = node_feats.shape[1]
    dst_rows = cotangent.shape[1]
    width = w_self.shape[1]
    n_own, n_dst = own_rows // T, dst_rows // T
    n_src = n_own + 2 * n_dom
    piece = dst_rows // n_feat
    sub = w_self.shape[0] // n_dom
    small = n_feat * sub
    me = lax.axis_index("dom")
    block = lax.axis_index("feat")
    me_s, block_s = me.reshape(1), block.reshape(1)

    def over_dom(x, k):
        return lax.ppermute(x, "dom", [(i, i ^ k) for i in range(n_dom)])

    def over_feat(x, k):
        return lax.ppermute(x, "feat", [(i, i ^ k) for i in range(n_feat)])

    def after(x, *events):
        return lax.optimization_barrier((x, events))[0]

    mine = jnp.stack(
        [
            lax.dynamic_slice_in_dim(w_self, me * sub, sub, axis=0),
            lax.dynamic_slice_in_dim(w_neigh, me * sub, sub, axis=0),
        ]
    )
    w, blocks = [mine[None]], [0]
    for bit in [1 << i for i in range(n_feat.bit_length() - 2, 0, -1)]:
        send = w[0] if len(w) == 1 else jnp.concatenate(w, axis=0)
        w.append(over_feat(send, bit))
        blocks += [k ^ bit for k in blocks]
    blocks += [k ^ 1 for k in blocks]

    sends, hubs = send_rows.reshape(n_dom, T), hub_rows[None, :]
    first, *outgoing = pack(
        me_s, node_feats, cotangent, bias_vec[None, :], sends, hubs, sub, n_feat
    )
    first = after(first, w[1])
    first = lax.all_to_all(first, "feat", 0, 0, tiled=True)
    incoming = [outgoing[0]] + [over_dom(outgoing[k], k) for k in range(1, n_dom)]

    halo_tile = n_own + 2 * ((tile_src - n_own) ^ me)
    hub_tile = n_own + 2 * ((tile_src - n_own - n_dom) ^ me) + 1
    place = jnp.where(
        tile_src < n_own, tile_src, jnp.where(tile_src < n_own + n_dom, halo_tile, hub_tile)
    )
    n_pos = n_dst * n_src
    slot = jnp.arange(tile_dst.shape[0], dtype=jnp.int32)
    key = jnp.where(slot < tile_count[0], tile_dst * n_src + place, n_pos)
    before = (key[None, :] < key[:, None]) | (
        (key[None, :] == key[:, None]) & (slot[None, :] < slot[:, None])
    )
    rank = jnp.sum(before.astype(jnp.int32), axis=1)
    order = jnp.sum(jnp.where(rank[:, None] == slot[None, :], slot[:, None], 0), axis=0)
    order = jnp.concatenate([order, jnp.zeros((2,), jnp.int32)])
    ends = jnp.arange(n_pos + 1, dtype=jnp.int32)
    start = jnp.sum((key[None, :] < ends[:, None]).astype(jnp.int32), axis=1)
    a_own, a_ext, agg = build_dense(
        tile_vals, order, start, node_feats, incoming, n_dst, n_src, n_own, n_feat
    )

    w[-1] = after(w[-1], agg)
    agg = after(agg, first)
    first = after(first, w[-1])
    w.append(over_feat(jnp.concatenate(w, axis=0), 1))
    agg = lax.all_to_all(agg, "feat", 0, 0, tiled=True).reshape(width, piece)

    bias, even, odd, *cross = whole_call(
        functools.partial(split_kernel, blocks, n_dom),
        "split",
        1.5,
        [
            shape(small, T, kind=F32),
            shape(small + width, piece),
            shape(small + width, piece),
        ]
        + [shape(2 * small + width, piece)] * (ny - 1),
        me_s,
        block_s,
        first,
        scalars=2,
    )
    cross = [over_dom(c, 2 * (j + 1)) for j, c in enumerate(cross)]
    evens = [even] + cross
    odds = [over_dom(odd, 1)] + [over_dom(c[small:], 1) for c in cross]
    agg_even = [agg] + [over_dom(agg, 2 * j) for j in range(1, ny)]
    agg_odd = [over_dom(a, 1) for a in agg_even]
    aggs = [a for pair in zip(agg_even, agg_odd) for a in pair]

    grad, act_even, act_odd, gagg_even, gagg_odd = whole_call(
        functools.partial(dense_kernel, ny, len(w)),
        "dense",
        3.0,
        [
            shape(n_dom, small, piece),
            shape(ny, small, piece),
            shape(ny, small, piece),
            shape(ny, width, piece),
            shape(ny, width, piece),
        ],
        bias,
        *w,
        *evens,
        *odds,
        *aggs,
    )

    got = over_dom(gagg_odd, 1)
    pair = whole_call(pair_kernel, "pair", 1.0, [shape(width, piece)] * ny, gagg_even, got)

    back_even, back_odd, parts, parts_odd = whole_call(
        functools.partial(grads_kernel, ny, len(w)),
        "grads",
        3.0,
        [
            shape(ny, width + small, piece),
            shape(ny, width + small, piece),
            shape(nz, sub, 2 * width + T),
            shape(nz, sub, 2 * width + T),
        ],
        grad,
        act_even,
        act_odd,
        *w,
        *evens,
        *odds,
        *aggs,
    )
    parts_odd, back_odd = after(parts_odd, pair), after(back_odd, pair)

    gaggs = [pair[0]] + [over_dom(pair[j], 2 * j) for j in range(1, ny)]
    back = whole_call(
        functools.partial(back_pair_kernel, width),
        "back_pair",
        1.0,
        [shape(width + 2 * small, piece)] * ny,
        back_even,
        over_dom(back_odd, 1),
    )
    back = [back[0]] + [after(b, gaggs) for b in back[1:]]
    back = [back[0]] + [over_dom(back[j], 2 * j) for j in range(1, ny)]
    from_x = over_feat(parts_odd, 1)
    parts = whole_call(pair_kernel, "x_sum", 1.0, [shape(sub, 2 * width + T)] * nz, parts, from_x)
    back[1:] = [after(b, parts) for b in back[1:]]
    back = whole_call(
        functools.partial(back_pack_kernel, blocks, ny),
        "back_pack",
        1.5,
        shape(n_feat, 3 * n_dom, sub, piece),
        me_s,
        block_s,
        *gaggs,
        *back,
        scalars=2,
    )
    back = lax.all_to_all(back, "feat", 0, 0, tiled=True).reshape(n_feat, 3 * rows, piece)
    parts = [parts[0]] + [over_feat(parts[j], blocks[j]) for j in range(1, nz)]

    gagg, *halo_grad = whole_call(
        halo_grad_kernel,
        "halo_grads",
        1.0,
        [shape(rows, dst_rows)] + [shape(rows, 2 * T)] * n_dom,
        back,
        a_ext,
    )
    halo_grad = after(halo_grad, parts)
    returned = [halo_grad[0]] + [over_dom(halo_grad[k], k) for k in range(1, n_dom)]

    total = whole_call(
        functools.partial(wsum_kernel, width), "w_sum", 1.0, shape(sub, 2 * width + T), *parts
    )
    whole = [total] + [over_dom(total, 2 * j) for j in range(1, ny)]
    gagg = after(gagg, total)
    grad_feats, activations = finish(me_s, gagg, a_own, returned, sends, hubs, back)
    whole[1:] = [after(e, grad_feats) for e in whole[1:]]
    whole = [t for e in whole for t in (e, over_dom(e, 1))]
    grad_self, grad_neigh, grad_bias = whole_call(
        wout_kernel,
        "w_out",
        1.0,
        [
            shape(n_dom, sub, width, kind=F32),
            shape(n_dom, sub, width, kind=F32),
            shape(n_dom, sub, T, kind=F32),
        ],
        me_s,
        *whole,
        scalars=1,
    )

    return (
        activations,
        grad_feats,
        grad_self.reshape(n_dom * sub, width),
        grad_neigh.reshape(n_dom * sub, width),
        grad_bias[:, :, 0].reshape(n_dom * sub),
    )


def solution(mesh):
    return jax.shard_map(
        body,
        mesh=mesh,
        in_specs=(
            P("feat", "dom"),
            P("dom"),
            P("dom"),
            P("dom"),
            P("dom"),
            P("dom"),
            P("dom", None, None),
            P("feat", None),
            P("feat", None),
            P("feat"),
            P("feat", "dom"),
        ),
        out_specs=(P("feat", "dom"), P("feat", "dom"), P("feat", None), P("feat", None), P("feat")),
        check_vma=False,
    )
```

```python
import functools

import jax
import jax.numpy as jnp
from jax import lax
from jax.experimental import pallas as pl
from jax.experimental.pallas import tpu as pltpu
from jax.sharding import PartitionSpec as P

T = 128
BF = jnp.bfloat16
F32 = jnp.float32
MIB = 1 << 20
VMEM = pl.BlockSpec(memory_space=pltpu.VMEM)
SMEM = pl.BlockSpec(memory_space=pltpu.SMEM)


def dot(left, right, dims):
    return lax.dot_general(left, right, (dims, ((), ())), preferred_element_type=F32)


def shape(*dims, kind=BF):
    return jax.ShapeDtypeStruct(dims, kind)


def whole_call(kernel, name, micros, out_shape, *args, scalars=0, mib=24):
    many = isinstance(out_shape, (list, tuple))
    return pl.pallas_call(
        kernel,
        out_shape=out_shape,
        in_specs=[SMEM] * scalars + [VMEM] * (len(args) - scalars),
        out_specs=[VMEM] * len(out_shape) if many else VMEM,
        compiler_params=pltpu.CompilerParams(vmem_limit_bytes=mib * MIB),
        cost_estimate=pl.CostEstimate(
            flops=0, bytes_accessed=int(micros * 3.0e6), transcendentals=0
        ),
        name=name,
    )(*args)


def pack_kernel(sub, me_ref, x_ref, cot_ref, bias_ref, send_ref, hub_ref, first_ref, *out_refs):
    groups, chunks, _, piece = first_ref.shape
    n = x_ref.shape[0] // sub
    bias = bias_ref[...]
    high = bias.astype(BF).astype(F32)
    row = lax.broadcasted_iota(jnp.int32, (sub, piece), 0)
    tail = jnp.where(row == 0, high, jnp.where(row == 1, bias - high, 0.0)).astype(BF)
    for b in range(groups):
        cols = slice(b * piece, (b + 1) * piece)
        first_ref[b, :n] = x_ref[:, cols].reshape(n, sub, piece)
        first_ref[b, n : 2 * n] = cot_ref[:, cols].reshape(n, sub, piece)
        first_ref[b, 2 * n] = tail
    x = x_ref[...]
    rows = lax.broadcasted_iota(jnp.int32, (x.shape[1], T), 0)
    readers = len(out_refs)
    for q in range(readers + 1):
        idx = send_ref[pl.ds(me_ref[0] ^ q, 1), :] if q < readers else hub_ref[...]
        hot = (rows == idx).astype(F32).astype(BF)
        got = dot(x, hot, ((1,), (0,))).astype(BF)
        if q < readers:
            out_refs[q][:, :T] = got
        else:
            for r in range(readers):
                out_refs[r][:, T:] = got


def pack(me, x, cot, bias, sends, hubs, sub, n_feat):
    n_dom = sends.shape[0]
    rows = x.shape[0]
    args = (x, cot, bias, sends, hubs)
    outs = [shape(n_feat, 2 * n_dom + 1, sub, cot.shape[1] // n_feat)]
    outs += [shape(rows, 2 * T)] * n_dom
    return pl.pallas_call(
        functools.partial(pack_kernel, sub),
        out_shape=outs,
        grid=(1,),
        in_specs=[SMEM] + [pl.BlockSpec(a.shape, lambda i, n=a.ndim: (0,) * n) for a in args],
        out_specs=[pl.BlockSpec(o.shape, lambda i, n=len(o.shape): (0,) * n) for o in outs],
        compiler_params=pltpu.CompilerParams(vmem_limit_bytes=60 * MIB),
        cost_estimate=pl.CostEstimate(flops=0, bytes_accessed=12000000, transcendentals=0),
        name="pack",
    )(me, *args)


def build_kernel(n_own, order_ref, start_ref, x_ref, vals_hbm, *refs):
    *halo_refs, own_ref, ext_ref, agg_ref, vals, sems = refs
    step = pl.program_id(0)
    slots = vals_hbm.shape[0]
    n_src = n_own + ext_ref.shape[1] // T
    chunks = sems.shape[0]
    per = slots // chunks

    def piece(i):
        span = pl.ds(i * per, per)
        return pltpu.make_async_copy(vals_hbm.at[span], vals.at[span], sems.at[i])

    @pl.when(step == 0)
    def _():
        for i in range(chunks):
            piece(i).start()
        vals[slots] = jnp.zeros((T, T), BF)
        for i in range(chunks):
            piece(i).wait()

    for v in range(own_ref.shape[0] // T):
        rows = slice(v * T, (v + 1) * T)
        for s in range(n_src):
            p = (step * (own_ref.shape[0] // T) + v) * n_src + s
            first, last = start_ref[p], start_ref[p + 1]
            one = jnp.where(last > first, order_ref[first], slots)
            two = jnp.where(last > first + 1, order_ref[first + 1], slots)
            total = vals[one].astype(F32) + vals[two].astype(F32)

            def more(i, total):
                return total + vals[order_ref[i]].astype(F32)

            total = lax.fori_loop(first + 2, last, more, total).astype(BF)
            if s < n_own:
                own_ref[rows, s * T : (s + 1) * T] = total
            else:
                ext_ref[rows, (s - n_own) * T : (s - n_own + 1) * T] = total
    halo = jnp.concatenate([r[...] for r in halo_refs], axis=1)
    total = dot(x_ref[...], own_ref[...], ((1,), (1,)))
    total = (total + dot(halo, ext_ref[...], ((1,), (1,)))).astype(BF)
    piece_n = agg_ref.shape[2]
    for b in range(agg_ref.shape[0]):
        agg_ref[b] = total[:, b * piece_n : (b + 1) * piece_n]


def build_dense(vals, order, start, x, halos, n_dst, n_src, n_own, n_feat):
    rows = x.shape[0]
    piece = n_dst * T // n_feat
    ext = (n_src - n_own) * T
    return pl.pallas_call(
        functools.partial(build_kernel, n_own),
        out_shape=(
            shape(n_dst * T, n_own * T),
            shape(n_dst * T, ext),
            shape(n_feat, rows, piece),
        ),
        grid_spec=pltpu.PrefetchScalarGridSpec(
            num_scalar_prefetch=2,
            grid=(n_dst // 2,),
            in_specs=[VMEM, pl.BlockSpec(memory_space=pl.ANY)] + [VMEM] * len(halos),
            out_specs=[
                pl.BlockSpec((2 * T, n_own * T), lambda u, *_: (u, 0)),
                pl.BlockSpec((2 * T, ext), lambda u, *_: (u, 0)),
                pl.BlockSpec((2 * T // piece, rows, piece), lambda u, *_: (u, 0, 0)),
            ],
            scratch_shapes=[
                pltpu.VMEM((vals.shape[0] + 1, T, T), BF),
                pltpu.SemaphoreType.DMA((8,)),
            ],
        ),
        compiler_params=pltpu.CompilerParams(vmem_limit_bytes=58 * MIB),
        cost_estimate=pl.CostEstimate(flops=0, bytes_accessed=30000000, transcendentals=0),
        name="build_dense",
    )(order, start, x, vals, *halos)


def split_kernel(blocks, n_dom, me_ref, block_ref, first_ref, bias_ref, *out_refs):
    _, _, sub, piece = first_ref.shape
    n = (first_ref.shape[1] - 1) // 2
    small = len(blocks) * sub
    width = len(blocks) * n * sub
    x = first_ref[:, :n].reshape(width, piece)
    row = lax.broadcasted_iota(jnp.int32, (sub, piece), 0) + me_ref[0] * sub
    lane = lax.broadcasted_iota(jnp.int32, (sub, piece), 1)
    for i, k in enumerate(blocks):
        b = block_ref[0] ^ k
        both = first_ref[b, 2 * n, 0:1].astype(F32) + first_ref[b, 2 * n, 1:2].astype(F32)
        mine = jnp.sum(jnp.where(row == lane, both, 0.0), axis=1, keepdims=True)
        bias_ref[i * sub : (i + 1) * sub, :] = jnp.broadcast_to(mine, (sub, T))
    even, odd = out_refs[0], out_refs[1]
    even[small:] = x
    odd[:width] = x
    for i, k in enumerate(blocks):
        b = block_ref[0] ^ k
        even[i * sub : (i + 1) * sub] = first_ref[b, n + me_ref[0]]
        odd[width + i * sub : width + (i + 1) * sub] = first_ref[b, n + (me_ref[0] ^ 1)]
    for j in range(1, n_dom // 2):
        ref = out_refs[1 + j]
        ref[small : small + width] = x
        for i, k in enumerate(blocks):
            b = block_ref[0] ^ k
            at = small + width + i * sub
            ref[i * sub : (i + 1) * sub] = first_ref[b, n + (me_ref[0] ^ (2 * j))]
            ref[at : at + sub] = first_ref[b, n + (me_ref[0] ^ (2 * j + 1))]


def weights(refs):
    return [jnp.concatenate([r[g, m] for r in refs for g in range(r.shape[0])]) for m in (0, 1)]


def dense_kernel(ny, nw, bias_ref, *refs):
    w_refs, refs = refs[:nw], refs[nw:]
    even, odd, agg = refs[:ny], refs[ny : 2 * ny], refs[2 * ny : 4 * ny]
    g_ref, act_even, act_odd, gagg_even, gagg_odd = refs[4 * ny :]
    w_self, w_neigh = weights(w_refs)
    small, width = w_self.shape
    bias = bias_ref[:, :1]
    for k in range(2 * ny):
        j = k // 2
        if k % 2 == 0:
            cot, x = even[j][:small, :], even[j][small : small + width, :]
            act_ref, gagg_ref = act_even, gagg_even
        else:
            x, cot = odd[j][:width, :], odd[j][width:, :]
            act_ref, gagg_ref = act_odd, gagg_odd
        pre = dot(w_self, x, ((1,), (0,)))
        pre += dot(w_neigh, agg[k][...], ((1,), (0,)))
        pre += bias
        sig = 1.0 / (1.0 + jnp.exp(-pre))
        act_ref[j] = (pre * sig).astype(BF)
        grad = (cot.astype(F32) * sig * (1.0 + pre * (1.0 - sig))).astype(BF)
        g_ref[k] = grad
        gagg_ref[j] = dot(w_neigh, grad, ((0,), (0,))).astype(BF)


def grads_kernel(ny, nw, g_ref, act_even, act_odd, *refs):
    w_refs, refs = refs[:nw], refs[nw:]
    even, odd, agg = refs[:ny], refs[ny : 2 * ny], refs[2 * ny : 4 * ny]
    back_even, back_odd, *out_refs = refs[4 * ny :]
    w_self, _ = weights(w_refs)
    small, width = w_self.shape
    sub = out_refs[0].shape[1]
    xs = []
    for k in range(2 * ny):
        j = k // 2
        act_ref, back_ref = (act_odd, back_odd) if k % 2 else (act_even, back_even)
        back_ref[j, :width] = dot(w_self, g_ref[k], ((0,), (0,))).astype(BF)
        back_ref[j, width:] = act_ref[j]
        xs.append(odd[j][:width, :] if k % 2 else even[j][small : small + width, :])
    grad = jnp.concatenate([g_ref[k] for k in range(2 * ny)], axis=1)
    own = dot(grad, jnp.concatenate(xs, axis=1), ((1,), (1,))).astype(BF)
    neigh = dot(grad, jnp.concatenate([r[...] for r in agg], axis=1), ((1,), (1,))).astype(BF)
    total = jnp.sum(grad.astype(F32), axis=1, keepdims=True)
    high = total.astype(BF).astype(F32)
    lane = lax.broadcasted_iota(jnp.int32, (small, T), 1)
    both = jnp.where(lane == 0, high, jnp.where(lane == 1, total - high, 0.0)).astype(BF)
    nz = out_refs[0].shape[0]
    for i in range(small // sub):
        rows, out_ref = slice(i * sub, (i + 1) * sub), out_refs[i // nz]
        out_ref[i % nz, :, :width] = own[rows]
        out_ref[i % nz, :, width : 2 * width] = neigh[rows]
        out_ref[i % nz, :, 2 * width :] = both[rows]


def pair_kernel(even_ref, got_ref, *out_refs):
    for j, out_ref in enumerate(out_refs):
        out_ref[...] = (even_ref[j].astype(F32) + got_ref[j].astype(F32)).astype(BF)


def back_pair_kernel(width, even_ref, got_ref, *out_refs):
    for j, out_ref in enumerate(out_refs):
        both = even_ref[j, :width].astype(F32) + got_ref[j, :width].astype(F32)
        small = even_ref.shape[1] - width
        out_ref[:width] = both.astype(BF)
        out_ref[width : width + small] = even_ref[j, width:]
        out_ref[width + small :] = got_ref[j, width:]


def back_pack_kernel(blocks, me_ref, block_ref, *refs):
    *in_refs, out_ref = refs
    groups, chunks, sub, piece = out_ref.shape
    n = chunks // 2
    width = groups * n * sub
    small = groups * sub
    total = in_refs[0][:width].astype(F32)
    for r in in_refs[1:]:
        total += r[:width].astype(F32)
    out_ref[:, :n] = total.astype(BF).reshape(groups, n, sub, piece)
    for k in range(2 * len(in_refs)):
        d = me_ref[0] ^ k
        for i, f in enumerate(blocks):
            at = width + (k % 2) * small + i * sub
            out_ref[block_ref[0] ^ f, n + d] = in_refs[k // 2][at : at + sub]


def wsum_kernel(width, *refs):
    *in_refs, out_ref = refs
    total = in_refs[0][...].astype(F32)
    for r in in_refs[1:]:
        total += r[...].astype(F32)
    out_ref[:, : 2 * width] = total[:, : 2 * width].astype(BF)
    bias = jnp.sum(total[:, 2 * width :], axis=1, keepdims=True)
    high = bias.astype(BF).astype(F32)
    lane = lax.broadcasted_iota(jnp.int32, (total.shape[0], T), 1)
    both = jnp.where(lane == 0, high, jnp.where(lane == 1, bias - high, 0.0))
    out_ref[:, 2 * width :] = both.astype(BF)


def wout_kernel(me_ref, *refs):
    *in_refs, self_ref, neigh_ref, bias_ref = refs
    width = self_ref.shape[2]
    for k, ref in enumerate(in_refs):
        d = me_ref[0] ^ k
        self_ref[d] = ref[:, :width].astype(F32)
        neigh_ref[d] = ref[:, width : 2 * width].astype(F32)
        total = jnp.sum(ref[:, 2 * width :].astype(F32), axis=1, keepdims=True)
        bias_ref[d] = jnp.broadcast_to(total, bias_ref.shape[1:])


def halo_grad_kernel(ga_ref, ext_ref, flat_ref, *out_refs):
    ga = jnp.concatenate([ga_ref[b] for b in range(ga_ref.shape[0])], axis=1)
    flat_ref[...] = ga
    for k, out_ref in enumerate(out_refs):
        span = slice(k * 2 * T, (k + 1) * 2 * T)
        out_ref[...] = dot(ga, ext_ref[:, span], ((1,), (0,))).astype(BF)


def add_returned(total, at, me_ref, send_ref, hub_ref, ret_refs):
    rows = lax.broadcasted_iota(jnp.int32, (total.shape[1], T), 0) + at
    hub = (rows == hub_ref[...]).astype(F32).astype(BF)
    hots, cols, hubs = [], [], 0.0
    for q, ret_ref in enumerate(ret_refs):
        idx = send_ref[pl.ds(me_ref[0] ^ q, 1), :]
        hots.append((rows == idx).astype(F32).astype(BF))
        cols.append(ret_ref[:, :T])
        hubs += ret_ref[:, T:].astype(F32)
    high = hubs.astype(BF)
    cols += [high, (hubs - high.astype(F32)).astype(BF)]
    hots += [hub, hub]
    return total + dot(jnp.concatenate(cols, axis=1), jnp.concatenate(hots, axis=1), ((1,), (1,)))


def finish_rest_kernel(top, me_ref, ga_ref, own_ref, send_ref, hub_ref, *refs):
    *ret_refs, out_ref = refs
    at = (pl.program_id(0) + top) * out_ref.shape[1]
    total = dot(ga_ref[...], own_ref[...], ((1,), (0,)))
    out_ref[...] = add_returned(total, at, me_ref, send_ref, hub_ref, ret_refs)


def finish_dst_kernel(me_ref, ga_ref, own_ref, send_ref, hub_ref, back_ref, grads_ref, *refs):
    *ret_refs, out_ref, act_ref = refs
    rows = ga_ref.shape[0]
    groups = range(back_ref.shape[0])
    own = jnp.concatenate([back_ref[b, :rows] for b in groups], axis=1).astype(F32)
    act_ref[...] = jnp.concatenate([back_ref[b, rows:] for b in groups], axis=1)
    at = pl.program_id(0) * out_ref.shape[1]
    total = dot(ga_ref[...], own_ref[...], ((1,), (0,))) + own
    out_ref[...] = add_returned(total, at, me_ref, send_ref, hub_ref, ret_refs)


WIDE = 512


def column(rows, first):
    return pl.BlockSpec((rows, WIDE), lambda i: (0, i + first))


def fixed(x):
    return pl.BlockSpec(x.shape, lambda i: (0, 0))


def finish_rest(me, ga, own, ret, sends, hubs, n_dst):
    rows, n, top = ga.shape[0], own.shape[1], n_dst // WIDE
    return pl.pallas_call(
        functools.partial(finish_rest_kernel, top),
        out_shape=shape(rows, n, kind=F32),
        grid=(n // WIDE - top,),
        in_specs=[SMEM, fixed(ga), column(n_dst, top), fixed(sends), fixed(hubs)]
        + [fixed(r) for r in ret],
        out_specs=column(rows, top),
        compiler_params=pltpu.CompilerParams(vmem_limit_bytes=56 * MIB),
        cost_estimate=pl.CostEstimate(flops=0, bytes_accessed=18000000, transcendentals=0),
        name="finish_rest",
    )(me, ga, own, sends, hubs, *ret)


def finish_dst(me, ga, own, ret, sends, hubs, back, grads):
    rows, n = grads.shape
    groups, _, piece = back.shape
    n_dst = groups * piece
    return pl.pallas_call(
        finish_dst_kernel,
        out_shape=[shape(rows, n, kind=F32), shape(rows, n_dst)],
        grid=(n_dst // WIDE,),
        in_specs=[
            SMEM,
            fixed(ga),
            column(n_dst, 0),
            fixed(sends),
            fixed(hubs),
            pl.BlockSpec((WIDE // piece, 2 * rows, piece), lambda i: (i, 0, 0)),
            pl.BlockSpec(memory_space=pl.ANY),
        ]
        + [fixed(r) for r in ret],
        out_specs=[column(rows, 0), column(rows, 0)],
        input_output_aliases={6: 0},
        compiler_params=pltpu.CompilerParams(vmem_limit_bytes=56 * MIB),
        cost_estimate=pl.CostEstimate(flops=0, bytes_accessed=6000000, transcendentals=0),
        name="finish_dst",
    )(me, ga, own, sends, hubs, back, grads, *ret)


def body(
    node_feats,
    send_rows,
    hub_rows,
    tile_dst,
    tile_src,
    tile_count,
    tile_vals,
    w_self,
    w_neigh,
    bias_vec,
    cotangent,
):
    n_dom = lax.axis_size("dom")
    n_feat = lax.axis_size("feat")
    ny, nz = n_dom // 2, n_feat // 2
    rows = node_feats.shape[0]
    own_rows = node_feats.shape[1]
    dst_rows = cotangent.shape[1]
    width = w_self.shape[1]
    n_own, n_dst = own_rows // T, dst_rows // T
    n_src = n_own + 2 * n_dom
    piece = dst_rows // n_feat
    sub = w_self.shape[0] // n_dom
    small = n_feat * sub
    me = lax.axis_index("dom")
    block = lax.axis_index("feat")
    me_s, block_s = me.reshape(1), block.reshape(1)

    def over_dom(x, k):
        return lax.ppermute(x, "dom", [(i, i ^ k) for i in range(n_dom)])

    def over_feat(x, k):
        return lax.ppermute(x, "feat", [(i, i ^ k) for i in range(n_feat)])

    def after(x, *events):
        return lax.optimization_barrier((x, events))[0]

    mine = jnp.stack(
        [
            lax.dynamic_slice_in_dim(w_self, me * sub, sub, axis=0),
            lax.dynamic_slice_in_dim(w_neigh, me * sub, sub, axis=0),
        ]
    )
    w, blocks = [mine[None]], [0]
    for bit in [1 << i for i in range(n_feat.bit_length() - 2, 0, -1)]:
        send = w[0] if len(w) == 1 else jnp.concatenate(w, axis=0)
        w.append(over_feat(send, bit))
        blocks += [k ^ bit for k in blocks]
    blocks += [k ^ 1 for k in blocks]

    sends, hubs = send_rows.reshape(n_dom, T), hub_rows[None, :]
    first, *outgoing = pack(
        me_s, node_feats, cotangent, bias_vec[None, :], sends, hubs, sub, n_feat
    )
    first = after(first, w[1])
    first = lax.all_to_all(first, "feat", 0, 0, tiled=True)
    incoming = [outgoing[0]] + [over_dom(outgoing[k], k) for k in range(1, n_dom)]

    halo_tile = n_own + 2 * ((tile_src - n_own) ^ me)
    hub_tile = n_own + 2 * ((tile_src - n_own - n_dom) ^ me) + 1
    place = jnp.where(
        tile_src < n_own, tile_src, jnp.where(tile_src < n_own + n_dom, halo_tile, hub_tile)
    )
    n_pos = n_dst * n_src
    slot = jnp.arange(tile_dst.shape[0], dtype=jnp.int32)
    key = jnp.where(slot < tile_count[0], tile_dst * n_src + place, n_pos)
    before = (key[None, :] < key[:, None]) | (
        (key[None, :] == key[:, None]) & (slot[None, :] < slot[:, None])
    )
    rank = jnp.sum(before.astype(jnp.int32), axis=1)
    order = jnp.sum(jnp.where(rank[:, None] == slot[None, :], slot[:, None], 0), axis=0)
    order = jnp.concatenate([order, jnp.zeros((2,), jnp.int32)])
    ends = jnp.arange(n_pos + 1, dtype=jnp.int32)
    start = jnp.sum((key[None, :] < ends[:, None]).astype(jnp.int32), axis=1)
    a_own, a_ext, agg = build_dense(
        tile_vals, order, start, node_feats, incoming, n_dst, n_src, n_own, n_feat
    )

    w[-1] = after(w[-1], agg)
    agg = after(agg, first)
    first = after(first, w[-1])
    w.append(over_feat(jnp.concatenate(w, axis=0), 1))
    agg = lax.all_to_all(agg, "feat", 0, 0, tiled=True).reshape(width, piece)

    bias, even, odd, *cross = whole_call(
        functools.partial(split_kernel, blocks, n_dom),
        "split",
        1.5,
        [
            shape(small, T, kind=F32),
            shape(small + width, piece),
            shape(small + width, piece),
        ]
        + [shape(2 * small + width, piece)] * (ny - 1),
        me_s,
        block_s,
        first,
        scalars=2,
    )
    cross = [over_dom(c, 2 * (j + 1)) for j, c in enumerate(cross)]
    evens = [even] + cross
    odds = [over_dom(odd, 1)] + [over_dom(c[small:], 1) for c in cross]
    agg_even = [agg] + [over_dom(agg, 2 * j) for j in range(1, ny)]
    agg_odd = [over_dom(a, 1) for a in agg_even]
    aggs = [a for pair in zip(agg_even, agg_odd) for a in pair]

    grad, act_even, act_odd, gagg_even, gagg_odd = whole_call(
        functools.partial(dense_kernel, ny, len(w)),
        "dense",
        3.0,
        [
            shape(n_dom, small, piece),
            shape(ny, small, piece),
            shape(ny, small, piece),
            shape(ny, width, piece),
            shape(ny, width, piece),
        ],
        bias,
        *w,
        *evens,
        *odds,
        *aggs,
    )

    got = over_dom(gagg_odd, 1)
    pair = whole_call(pair_kernel, "pair", 1.0, [shape(width, piece)] * ny, gagg_even, got)

    back_even, back_odd, parts, parts_odd = whole_call(
        functools.partial(grads_kernel, ny, len(w)),
        "grads",
        3.0,
        [
            shape(ny, width + small, piece),
            shape(ny, width + small, piece),
            shape(nz, sub, 2 * width + T),
            shape(nz, sub, 2 * width + T),
        ],
        grad,
        act_even,
        act_odd,
        *w,
        *evens,
        *odds,
        *aggs,
    )
    parts_odd, back_odd = after(parts_odd, pair), after(back_odd, pair)

    gagg = pair[0].astype(F32)
    for j in range(1, ny):
        gagg += over_dom(pair[j], 2 * j).astype(F32)
    gagg = gagg.astype(BF).reshape(n_feat, rows, piece)
    from_x = over_feat(parts_odd, 1)
    from_core = over_dom(back_odd, 1)
    from_x, from_core = after(from_x, gagg), after(from_core, gagg)

    gagg = lax.all_to_all(gagg, "feat", 0, 0, tiled=True)
    back = whole_call(
        functools.partial(back_pair_kernel, width),
        "back_pair",
        1.0,
        [shape(width + 2 * small, piece)] * ny,
        back_even,
        from_core,
    )
    back = [back[0]] + [over_dom(back[j], 2 * j) for j in range(1, ny)]
    parts = whole_call(pair_kernel, "x_sum", 1.0, [shape(sub, 2 * width + T)] * nz, parts, from_x)
    gagg = after(gagg, parts)
    parts = [parts[0]] + [over_feat(parts[j], blocks[j]) for j in range(1, nz)]

    gagg, *halo_grad = whole_call(
        halo_grad_kernel,
        "halo_grads",
        1.0,
        [shape(rows, dst_rows)] + [shape(rows, 2 * T)] * n_dom,
        gagg,
        a_ext,
    )
    returned = [halo_grad[0]] + [over_dom(halo_grad[k], k) for k in range(1, n_dom)]
    back = after(back, returned, parts)

    back = whole_call(
        functools.partial(back_pack_kernel, blocks),
        "back_pack",
        1.0,
        shape(n_feat, 2 * n_dom, sub, piece),
        me_s,
        block_s,
        *back,
        scalars=2,
    )
    back = lax.all_to_all(back, "feat", 0, 0, tiled=True).reshape(n_feat, 2 * rows, piece)
    total = whole_call(
        functools.partial(wsum_kernel, width), "w_sum", 1.0, shape(sub, 2 * width + T), *parts
    )
    whole = [total] + [over_dom(total, 2 * j) for j in range(1, ny)]
    grads = finish_rest(me_s, gagg, a_own, returned, sends, hubs, dst_rows)
    whole[1:] = [after(e, grads) for e in whole[1:]]
    whole = [t for e in whole for t in (e, over_dom(e, 1))]
    grad_self, grad_neigh, grad_bias = whole_call(
        wout_kernel,
        "w_out",
        1.0,
        [
            shape(n_dom, sub, width, kind=F32),
            shape(n_dom, sub, width, kind=F32),
            shape(n_dom, sub, T, kind=F32),
        ],
        me_s,
        *whole,
        scalars=1,
    )

    grad_feats, activations = finish_dst(
        me_s, gagg, a_own, returned, sends, hubs, back, grads
    )
    return (
        activations,
        grad_feats,
        grad_self.reshape(n_dom * sub, width),
        grad_neigh.reshape(n_dom * sub, width),
        grad_bias[:, :, 0].reshape(n_dom * sub),
    )


def solution(mesh):
    return jax.shard_map(
        body,
        mesh=mesh,
        in_specs=(
            P("feat", "dom"),
            P("dom"),
            P("dom"),
            P("dom"),
            P("dom"),
            P("dom"),
            P("dom", None, None),
            P("feat", None),
            P("feat", None),
            P("feat"),
            P("feat", "dom"),
        ),
        out_specs=(P("feat", "dom"), P("feat", "dom"), P("feat", None), P("feat", None), P("feat")),
        check_vma=False,
    )
```

```python
import functools

import jax
import jax.numpy as jnp
from jax import lax
from jax.experimental import pallas as pl
from jax.experimental.pallas import tpu as pltpu
from jax.sharding import PartitionSpec as P

T = 128
BF = jnp.bfloat16
F32 = jnp.float32
MIB = 1 << 20
VMEM = pl.BlockSpec(memory_space=pltpu.VMEM)
SMEM = pl.BlockSpec(memory_space=pltpu.SMEM)


def dot(left, right, dims):
    return lax.dot_general(left, right, (dims, ((), ())), preferred_element_type=F32)


def shape(*dims, kind=BF):
    return jax.ShapeDtypeStruct(dims, kind)


def whole_call(kernel, name, micros, out_shape, *args, scalars=0, mib=24):
    many = isinstance(out_shape, (list, tuple))
    return pl.pallas_call(
        kernel,
        out_shape=out_shape,
        in_specs=[SMEM] * scalars + [VMEM] * (len(args) - scalars),
        out_specs=[VMEM] * len(out_shape) if many else VMEM,
        compiler_params=pltpu.CompilerParams(vmem_limit_bytes=mib * MIB),
        cost_estimate=pl.CostEstimate(
            flops=0, bytes_accessed=int(micros * 3.0e6), transcendentals=0
        ),
        name=name,
    )(*args)


def pack_kernel(sub, me_ref, x_ref, cot_ref, bias_ref, send_ref, hub_ref, first_ref, *out_refs):
    groups, chunks, _, piece = first_ref.shape
    n = x_ref.shape[0] // sub
    bias = bias_ref[...]
    high = bias.astype(BF).astype(F32)
    row = lax.broadcasted_iota(jnp.int32, (sub, piece), 0)
    tail = jnp.where(row == 0, high, jnp.where(row == 1, bias - high, 0.0)).astype(BF)
    for b in range(groups):
        cols = slice(b * piece, (b + 1) * piece)
        first_ref[b, :n] = x_ref[:, cols].reshape(n, sub, piece)
        first_ref[b, n : 2 * n] = cot_ref[:, cols].reshape(n, sub, piece)
        first_ref[b, 2 * n] = tail
    x = x_ref[...]
    rows = lax.broadcasted_iota(jnp.int32, (x.shape[1], T), 0)
    readers = len(out_refs)
    for q in range(readers + 1):
        idx = send_ref[pl.ds(me_ref[0] ^ q, 1), :] if q < readers else hub_ref[...]
        hot = (rows == idx).astype(F32).astype(BF)
        got = dot(x, hot, ((1,), (0,))).astype(BF)
        if q < readers:
            out_refs[q][:, :T] = got
        else:
            for r in range(readers):
                out_refs[r][:, T:] = got


def pack(me, x, cot, bias, sends, hubs, sub, n_feat):
    n_dom = sends.shape[0]
    rows = x.shape[0]
    args = (x, cot, bias, sends, hubs)
    outs = [shape(n_feat, 2 * n_dom + 1, sub, cot.shape[1] // n_feat)]
    outs += [shape(rows, 2 * T)] * n_dom
    return pl.pallas_call(
        functools.partial(pack_kernel, sub),
        out_shape=outs,
        grid=(1,),
        in_specs=[SMEM] + [pl.BlockSpec(a.shape, lambda i, n=a.ndim: (0,) * n) for a in args],
        out_specs=[pl.BlockSpec(o.shape, lambda i, n=len(o.shape): (0,) * n) for o in outs],
        compiler_params=pltpu.CompilerParams(vmem_limit_bytes=60 * MIB),
        cost_estimate=pl.CostEstimate(flops=0, bytes_accessed=12000000, transcendentals=0),
        name="pack",
    )(me, *args)


def build_kernel(n_own, order_ref, start_ref, x_ref, vals_hbm, *refs):
    *halo_refs, own_ref, ext_ref, agg_ref, vals, sems = refs
    step = pl.program_id(0)
    slots = vals_hbm.shape[0]
    n_src = n_own + ext_ref.shape[1] // T
    chunks = sems.shape[0]
    per = slots // chunks

    def piece(i):
        span = pl.ds(i * per, per)
        return pltpu.make_async_copy(vals_hbm.at[span], vals.at[span], sems.at[i])

    @pl.when(step == 0)
    def _():
        for i in range(chunks):
            piece(i).start()
        vals[slots] = jnp.zeros((T, T), BF)
        for i in range(chunks):
            piece(i).wait()

    for v in range(own_ref.shape[0] // T):
        rows = slice(v * T, (v + 1) * T)
        for s in range(n_src):
            p = (step * (own_ref.shape[0] // T) + v) * n_src + s
            first, last = start_ref[p], start_ref[p + 1]
            one = jnp.where(last > first, order_ref[first], slots)
            two = jnp.where(last > first + 1, order_ref[first + 1], slots)
            total = vals[one].astype(F32) + vals[two].astype(F32)

            def more(i, total):
                return total + vals[order_ref[i]].astype(F32)

            total = lax.fori_loop(first + 2, last, more, total).astype(BF)
            if s < n_own:
                own_ref[rows, s * T : (s + 1) * T] = total
            else:
                ext_ref[rows, (s - n_own) * T : (s - n_own + 1) * T] = total
    halo = jnp.concatenate([r[...] for r in halo_refs], axis=1)
    total = dot(x_ref[...], own_ref[...], ((1,), (1,)))
    total = (total + dot(halo, ext_ref[...], ((1,), (1,)))).astype(BF)
    piece_n = agg_ref.shape[2]
    for b in range(agg_ref.shape[0]):
        agg_ref[b] = total[:, b * piece_n : (b + 1) * piece_n]


def build_dense(vals, order, start, x, halos, n_dst, n_src, n_own, n_feat):
    rows = x.shape[0]
    piece = n_dst * T // n_feat
    ext = (n_src - n_own) * T
    return pl.pallas_call(
        functools.partial(build_kernel, n_own),
        out_shape=(
            shape(n_dst * T, n_own * T),
            shape(n_dst * T, ext),
            shape(n_feat, rows, piece),
        ),
        grid_spec=pltpu.PrefetchScalarGridSpec(
            num_scalar_prefetch=2,
            grid=(n_dst // 2,),
            in_specs=[VMEM, pl.BlockSpec(memory_space=pl.ANY)] + [VMEM] * len(halos),
            out_specs=[
                pl.BlockSpec((2 * T, n_own * T), lambda u, *_: (u, 0)),
                pl.BlockSpec((2 * T, ext), lambda u, *_: (u, 0)),
                pl.BlockSpec((2 * T // piece, rows, piece), lambda u, *_: (u, 0, 0)),
            ],
            scratch_shapes=[
                pltpu.VMEM((vals.shape[0] + 1, T, T), BF),
                pltpu.SemaphoreType.DMA((8,)),
            ],
        ),
        compiler_params=pltpu.CompilerParams(vmem_limit_bytes=58 * MIB),
        cost_estimate=pl.CostEstimate(flops=0, bytes_accessed=30000000, transcendentals=0),
        name="build_dense",
    )(order, start, x, vals, *halos)


def split_kernel(blocks, n_dom, me_ref, block_ref, first_ref, bias_ref, *out_refs):
    _, _, sub, piece = first_ref.shape
    n = (first_ref.shape[1] - 1) // 2
    small = len(blocks) * sub
    width = len(blocks) * n * sub
    x = first_ref[:, :n].reshape(width, piece)
    row = lax.broadcasted_iota(jnp.int32, (sub, piece), 0) + me_ref[0] * sub
    lane = lax.broadcasted_iota(jnp.int32, (sub, piece), 1)
    for i, k in enumerate(blocks):
        b = block_ref[0] ^ k
        both = first_ref[b, 2 * n, 0:1].astype(F32) + first_ref[b, 2 * n, 1:2].astype(F32)
        mine = jnp.sum(jnp.where(row == lane, both, 0.0), axis=1, keepdims=True)
        bias_ref[i * sub : (i + 1) * sub, :] = jnp.broadcast_to(mine, (sub, T))
    even, odd = out_refs[0], out_refs[1]
    even[small:] = x
    odd[:width] = x
    for i, k in enumerate(blocks):
        b = block_ref[0] ^ k
        even[i * sub : (i + 1) * sub] = first_ref[b, n + me_ref[0]]
        odd[width + i * sub : width + (i + 1) * sub] = first_ref[b, n + (me_ref[0] ^ 1)]
    for j in range(1, n_dom // 2):
        ref = out_refs[1 + j]
        ref[small : small + width] = x
        for i, k in enumerate(blocks):
            b = block_ref[0] ^ k
            at = small + width + i * sub
            ref[i * sub : (i + 1) * sub] = first_ref[b, n + (me_ref[0] ^ (2 * j))]
            ref[at : at + sub] = first_ref[b, n + (me_ref[0] ^ (2 * j + 1))]


def weights(refs):
    return [jnp.concatenate([r[g, m] for r in refs for g in range(r.shape[0])]) for m in (0, 1)]


def dense_kernel(ny, nw, bias_ref, *refs):
    w_refs, refs = refs[:nw], refs[nw:]
    even, odd, agg = refs[:ny], refs[ny : 2 * ny], refs[2 * ny : 4 * ny]
    g_ref, act_even, act_odd, gagg_even, gagg_odd = refs[4 * ny :]
    w_self, w_neigh = weights(w_refs)
    small, width = w_self.shape
    bias = bias_ref[:, :1]
    for k in range(2 * ny):
        j = k // 2
        if k % 2 == 0:
            cot, x = even[j][:small, :], even[j][small : small + width, :]
            act_ref, gagg_ref = act_even, gagg_even
        else:
            x, cot = odd[j][:width, :], odd[j][width:, :]
            act_ref, gagg_ref = act_odd, gagg_odd
        pre = dot(w_self, x, ((1,), (0,)))
        pre += dot(w_neigh, agg[k][...], ((1,), (0,)))
        pre += bias
        sig = 1.0 / (1.0 + jnp.exp(-pre))
        act_ref[j] = (pre * sig).astype(BF)
        grad = (cot.astype(F32) * sig * (1.0 + pre * (1.0 - sig))).astype(BF)
        g_ref[k] = grad
        gagg_ref[j] = dot(w_neigh, grad, ((0,), (0,))).astype(BF)


def grads_kernel(ny, nw, g_ref, act_even, act_odd, *refs):
    w_refs, refs = refs[:nw], refs[nw:]
    even, odd, agg = refs[:ny], refs[ny : 2 * ny], refs[2 * ny : 4 * ny]
    back_even, back_odd, *out_refs = refs[4 * ny :]
    w_self, _ = weights(w_refs)
    small, width = w_self.shape
    sub = out_refs[0].shape[1]
    xs = []
    for k in range(2 * ny):
        j = k // 2
        act_ref, back_ref = (act_odd, back_odd) if k % 2 else (act_even, back_even)
        back_ref[j, :width] = dot(w_self, g_ref[k], ((0,), (0,))).astype(BF)
        back_ref[j, width:] = act_ref[j]
        xs.append(odd[j][:width, :] if k % 2 else even[j][small : small + width, :])
    grad = jnp.concatenate([g_ref[k] for k in range(2 * ny)], axis=1)
    own = dot(grad, jnp.concatenate(xs, axis=1), ((1,), (1,))).astype(BF)
    neigh = dot(grad, jnp.concatenate([r[...] for r in agg], axis=1), ((1,), (1,))).astype(BF)
    total = jnp.sum(grad.astype(F32), axis=1, keepdims=True)
    high = total.astype(BF).astype(F32)
    lane = lax.broadcasted_iota(jnp.int32, (small, T), 1)
    both = jnp.where(lane == 0, high, jnp.where(lane == 1, total - high, 0.0)).astype(BF)
    nz = out_refs[0].shape[0]
    for i in range(small // sub):
        rows, out_ref = slice(i * sub, (i + 1) * sub), out_refs[i // nz]
        out_ref[i % nz, :, :width] = own[rows]
        out_ref[i % nz, :, width : 2 * width] = neigh[rows]
        out_ref[i % nz, :, 2 * width :] = both[rows]


def pair_kernel(even_ref, got_ref, *out_refs):
    for j, out_ref in enumerate(out_refs):
        out_ref[...] = (even_ref[j].astype(F32) + got_ref[j].astype(F32)).astype(BF)


def back_pair_kernel(width, even_ref, got_ref, *out_refs):
    for j, out_ref in enumerate(out_refs):
        both = even_ref[j, :width].astype(F32) + got_ref[j, :width].astype(F32)
        small = even_ref.shape[1] - width
        out_ref[:width] = both.astype(BF)
        out_ref[width : width + small] = even_ref[j, width:]
        out_ref[width + small :] = got_ref[j, width:]


def back_pack_kernel(blocks, me_ref, block_ref, *refs):
    *in_refs, out_ref = refs
    groups, chunks, sub, piece = out_ref.shape
    n = chunks // 2
    width = groups * n * sub
    small = groups * sub
    total = in_refs[0][:width].astype(F32)
    for r in in_refs[1:]:
        total += r[:width].astype(F32)
    out_ref[:, :n] = total.astype(BF).reshape(groups, n, sub, piece)
    for k in range(2 * len(in_refs)):
        d = me_ref[0] ^ k
        for i, f in enumerate(blocks):
            at = width + (k % 2) * small + i * sub
            out_ref[block_ref[0] ^ f, n + d] = in_refs[k // 2][at : at + sub]


def wsum_kernel(width, *refs):
    *in_refs, out_ref = refs
    total = in_refs[0][...].astype(F32)
    for r in in_refs[1:]:
        total += r[...].astype(F32)
    out_ref[:, : 2 * width] = total[:, : 2 * width].astype(BF)
    bias = jnp.sum(total[:, 2 * width :], axis=1, keepdims=True)
    high = bias.astype(BF).astype(F32)
    lane = lax.broadcasted_iota(jnp.int32, (total.shape[0], T), 1)
    both = jnp.where(lane == 0, high, jnp.where(lane == 1, bias - high, 0.0))
    out_ref[:, 2 * width :] = both.astype(BF)


def wout_kernel(me_ref, *refs):
    *in_refs, self_ref, neigh_ref, bias_ref = refs
    width = self_ref.shape[2]
    for k, ref in enumerate(in_refs):
        d = me_ref[0] ^ k
        self_ref[d] = ref[:, :width].astype(F32)
        neigh_ref[d] = ref[:, width : 2 * width].astype(F32)
        total = jnp.sum(ref[:, 2 * width :].astype(F32), axis=1, keepdims=True)
        bias_ref[d] = jnp.broadcast_to(total, bias_ref.shape[1:])


def halo_grad_kernel(ga_ref, ext_ref, flat_ref, *out_refs):
    ga = jnp.concatenate([ga_ref[b] for b in range(ga_ref.shape[0])], axis=1)
    flat_ref[...] = ga
    for k, out_ref in enumerate(out_refs):
        span = slice(k * 2 * T, (k + 1) * 2 * T)
        out_ref[...] = dot(ga, ext_ref[:, span], ((1,), (0,))).astype(BF)


def add_returned(total, at, me_ref, send_ref, hub_ref, ret_refs):
    rows = lax.broadcasted_iota(jnp.int32, (total.shape[1], T), 0) + at
    hub = (rows == hub_ref[...]).astype(F32).astype(BF)
    hots, cols, hubs = [], [], 0.0
    for q, ret_ref in enumerate(ret_refs):
        idx = send_ref[pl.ds(me_ref[0] ^ q, 1), :]
        hots.append((rows == idx).astype(F32).astype(BF))
        cols.append(ret_ref[:, :T])
        hubs += ret_ref[:, T:].astype(F32)
    high = hubs.astype(BF)
    cols += [high, (hubs - high.astype(F32)).astype(BF)]
    hots += [hub, hub]
    return total + dot(jnp.concatenate(cols, axis=1), jnp.concatenate(hots, axis=1), ((1,), (1,)))


SPLIT = 4


def times_owned(ga_ref, own_refs):
    depth = own_refs[0].shape[0]
    total = 0.0
    for r, ref in enumerate(own_refs):
        total += dot(ga_ref[:, r * depth : (r + 1) * depth], ref[...], ((1,), (0,)))
    return total


def finish_rest_kernel(top, me_ref, ga_ref, send_ref, hub_ref, *refs):
    own_refs, ret_refs, out_ref = refs[:SPLIT], refs[SPLIT:-1], refs[-1]
    at = (pl.program_id(0) + top) * out_ref.shape[1]
    total = times_owned(ga_ref, own_refs)
    out_ref[...] = add_returned(total, at, me_ref, send_ref, hub_ref, ret_refs)


def finish_dst_kernel(me_ref, ga_ref, send_ref, hub_ref, back_ref, grads_ref, *refs):
    own_refs, ret_refs, out_ref, act_ref = refs[:SPLIT], refs[SPLIT:-2], refs[-2], refs[-1]
    rows = ga_ref.shape[0]
    groups = range(back_ref.shape[0])
    own = jnp.concatenate([back_ref[b, :rows] for b in groups], axis=1).astype(F32)
    act_ref[...] = jnp.concatenate([back_ref[b, rows:] for b in groups], axis=1)
    at = pl.program_id(0) * out_ref.shape[1]
    total = times_owned(ga_ref, own_refs) + own
    out_ref[...] = add_returned(total, at, me_ref, send_ref, hub_ref, ret_refs)


WIDE = 512


def column(rows, first, at=0):
    return pl.BlockSpec((rows, WIDE), lambda i: (at, i + first))


def row_blocks(n_dst, first):
    return [column(n_dst // SPLIT, first, r) for r in range(SPLIT)]


def fixed(x):
    return pl.BlockSpec(x.shape, lambda i: (0, 0))


def finish_rest(me, ga, own, ret, sends, hubs, n_dst):
    rows, n, top = ga.shape[0], own.shape[1], n_dst // WIDE
    return pl.pallas_call(
        functools.partial(finish_rest_kernel, top),
        out_shape=shape(rows, n, kind=F32),
        grid=(n // WIDE - top,),
        in_specs=[SMEM, fixed(ga), fixed(sends), fixed(hubs)]
        + row_blocks(n_dst, top)
        + [fixed(r) for r in ret],
        out_specs=column(rows, top),
        compiler_params=pltpu.CompilerParams(vmem_limit_bytes=56 * MIB),
        cost_estimate=pl.CostEstimate(flops=0, bytes_accessed=18000000, transcendentals=0),
        name="finish_rest",
    )(me, ga, sends, hubs, *[own] * SPLIT, *ret)


def finish_dst(me, ga, own, ret, sends, hubs, back, grads):
    rows, n = grads.shape
    groups, _, piece = back.shape
    n_dst = groups * piece
    return pl.pallas_call(
        finish_dst_kernel,
        out_shape=[shape(rows, n, kind=F32), shape(rows, n_dst)],
        grid=(n_dst // WIDE,),
        in_specs=[
            SMEM,
            fixed(ga),
            fixed(sends),
            fixed(hubs),
            pl.BlockSpec((WIDE // piece, 2 * rows, piece), lambda i: (i, 0, 0)),
            pl.BlockSpec(memory_space=pl.ANY),
        ]
        + row_blocks(n_dst, 0)
        + [fixed(r) for r in ret],
        out_specs=[column(rows, 0), column(rows, 0)],
        input_output_aliases={5: 0},
        compiler_params=pltpu.CompilerParams(vmem_limit_bytes=56 * MIB),
        cost_estimate=pl.CostEstimate(flops=0, bytes_accessed=6000000, transcendentals=0),
        name="finish_dst",
    )(me, ga, sends, hubs, back, grads, *[own] * SPLIT, *ret)


def body(
    node_feats,
    send_rows,
    hub_rows,
    tile_dst,
    tile_src,
    tile_count,
    tile_vals,
    w_self,
    w_neigh,
    bias_vec,
    cotangent,
):
    n_dom = lax.axis_size("dom")
    n_feat = lax.axis_size("feat")
    ny, nz = n_dom // 2, n_feat // 2
    rows = node_feats.shape[0]
    own_rows = node_feats.shape[1]
    dst_rows = cotangent.shape[1]
    width = w_self.shape[1]
    n_own, n_dst = own_rows // T, dst_rows // T
    n_src = n_own + 2 * n_dom
    piece = dst_rows // n_feat
    sub = w_self.shape[0] // n_dom
    small = n_feat * sub
    me = lax.axis_index("dom")
    block = lax.axis_index("feat")
    me_s, block_s = me.reshape(1), block.reshape(1)

    def over_dom(x, k):
        return lax.ppermute(x, "dom", [(i, i ^ k) for i in range(n_dom)])

    def over_feat(x, k):
        return lax.ppermute(x, "feat", [(i, i ^ k) for i in range(n_feat)])

    def after(x, *events):
        return lax.optimization_barrier((x, events))[0]

    mine = jnp.stack(
        [
            lax.dynamic_slice_in_dim(w_self, me * sub, sub, axis=0),
            lax.dynamic_slice_in_dim(w_neigh, me * sub, sub, axis=0),
        ]
    )
    w, blocks = [mine[None]], [0]
    for bit in [1 << i for i in range(n_feat.bit_length() - 2, 0, -1)]:
        send = w[0] if len(w) == 1 else jnp.concatenate(w, axis=0)
        w.append(over_feat(send, bit))
        blocks += [k ^ bit for k in blocks]
    blocks += [k ^ 1 for k in blocks]

    sends, hubs = send_rows.reshape(n_dom, T), hub_rows[None, :]
    first, *outgoing = pack(
        me_s, node_feats, cotangent, bias_vec[None, :], sends, hubs, sub, n_feat
    )
    first = after(first, w[1])
    first = lax.all_to_all(first, "feat", 0, 0, tiled=True)
    incoming = [outgoing[0]] + [over_dom(outgoing[k], k) for k in range(1, n_dom)]

    halo_tile = n_own + 2 * ((tile_src - n_own) ^ me)
    hub_tile = n_own + 2 * ((tile_src - n_own - n_dom) ^ me) + 1
    place = jnp.where(
        tile_src < n_own, tile_src, jnp.where(tile_src < n_own + n_dom, halo_tile, hub_tile)
    )
    n_pos = n_dst * n_src
    slot = jnp.arange(tile_dst.shape[0], dtype=jnp.int32)
    key = jnp.where(slot < tile_count[0], tile_dst * n_src + place, n_pos)
    before = (key[None, :] < key[:, None]) | (
        (key[None, :] == key[:, None]) & (slot[None, :] < slot[:, None])
    )
    rank = jnp.sum(before.astype(jnp.int32), axis=1)
    order = jnp.sum(jnp.where(rank[:, None] == slot[None, :], slot[:, None], 0), axis=0)
    order = jnp.concatenate([order, jnp.zeros((2,), jnp.int32)])
    ends = jnp.arange(n_pos + 1, dtype=jnp.int32)
    start = jnp.sum((key[None, :] < ends[:, None]).astype(jnp.int32), axis=1)
    a_own, a_ext, agg = build_dense(
        tile_vals, order, start, node_feats, incoming, n_dst, n_src, n_own, n_feat
    )

    w[-1] = after(w[-1], agg)
    agg = after(agg, first)
    first = after(first, w[-1])
    w.append(over_feat(jnp.concatenate(w, axis=0), 1))
    agg = lax.all_to_all(agg, "feat", 0, 0, tiled=True).reshape(width, piece)

    bias, even, odd, *cross = whole_call(
        functools.partial(split_kernel, blocks, n_dom),
        "split",
        1.5,
        [
            shape(small, T, kind=F32),
            shape(small + width, piece),
            shape(small + width, piece),
        ]
        + [shape(2 * small + width, piece)] * (ny - 1),
        me_s,
        block_s,
        first,
        scalars=2,
    )
    cross = [over_dom(c, 2 * (j + 1)) for j, c in enumerate(cross)]
    evens = [even] + cross
    odds = [over_dom(odd, 1)] + [over_dom(c[small:], 1) for c in cross]
    agg_even = [agg] + [over_dom(agg, 2 * j) for j in range(1, ny)]
    agg_odd = [over_dom(a, 1) for a in agg_even]
    aggs = [a for pair in zip(agg_even, agg_odd) for a in pair]

    grad, act_even, act_odd, gagg_even, gagg_odd = whole_call(
        functools.partial(dense_kernel, ny, len(w)),
        "dense",
        3.0,
        [
            shape(n_dom, small, piece),
            shape(ny, small, piece),
            shape(ny, small, piece),
            shape(ny, width, piece),
            shape(ny, width, piece),
        ],
        bias,
        *w,
        *evens,
        *odds,
        *aggs,
    )

    got = over_dom(gagg_odd, 1)
    pair = whole_call(pair_kernel, "pair", 1.0, [shape(width, piece)] * ny, gagg_even, got)

    back_even, back_odd, parts, parts_odd = whole_call(
        functools.partial(grads_kernel, ny, len(w)),
        "grads",
        3.0,
        [
            shape(ny, width + small, piece),
            shape(ny, width + small, piece),
            shape(nz, sub, 2 * width + T),
            shape(nz, sub, 2 * width + T),
        ],
        grad,
        act_even,
        act_odd,
        *w,
        *evens,
        *odds,
        *aggs,
    )
    parts_odd, back_odd = after(parts_odd, pair), after(back_odd, pair)

    gagg = pair[0].astype(F32)
    for j in range(1, ny):
        gagg += over_dom(pair[j], 2 * j).astype(F32)
    gagg = gagg.astype(BF).reshape(n_feat, rows, piece)
    from_x = over_feat(parts_odd, 1)
    from_core = over_dom(back_odd, 1)
    from_x, from_core = after(from_x, gagg), after(from_core, gagg)

    gagg = lax.all_to_all(gagg, "feat", 0, 0, tiled=True)
    parts = whole_call(pair_kernel, "x_sum", 1.0, [shape(sub, 2 * width + T)] * nz, parts, from_x)
    from_core = after(from_core, parts)
    back = whole_call(
        functools.partial(back_pair_kernel, width),
        "back_pair",
        1.0,
        [shape(width + 2 * small, piece)] * ny,
        back_even,
        from_core,
    )
    back = [back[0]] + [over_dom(back[j], 2 * j) for j in range(1, ny)]
    gagg = after(gagg, parts)
    parts = [parts[0]] + [over_feat(parts[j], blocks[j]) for j in range(1, nz)]

    gagg, *halo_grad = whole_call(
        halo_grad_kernel,
        "halo_grads",
        1.0,
        [shape(rows, dst_rows)] + [shape(rows, 2 * T)] * n_dom,
        gagg,
        a_ext,
    )
    returned = [halo_grad[0]] + [over_dom(halo_grad[k], k) for k in range(1, n_dom)]
    back = after(back, returned, parts)

    back = whole_call(
        functools.partial(back_pack_kernel, blocks),
        "back_pack",
        1.0,
        shape(n_feat, 2 * n_dom, sub, piece),
        me_s,
        block_s,
        *back,
        scalars=2,
    )
    back = lax.all_to_all(back, "feat", 0, 0, tiled=True).reshape(n_feat, 2 * rows, piece)
    total = whole_call(
        functools.partial(wsum_kernel, width), "w_sum", 1.0, shape(sub, 2 * width + T), *parts
    )
    whole = [total] + [over_dom(total, 2 * j) for j in range(1, ny)]
    grads = finish_rest(me_s, gagg, a_own, returned, sends, hubs, dst_rows)
    whole[1:] = [after(e, grads) for e in whole[1:]]
    whole = [t for e in whole for t in (e, over_dom(e, 1))]
    grad_self, grad_neigh, grad_bias = whole_call(
        wout_kernel,
        "w_out",
        1.0,
        [
            shape(n_dom, sub, width, kind=F32),
            shape(n_dom, sub, width, kind=F32),
            shape(n_dom, sub, T, kind=F32),
        ],
        me_s,
        *whole,
        scalars=1,
    )

    grad_feats, activations = finish_dst(
        me_s, gagg, a_own, returned, sends, hubs, back, grads
    )
    return (
        activations,
        grad_feats,
        grad_self.reshape(n_dom * sub, width),
        grad_neigh.reshape(n_dom * sub, width),
        grad_bias[:, :, 0].reshape(n_dom * sub),
    )


def solution(mesh):
    return jax.shard_map(
        body,
        mesh=mesh,
        in_specs=(
            P("feat", "dom"),
            P("dom"),
            P("dom"),
            P("dom"),
            P("dom"),
            P("dom"),
            P("dom", None, None),
            P("feat", None),
            P("feat", None),
            P("feat"),
            P("feat", "dom"),
        ),
        out_specs=(P("feat", "dom"), P("feat", "dom"), P("feat", None), P("feat", None), P("feat")),
        check_vma=False,
    )
```

```python
import functools

import jax
import jax.numpy as jnp
from jax import lax
from jax.experimental import pallas as pl
from jax.experimental.pallas import tpu as pltpu
from jax.sharding import PartitionSpec as P

T = 128
BF = jnp.bfloat16
F32 = jnp.float32
MIB = 1 << 20
WIDE = 512
VMEM = pl.BlockSpec(memory_space=pltpu.VMEM)
SMEM = pl.BlockSpec(memory_space=pltpu.SMEM)


def dot(left, right, dims):
    return lax.dot_general(left, right, (dims, ((), ())), preferred_element_type=F32)


def shape(*dims, kind=BF):
    return jax.ShapeDtypeStruct(dims, kind)


def whole_call(kernel, name, micros, out_shape, *args, scalars=0, mib=24):
    many = isinstance(out_shape, (list, tuple))
    return pl.pallas_call(
        kernel,
        out_shape=out_shape,
        in_specs=[SMEM] * scalars + [VMEM] * (len(args) - scalars),
        out_specs=[VMEM] * len(out_shape) if many else VMEM,
        compiler_params=pltpu.CompilerParams(vmem_limit_bytes=mib * MIB),
        cost_estimate=pl.CostEstimate(
            flops=0, bytes_accessed=int(micros * 3.0e6), transcendentals=0
        ),
        name=name,
    )(*args)


def pack_kernel(sub, me_ref, x_ref, cot_ref, bias_ref, send_ref, hub_ref, first_ref, *out_refs):
    groups, chunks, _, piece = first_ref.shape
    n = x_ref.shape[0] // sub
    bias = bias_ref[...]
    high = bias.astype(BF).astype(F32)
    row = lax.broadcasted_iota(jnp.int32, (sub, piece), 0)
    tail = jnp.where(row == 0, high, jnp.where(row == 1, bias - high, 0.0)).astype(BF)
    for b in range(groups):
        cols = slice(b * piece, (b + 1) * piece)
        first_ref[b, :n] = x_ref[:, cols].reshape(n, sub, piece)
        first_ref[b, n : 2 * n] = cot_ref[:, cols].reshape(n, sub, piece)
        first_ref[b, 2 * n] = tail
    x = x_ref[...]
    rows = lax.broadcasted_iota(jnp.int32, (x.shape[1], T), 0)
    readers = len(out_refs)
    for q in range(readers + 1):
        idx = send_ref[pl.ds(me_ref[0] ^ q, 1), :] if q < readers else hub_ref[...]
        hot = (rows == idx).astype(F32).astype(BF)
        got = dot(x, hot, ((1,), (0,))).astype(BF)
        if q < readers:
            out_refs[q][:, :T] = got
        else:
            for r in range(readers):
                out_refs[r][:, T:] = got


def pack(me, x, cot, bias, sends, hubs, sub, n_feat):
    n_dom = sends.shape[0]
    rows = x.shape[0]
    args = (x, cot, bias, sends, hubs)
    outs = [shape(n_feat, 2 * n_dom + 1, sub, cot.shape[1] // n_feat)]
    outs += [shape(rows, 2 * T)] * n_dom
    return pl.pallas_call(
        functools.partial(pack_kernel, sub),
        out_shape=outs,
        grid=(1,),
        in_specs=[SMEM] + [pl.BlockSpec(a.shape, lambda i, n=a.ndim: (0,) * n) for a in args],
        out_specs=[pl.BlockSpec(o.shape, lambda i, n=len(o.shape): (0,) * n) for o in outs],
        compiler_params=pltpu.CompilerParams(vmem_limit_bytes=60 * MIB),
        cost_estimate=pl.CostEstimate(flops=0, bytes_accessed=12000000, transcendentals=0),
        name="pack",
    )(me, *args)


def build_kernel(n_own, order_ref, start_ref, x_ref, vals_hbm, *refs):
    *halo_refs, own_ref, ext_ref, agg_ref, vals, sems = refs
    step = pl.program_id(0)
    slots = vals_hbm.shape[0]
    n_src = n_own + ext_ref.shape[1] // T
    tiles, wide = own_ref.shape[1] // T, own_ref.shape[2]
    chunks = sems.shape[0]
    per = slots // chunks

    def piece(i):
        span = pl.ds(i * per, per)
        return pltpu.make_async_copy(vals_hbm.at[span], vals.at[span], sems.at[i])

    @pl.when(step == 0)
    def _():
        for i in range(chunks):
            piece(i).start()
        vals[slots] = jnp.zeros((T, T), BF)
        for i in range(chunks):
            piece(i).wait()

    for v in range(tiles):
        rows = slice(v * T, (v + 1) * T)
        for s in range(n_src):
            p = (step * tiles + v) * n_src + s
            first, last = start_ref[p], start_ref[p + 1]
            one = jnp.where(last > first, order_ref[first], slots)
            two = jnp.where(last > first + 1, order_ref[first + 1], slots)
            total = vals[one].astype(F32) + vals[two].astype(F32)

            def more(i, total):
                return total + vals[order_ref[i]].astype(F32)

            total = lax.fori_loop(first + 2, last, more, total).astype(BF)
            if s < n_own:
                at = s * T % wide
                own_ref[s * T // wide, rows, at : at + T] = total
            else:
                ext_ref[rows, (s - n_own) * T : (s - n_own + 1) * T] = total
    halo = jnp.concatenate([r[...] for r in halo_refs], axis=1)
    total = 0.0
    for b in range(own_ref.shape[0]):
        total += dot(x_ref[:, b * wide : (b + 1) * wide], own_ref[b], ((1,), (1,)))
    total = (total + dot(halo, ext_ref[...], ((1,), (1,)))).astype(BF)
    piece_n = agg_ref.shape[2]
    for b in range(agg_ref.shape[0]):
        agg_ref[b] = total[:, b * piece_n : (b + 1) * piece_n]


def build_dense(vals, order, start, x, halos, n_dst, n_src, n_own, n_feat):
    rows = x.shape[0]
    piece = n_dst * T // n_feat
    ext = (n_src - n_own) * T
    return pl.pallas_call(
        functools.partial(build_kernel, n_own),
        out_shape=(
            shape(n_own * T // WIDE, n_dst * T, WIDE),
            shape(n_dst * T, ext),
            shape(n_feat, rows, piece),
        ),
        grid_spec=pltpu.PrefetchScalarGridSpec(
            num_scalar_prefetch=2,
            grid=(n_dst // 2,),
            in_specs=[VMEM, pl.BlockSpec(memory_space=pl.ANY)] + [VMEM] * len(halos),
            out_specs=[
                pl.BlockSpec((n_own * T // WIDE, 2 * T, WIDE), lambda u, *_: (0, u, 0)),
                pl.BlockSpec((2 * T, ext), lambda u, *_: (u, 0)),
                pl.BlockSpec((2 * T // piece, rows, piece), lambda u, *_: (u, 0, 0)),
            ],
            scratch_shapes=[
                pltpu.VMEM((vals.shape[0] + 1, T, T), BF),
                pltpu.SemaphoreType.DMA((8,)),
            ],
        ),
        compiler_params=pltpu.CompilerParams(vmem_limit_bytes=58 * MIB),
        cost_estimate=pl.CostEstimate(flops=0, bytes_accessed=30000000, transcendentals=0),
        name="build_dense",
    )(order, start, x, vals, *halos)


def split_kernel(blocks, n_dom, me_ref, block_ref, first_ref, bias_ref, *out_refs):
    _, _, sub, piece = first_ref.shape
    n = (first_ref.shape[1] - 1) // 2
    small = len(blocks) * sub
    width = len(blocks) * n * sub
    x = first_ref[:, :n].reshape(width, piece)
    row = lax.broadcasted_iota(jnp.int32, (sub, piece), 0) + me_ref[0] * sub
    lane = lax.broadcasted_iota(jnp.int32, (sub, piece), 1)
    for i, k in enumerate(blocks):
        b = block_ref[0] ^ k
        both = first_ref[b, 2 * n, 0:1].astype(F32) + first_ref[b, 2 * n, 1:2].astype(F32)
        mine = jnp.sum(jnp.where(row == lane, both, 0.0), axis=1, keepdims=True)
        bias_ref[i * sub : (i + 1) * sub, :] = jnp.broadcast_to(mine, (sub, T))
    even, odd = out_refs[0], out_refs[1]
    even[small:] = x
    odd[:width] = x
    for i, k in enumerate(blocks):
        b = block_ref[0] ^ k
        even[i * sub : (i + 1) * sub] = first_ref[b, n + me_ref[0]]
        odd[width + i * sub : width + (i + 1) * sub] = first_ref[b, n + (me_ref[0] ^ 1)]
    for j in range(1, n_dom // 2):
        ref = out_refs[1 + j]
        ref[small : small + width] = x
        for i, k in enumerate(blocks):
            b = block_ref[0] ^ k
            at = small + width + i * sub
            ref[i * sub : (i + 1) * sub] = first_ref[b, n + (me_ref[0] ^ (2 * j))]
            ref[at : at + sub] = first_ref[b, n + (me_ref[0] ^ (2 * j + 1))]


def weights(refs):
    return [jnp.concatenate([r[g, m] for r in refs for g in range(r.shape[0])]) for m in (0, 1)]


def dense_kernel(ny, nw, bias_ref, *refs):
    w_refs, refs = refs[:nw], refs[nw:]
    even, odd, agg = refs[:ny], refs[ny : 2 * ny], refs[2 * ny : 4 * ny]
    g_ref, act_even, act_odd, gagg_even, gagg_odd = refs[4 * ny :]
    w_self, w_neigh = weights(w_refs)
    small, width = w_self.shape
    bias = bias_ref[:, :1]
    for k in range(2 * ny):
        j = k // 2
        if k % 2 == 0:
            cot, x = even[j][:small, :], even[j][small : small + width, :]
            act_ref, gagg_ref = act_even, gagg_even
        else:
            x, cot = odd[j][:width, :], odd[j][width:, :]
            act_ref, gagg_ref = act_odd, gagg_odd
        pre = dot(w_self, x, ((1,), (0,)))
        pre += dot(w_neigh, agg[k][...], ((1,), (0,)))
        pre += bias
        sig = 1.0 / (1.0 + jnp.exp(-pre))
        act_ref[j] = (pre * sig).astype(BF)
        grad = (cot.astype(F32) * sig * (1.0 + pre * (1.0 - sig))).astype(BF)
        g_ref[k] = grad
        gagg_ref[j] = dot(w_neigh, grad, ((0,), (0,))).astype(BF)


def grads_kernel(ny, nw, g_ref, act_even, act_odd, *refs):
    w_refs, refs = refs[:nw], refs[nw:]
    even, odd, agg = refs[:ny], refs[ny : 2 * ny], refs[2 * ny : 4 * ny]
    back_even, back_odd, *out_refs = refs[4 * ny :]
    w_self, _ = weights(w_refs)
    small, width = w_self.shape
    sub = out_refs[0].shape[1]
    xs = []
    for k in range(2 * ny):
        j = k // 2
        act_ref, back_ref = (act_odd, back_odd) if k % 2 else (act_even, back_even)
        back_ref[j, :width] = dot(w_self, g_ref[k], ((0,), (0,))).astype(BF)
        back_ref[j, width:] = act_ref[j]
        xs.append(odd[j][:width, :] if k % 2 else even[j][small : small + width, :])
    grad = jnp.concatenate([g_ref[k] for k in range(2 * ny)], axis=1)
    own = dot(grad, jnp.concatenate(xs, axis=1), ((1,), (1,))).astype(BF)
    neigh = dot(grad, jnp.concatenate([r[...] for r in agg], axis=1), ((1,), (1,))).astype(BF)
    total = jnp.sum(grad.astype(F32), axis=1, keepdims=True)
    high = total.astype(BF).astype(F32)
    lane = lax.broadcasted_iota(jnp.int32, (small, T), 1)
    both = jnp.where(lane == 0, high, jnp.where(lane == 1, total - high, 0.0)).astype(BF)
    nz = out_refs[0].shape[0]
    for i in range(small // sub):
        rows, out_ref = slice(i * sub, (i + 1) * sub), out_refs[i // nz]
        out_ref[i % nz, :, :width] = own[rows]
        out_ref[i % nz, :, width : 2 * width] = neigh[rows]
        out_ref[i % nz, :, 2 * width :] = both[rows]


def pair_kernel(even_ref, got_ref, *out_refs):
    for j, out_ref in enumerate(out_refs):
        out_ref[...] = (even_ref[j].astype(F32) + got_ref[j].astype(F32)).astype(BF)


def back_pair_kernel(width, even_ref, got_ref, *out_refs):
    for j, out_ref in enumerate(out_refs):
        both = even_ref[j, :width].astype(F32) + got_ref[j, :width].astype(F32)
        small = even_ref.shape[1] - width
        out_ref[:width] = both.astype(BF)
        out_ref[width : width + small] = even_ref[j, width:]
        out_ref[width + small :] = got_ref[j, width:]


def back_pack_kernel(blocks, me_ref, block_ref, *refs):
    *in_refs, out_ref = refs
    groups, chunks, sub, piece = out_ref.shape
    n = chunks // 2
    width = groups * n * sub
    small = groups * sub
    total = in_refs[0][:width].astype(F32)
    for r in in_refs[1:]:
        total += r[:width].astype(F32)
    out_ref[:, :n] = total.astype(BF).reshape(groups, n, sub, piece)
    for k in range(2 * len(in_refs)):
        d = me_ref[0] ^ k
        for i, f in enumerate(blocks):
            at = width + (k % 2) * small + i * sub
            out_ref[block_ref[0] ^ f, n + d] = in_refs[k // 2][at : at + sub]


def wsum_kernel(width, *refs):
    *in_refs, out_ref = refs
    total = in_refs[0][...].astype(F32)
    for r in in_refs[1:]:
        total += r[...].astype(F32)
    out_ref[:, : 2 * width] = total[:, : 2 * width].astype(BF)
    bias = jnp.sum(total[:, 2 * width :], axis=1, keepdims=True)
    high = bias.astype(BF).astype(F32)
    lane = lax.broadcasted_iota(jnp.int32, (total.shape[0], T), 1)
    both = jnp.where(lane == 0, high, jnp.where(lane == 1, bias - high, 0.0))
    out_ref[:, 2 * width :] = both.astype(BF)


def wout_kernel(me_ref, *refs):
    *in_refs, self_ref, neigh_ref, bias_ref = refs
    width = self_ref.shape[2]
    for k, ref in enumerate(in_refs):
        d = me_ref[0] ^ k
        self_ref[d] = ref[:, :width].astype(F32)
        neigh_ref[d] = ref[:, width : 2 * width].astype(F32)
        total = jnp.sum(ref[:, 2 * width :].astype(F32), axis=1, keepdims=True)
        bias_ref[d] = jnp.broadcast_to(total, bias_ref.shape[1:])


def halo_grad_kernel(ga_ref, ext_ref, flat_ref, *out_refs):
    ga = jnp.concatenate([ga_ref[b] for b in range(ga_ref.shape[0])], axis=1)
    flat_ref[...] = ga
    for k, out_ref in enumerate(out_refs):
        span = slice(k * 2 * T, (k + 1) * 2 * T)
        out_ref[...] = dot(ga, ext_ref[:, span], ((1,), (0,))).astype(BF)


def add_returned(total, at, me_ref, send_ref, hub_ref, ret_refs):
    rows = lax.broadcasted_iota(jnp.int32, (total.shape[1], T), 0) + at
    hub = (rows == hub_ref[...]).astype(F32).astype(BF)
    hots, cols, hubs = [], [], 0.0
    for q, ret_ref in enumerate(ret_refs):
        idx = send_ref[pl.ds(me_ref[0] ^ q, 1), :]
        hots.append((rows == idx).astype(F32).astype(BF))
        cols.append(ret_ref[:, :T])
        hubs += ret_ref[:, T:].astype(F32)
    high = hubs.astype(BF)
    cols += [high, (hubs - high.astype(F32)).astype(BF)]
    hots += [hub, hub]
    return total + dot(jnp.concatenate(cols, axis=1), jnp.concatenate(hots, axis=1), ((1,), (1,)))


SPLIT = 4


def times_owned(ga_ref, own_refs):
    depth = own_refs[0].shape[0]
    total = 0.0
    for r, ref in enumerate(own_refs):
        total += dot(ga_ref[:, r * depth : (r + 1) * depth], ref[...], ((1,), (0,)))
    return total


def finish_rest_kernel(top, me_ref, ga_ref, send_ref, hub_ref, *refs):
    own_refs, ret_refs, out_ref = refs[:SPLIT], refs[SPLIT:-1], refs[-1]
    at = (pl.program_id(0) + top) * out_ref.shape[1]
    total = times_owned(ga_ref, own_refs)
    out_ref[...] = add_returned(total, at, me_ref, send_ref, hub_ref, ret_refs)


def finish_dst_kernel(me_ref, ga_ref, send_ref, hub_ref, back_ref, grads_ref, *refs):
    own_refs, ret_refs, out_ref, act_ref = refs[:SPLIT], refs[SPLIT:-2], refs[-2], refs[-1]
    rows = ga_ref.shape[0]
    groups = range(back_ref.shape[0])
    own = jnp.concatenate([back_ref[b, :rows] for b in groups], axis=1).astype(F32)
    act_ref[...] = jnp.concatenate([back_ref[b, rows:] for b in groups], axis=1)
    at = pl.program_id(0) * out_ref.shape[1]
    total = times_owned(ga_ref, own_refs) + own
    out_ref[...] = add_returned(total, at, me_ref, send_ref, hub_ref, ret_refs)


def column(rows, first):
    return pl.BlockSpec((rows, WIDE), lambda i: (0, i + first))


def row_blocks(n_dst, first):
    block = (None, n_dst // SPLIT, WIDE)
    return [pl.BlockSpec(block, lambda i, r=r: (i + first, r, 0)) for r in range(SPLIT)]


def fixed(x):
    return pl.BlockSpec(x.shape, lambda i: (0, 0))


def finish_rest(me, ga, own, ret, sends, hubs, n_dst):
    rows, n, top = ga.shape[0], own.shape[0] * WIDE, n_dst // WIDE
    return pl.pallas_call(
        functools.partial(finish_rest_kernel, top),
        out_shape=shape(rows, n, kind=F32),
        grid=(n // WIDE - top,),
        in_specs=[SMEM, fixed(ga), fixed(sends), fixed(hubs)]
        + row_blocks(n_dst, top)
        + [fixed(r) for r in ret],
        out_specs=column(rows, top),
        compiler_params=pltpu.CompilerParams(vmem_limit_bytes=56 * MIB),
        cost_estimate=pl.CostEstimate(flops=0, bytes_accessed=18000000, transcendentals=0),
        name="finish_rest",
    )(me, ga, sends, hubs, *[own] * SPLIT, *ret)


def finish_dst(me, ga, own, ret, sends, hubs, back, grads):
    rows, n = grads.shape
    groups, _, piece = back.shape
    n_dst = groups * piece
    return pl.pallas_call(
        finish_dst_kernel,
        out_shape=[shape(rows, n, kind=F32), shape(rows, n_dst)],
        grid=(n_dst // WIDE,),
        in_specs=[
            SMEM,
            fixed(ga),
            fixed(sends),
            fixed(hubs),
            pl.BlockSpec((WIDE // piece, 2 * rows, piece), lambda i: (i, 0, 0)),
            pl.BlockSpec(memory_space=pl.ANY),
        ]
        + row_blocks(n_dst, 0)
        + [fixed(r) for r in ret],
        out_specs=[column(rows, 0), column(rows, 0)],
        input_output_aliases={5: 0},
        compiler_params=pltpu.CompilerParams(vmem_limit_bytes=56 * MIB),
        cost_estimate=pl.CostEstimate(flops=0, bytes_accessed=6000000, transcendentals=0),
        name="finish_dst",
    )(me, ga, sends, hubs, back, grads, *[own] * SPLIT, *ret)


def body(
    node_feats,
    send_rows,
    hub_rows,
    tile_dst,
    tile_src,
    tile_count,
    tile_vals,
    w_self,
    w_neigh,
    bias_vec,
    cotangent,
):
    n_dom = lax.axis_size("dom")
    n_feat = lax.axis_size("feat")
    ny, nz = n_dom // 2, n_feat // 2
    rows = node_feats.shape[0]
    own_rows = node_feats.shape[1]
    dst_rows = cotangent.shape[1]
    width = w_self.shape[1]
    n_own, n_dst = own_rows // T, dst_rows // T
    n_src = n_own + 2 * n_dom
    piece = dst_rows // n_feat
    sub = w_self.shape[0] // n_dom
    small = n_feat * sub
    me = lax.axis_index("dom")
    block = lax.axis_index("feat")
    me_s, block_s = me.reshape(1), block.reshape(1)

    def over_dom(x, k):
        return lax.ppermute(x, "dom", [(i, i ^ k) for i in range(n_dom)])

    def over_feat(x, k):
        return lax.ppermute(x, "feat", [(i, i ^ k) for i in range(n_feat)])

    def after(x, *events):
        return lax.optimization_barrier((x, events))[0]

    mine = jnp.stack(
        [
            lax.dynamic_slice_in_dim(w_self, me * sub, sub, axis=0),
            lax.dynamic_slice_in_dim(w_neigh, me * sub, sub, axis=0),
        ]
    )
    w, blocks = [mine[None]], [0]
    for bit in [1 << i for i in range(n_feat.bit_length() - 2, 0, -1)]:
        send = w[0] if len(w) == 1 else jnp.concatenate(w, axis=0)
        w.append(over_feat(send, bit))
        blocks += [k ^ bit for k in blocks]
    blocks += [k ^ 1 for k in blocks]

    sends, hubs = send_rows.reshape(n_dom, T), hub_rows[None, :]
    first, *outgoing = pack(
        me_s, node_feats, cotangent, bias_vec[None, :], sends, hubs, sub, n_feat
    )
    first = after(first, w[1])
    first = lax.all_to_all(first, "feat", 0, 0, tiled=True)
    incoming = [outgoing[0]] + [over_dom(outgoing[k], k) for k in range(1, n_dom)]

    halo_tile = n_own + 2 * ((tile_src - n_own) ^ me)
    hub_tile = n_own + 2 * ((tile_src - n_own - n_dom) ^ me) + 1
    place = jnp.where(
        tile_src < n_own, tile_src, jnp.where(tile_src < n_own + n_dom, halo_tile, hub_tile)
    )
    n_pos = n_dst * n_src
    slot = jnp.arange(tile_dst.shape[0], dtype=jnp.int32)
    key = jnp.where(slot < tile_count[0], tile_dst * n_src + place, n_pos)
    before = (key[None, :] < key[:, None]) | (
        (key[None, :] == key[:, None]) & (slot[None, :] < slot[:, None])
    )
    rank = jnp.sum(before.astype(jnp.int32), axis=1)
    order = jnp.sum(jnp.where(rank[:, None] == slot[None, :], slot[:, None], 0), axis=0)
    order = jnp.concatenate([order, jnp.zeros((2,), jnp.int32)])
    ends = jnp.arange(n_pos + 1, dtype=jnp.int32)
    start = jnp.sum((key[None, :] < ends[:, None]).astype(jnp.int32), axis=1)
    a_own, a_ext, agg = build_dense(
        tile_vals, order, start, node_feats, incoming, n_dst, n_src, n_own, n_feat
    )

    w[-1] = after(w[-1], agg)
    agg = after(agg, first)
    first = after(first, w[-1])
    w.append(over_feat(jnp.concatenate(w, axis=0), 1))
    agg = lax.all_to_all(agg, "feat", 0, 0, tiled=True).reshape(width, piece)

    bias, even, odd, *cross = whole_call(
        functools.partial(split_kernel, blocks, n_dom),
        "split",
        1.5,
        [
            shape(small, T, kind=F32),
            shape(small + width, piece),
            shape(small + width, piece),
        ]
        + [shape(2 * small + width, piece)] * (ny - 1),
        me_s,
        block_s,
        first,
        scalars=2,
    )
    cross = [over_dom(c, 2 * (j + 1)) for j, c in enumerate(cross)]
    evens = [even] + cross
    odds = [over_dom(odd, 1)] + [over_dom(c[small:], 1) for c in cross]
    agg_even = [agg] + [over_dom(agg, 2 * j) for j in range(1, ny)]
    agg_odd = [over_dom(a, 1) for a in agg_even]
    aggs = [a for pair in zip(agg_even, agg_odd) for a in pair]

    grad, act_even, act_odd, gagg_even, gagg_odd = whole_call(
        functools.partial(dense_kernel, ny, len(w)),
        "dense",
        3.0,
        [
            shape(n_dom, small, piece),
            shape(ny, small, piece),
            shape(ny, small, piece),
            shape(ny, width, piece),
            shape(ny, width, piece),
        ],
        bias,
        *w,
        *evens,
        *odds,
        *aggs,
    )

    got = over_dom(gagg_odd, 1)
    pair = whole_call(pair_kernel, "pair", 1.0, [shape(width, piece)] * ny, gagg_even, got)

    back_even, back_odd, parts, parts_odd = whole_call(
        functools.partial(grads_kernel, ny, len(w)),
        "grads",
        3.0,
        [
            shape(ny, width + small, piece),
            shape(ny, width + small, piece),
            shape(nz, sub, 2 * width + T),
            shape(nz, sub, 2 * width + T),
        ],
        grad,
        act_even,
        act_odd,
        *w,
        *evens,
        *odds,
        *aggs,
    )
    parts_odd, back_odd = after(parts_odd, pair), after(back_odd, pair)

    gagg = pair[0].astype(F32)
    for j in range(1, ny):
        gagg += over_dom(pair[j], 2 * j).astype(F32)
    gagg = gagg.astype(BF).reshape(n_feat, rows, piece)
    from_x = over_feat(parts_odd, 1)
    from_core = over_dom(back_odd, 1)
    from_x, from_core = after(from_x, gagg), after(from_core, gagg)

    gagg = lax.all_to_all(gagg, "feat", 0, 0, tiled=True)
    parts = whole_call(pair_kernel, "x_sum", 1.0, [shape(sub, 2 * width + T)] * nz, parts, from_x)
    back = whole_call(
        functools.partial(back_pair_kernel, width),
        "back_pair",
        1.0,
        [shape(width + 2 * small, piece)] * ny,
        back_even,
        from_core,
    )
    back = [back[0]] + [over_dom(back[j], 2 * j) for j in range(1, ny)]
    gagg = after(gagg, parts)
    parts = [parts[0]] + [over_feat(parts[j], blocks[j]) for j in range(1, nz)]

    gagg, *halo_grad = whole_call(
        halo_grad_kernel,
        "halo_grads",
        1.0,
        [shape(rows, dst_rows)] + [shape(rows, 2 * T)] * n_dom,
        gagg,
        a_ext,
    )
    returned = [halo_grad[0]] + [over_dom(halo_grad[k], k) for k in range(1, n_dom)]
    back = after(back, halo_grad, parts)

    back = whole_call(
        functools.partial(back_pack_kernel, blocks),
        "back_pack",
        1.0,
        shape(n_feat, 2 * n_dom, sub, piece),
        me_s,
        block_s,
        *back,
        scalars=2,
    )
    back = lax.all_to_all(back, "feat", 0, 0, tiled=True).reshape(n_feat, 2 * rows, piece)
    total = whole_call(
        functools.partial(wsum_kernel, width), "w_sum", 1.0, shape(sub, 2 * width + T), *parts
    )
    whole = [total] + [over_dom(total, 2 * j) for j in range(1, ny)]
    grads = finish_rest(me_s, gagg, a_own, returned, sends, hubs, dst_rows)
    whole[1:] = [after(e, grads) for e in whole[1:]]
    whole = [t for e in whole for t in (e, over_dom(e, 1))]
    grad_self, grad_neigh, grad_bias = whole_call(
        wout_kernel,
        "w_out",
        1.0,
        [
            shape(n_dom, sub, width, kind=F32),
            shape(n_dom, sub, width, kind=F32),
            shape(n_dom, sub, T, kind=F32),
        ],
        me_s,
        *whole,
        scalars=1,
    )

    grad_feats, activations = finish_dst(
        me_s, gagg, a_own, returned, sends, hubs, back, grads
    )
    return (
        activations,
        grad_feats,
        grad_self.reshape(n_dom * sub, width),
        grad_neigh.reshape(n_dom * sub, width),
        grad_bias[:, :, 0].reshape(n_dom * sub),
    )


def solution(mesh):
    return jax.shard_map(
        body,
        mesh=mesh,
        in_specs=(
            P("feat", "dom"),
            P("dom"),
            P("dom"),
            P("dom"),
            P("dom"),
            P("dom"),
            P("dom", None, None),
            P("feat", None),
            P("feat", None),
            P("feat"),
            P("feat", "dom"),
        ),
        out_specs=(P("feat", "dom"), P("feat", "dom"), P("feat", None), P("feat", None), P("feat")),
        check_vma=False,
    )
```

```python
import functools

import jax
import jax.numpy as jnp
from jax import lax
from jax.experimental import pallas as pl
from jax.experimental.pallas import tpu as pltpu
from jax.sharding import PartitionSpec as P

T = 128
BF = jnp.bfloat16
F32 = jnp.float32
MIB = 1 << 20
WIDE = 512
VMEM = pl.BlockSpec(memory_space=pltpu.VMEM)
SMEM = pl.BlockSpec(memory_space=pltpu.SMEM)


def dot(left, right, dims):
    return lax.dot_general(left, right, (dims, ((), ())), preferred_element_type=F32)


def shape(*dims, kind=BF):
    return jax.ShapeDtypeStruct(dims, kind)


def whole_call(kernel, name, micros, out_shape, *args, scalars=0, mib=24):
    many = isinstance(out_shape, (list, tuple))
    return pl.pallas_call(
        kernel,
        out_shape=out_shape,
        in_specs=[SMEM] * scalars + [VMEM] * (len(args) - scalars),
        out_specs=[VMEM] * len(out_shape) if many else VMEM,
        compiler_params=pltpu.CompilerParams(vmem_limit_bytes=mib * MIB),
        cost_estimate=pl.CostEstimate(
            flops=0, bytes_accessed=int(micros * 3.0e6), transcendentals=0
        ),
        name=name,
    )(*args)


def pack_kernel(sub, me_ref, x_ref, cot_ref, bias_ref, send_ref, hub_ref, first_ref, *out_refs):
    groups, chunks, _, piece = first_ref.shape
    n = x_ref.shape[0] // sub
    bias = bias_ref[...]
    high = bias.astype(BF).astype(F32)
    row = lax.broadcasted_iota(jnp.int32, (sub, piece), 0)
    tail = jnp.where(row == 0, high, jnp.where(row == 1, bias - high, 0.0)).astype(BF)
    for b in range(groups):
        cols = slice(b * piece, (b + 1) * piece)
        first_ref[b, :n] = x_ref[:, cols].reshape(n, sub, piece)
        first_ref[b, n : 2 * n] = cot_ref[:, cols].reshape(n, sub, piece)
        first_ref[b, 2 * n] = tail
    x = x_ref[...]
    rows = lax.broadcasted_iota(jnp.int32, (x.shape[1], T), 0)
    readers = len(out_refs)
    for q in range(readers + 1):
        idx = send_ref[pl.ds(me_ref[0] ^ q, 1), :] if q < readers else hub_ref[...]
        hot = (rows == idx).astype(F32).astype(BF)
        got = dot(x, hot, ((1,), (0,))).astype(BF)
        if q < readers:
            out_refs[q][:, :T] = got
        else:
            for r in range(readers):
                out_refs[r][:, T:] = got


def pack(me, x, cot, bias, sends, hubs, sub, n_feat):
    n_dom = sends.shape[0]
    rows = x.shape[0]
    args = (x, cot, bias, sends, hubs)
    outs = [shape(n_feat, 2 * n_dom + 1, sub, cot.shape[1] // n_feat)]
    outs += [shape(rows, 2 * T)] * n_dom
    return pl.pallas_call(
        functools.partial(pack_kernel, sub),
        out_shape=outs,
        grid=(1,),
        in_specs=[SMEM] + [pl.BlockSpec(a.shape, lambda i, n=a.ndim: (0,) * n) for a in args],
        out_specs=[pl.BlockSpec(o.shape, lambda i, n=len(o.shape): (0,) * n) for o in outs],
        compiler_params=pltpu.CompilerParams(vmem_limit_bytes=60 * MIB),
        cost_estimate=pl.CostEstimate(flops=0, bytes_accessed=12000000, transcendentals=0),
        name="pack",
    )(me, *args)


def build_kernel(n_own, order_ref, start_ref, x_ref, vals_hbm, *refs):
    *halo_refs, own_ref, ext_ref, agg_ref, vals, sems = refs
    step = pl.program_id(0)
    slots = vals_hbm.shape[0]
    n_src = n_own + ext_ref.shape[1] // T
    tiles, wide = own_ref.shape[1] // T, own_ref.shape[2]
    chunks = sems.shape[0]
    per = slots // chunks

    def piece(i):
        span = pl.ds(i * per, per)
        return pltpu.make_async_copy(vals_hbm.at[span], vals.at[span], sems.at[i])

    @pl.when(step == 0)
    def _():
        for i in range(chunks):
            piece(i).start()
        vals[slots] = jnp.zeros((T, T), BF)
        for i in range(chunks):
            piece(i).wait()

    for v in range(tiles):
        rows = slice(v * T, (v + 1) * T)
        for s in range(n_src):
            p = (step * tiles + v) * n_src + s
            first, last = start_ref[p], start_ref[p + 1]
            one = jnp.where(last > first, order_ref[first], slots)
            two = jnp.where(last > first + 1, order_ref[first + 1], slots)
            total = vals[one].astype(F32) + vals[two].astype(F32)

            def more(i, total):
                return total + vals[order_ref[i]].astype(F32)

            total = lax.fori_loop(first + 2, last, more, total).astype(BF)
            if s < n_own:
                at = s * T % wide
                own_ref[s * T // wide, rows, at : at + T] = total
            else:
                ext_ref[rows, (s - n_own) * T : (s - n_own + 1) * T] = total
    halo = jnp.concatenate([r[...] for r in halo_refs], axis=1)
    total = 0.0
    for b in range(own_ref.shape[0]):
        total += dot(x_ref[:, b * wide : (b + 1) * wide], own_ref[b], ((1,), (1,)))
    total = (total + dot(halo, ext_ref[...], ((1,), (1,)))).astype(BF)
    piece_n = agg_ref.shape[2]
    for b in range(agg_ref.shape[0]):
        agg_ref[b] = total[:, b * piece_n : (b + 1) * piece_n]


def build_dense(vals, order, start, x, halos, n_dst, n_src, n_own, n_feat):
    rows = x.shape[0]
    piece = n_dst * T // n_feat
    ext = (n_src - n_own) * T
    return pl.pallas_call(
        functools.partial(build_kernel, n_own),
        out_shape=(
            shape(n_own * T // WIDE, n_dst * T, WIDE),
            shape(n_dst * T, ext),
            shape(n_feat, rows, piece),
        ),
        grid_spec=pltpu.PrefetchScalarGridSpec(
            num_scalar_prefetch=2,
            grid=(n_dst // 2,),
            in_specs=[VMEM, pl.BlockSpec(memory_space=pl.ANY)] + [VMEM] * len(halos),
            out_specs=[
                pl.BlockSpec((n_own * T // WIDE, 2 * T, WIDE), lambda u, *_: (0, u, 0)),
                pl.BlockSpec((2 * T, ext), lambda u, *_: (u, 0)),
                pl.BlockSpec((2 * T // piece, rows, piece), lambda u, *_: (u, 0, 0)),
            ],
            scratch_shapes=[
                pltpu.VMEM((vals.shape[0] + 1, T, T), BF),
                pltpu.SemaphoreType.DMA((8,)),
            ],
        ),
        compiler_params=pltpu.CompilerParams(vmem_limit_bytes=58 * MIB),
        cost_estimate=pl.CostEstimate(flops=0, bytes_accessed=30000000, transcendentals=0),
        name="build_dense",
    )(order, start, x, vals, *halos)


def split_kernel(blocks, n_dom, me_ref, block_ref, first_ref, bias_ref, *out_refs):
    _, _, sub, piece = first_ref.shape
    n = (first_ref.shape[1] - 1) // 2
    small = len(blocks) * sub
    width = len(blocks) * n * sub
    x = first_ref[:, :n].reshape(width, piece)
    row = lax.broadcasted_iota(jnp.int32, (sub, piece), 0) + me_ref[0] * sub
    lane = lax.broadcasted_iota(jnp.int32, (sub, piece), 1)
    for i, k in enumerate(blocks):
        b = block_ref[0] ^ k
        both = first_ref[b, 2 * n, 0:1].astype(F32) + first_ref[b, 2 * n, 1:2].astype(F32)
        mine = jnp.sum(jnp.where(row == lane, both, 0.0), axis=1, keepdims=True)
        bias_ref[i * sub : (i + 1) * sub, :] = jnp.broadcast_to(mine, (sub, T))
    even, odd = out_refs[0], out_refs[1]
    even[small:] = x
    odd[:width] = x
    for i, k in enumerate(blocks):
        b = block_ref[0] ^ k
        even[i * sub : (i + 1) * sub] = first_ref[b, n + me_ref[0]]
        odd[width + i * sub : width + (i + 1) * sub] = first_ref[b, n + (me_ref[0] ^ 1)]
    for j in range(1, n_dom // 2):
        ref = out_refs[1 + j]
        ref[small : small + width] = x
        for i, k in enumerate(blocks):
            b = block_ref[0] ^ k
            at = small + width + i * sub
            ref[i * sub : (i + 1) * sub] = first_ref[b, n + (me_ref[0] ^ (2 * j))]
            ref[at : at + sub] = first_ref[b, n + (me_ref[0] ^ (2 * j + 1))]


def weights(refs):
    return [jnp.concatenate([r[g, m] for r in refs for g in range(r.shape[0])]) for m in (0, 1)]


def dense_kernel(ny, nw, bias_ref, *refs):
    w_refs, refs = refs[:nw], refs[nw:]
    even, odd, agg = refs[:ny], refs[ny : 2 * ny], refs[2 * ny : 4 * ny]
    g_ref, act_even, act_odd, gagg_even, gagg_odd = refs[4 * ny :]
    w_self, w_neigh = weights(w_refs)
    small, width = w_self.shape
    bias = bias_ref[:, :1]
    for k in range(2 * ny):
        j = k // 2
        if k % 2 == 0:
            cot, x = even[j][:small, :], even[j][small : small + width, :]
            act_ref, gagg_ref = act_even, gagg_even
        else:
            x, cot = odd[j][:width, :], odd[j][width:, :]
            act_ref, gagg_ref = act_odd, gagg_odd
        pre = dot(w_self, x, ((1,), (0,)))
        pre += dot(w_neigh, agg[k][...], ((1,), (0,)))
        pre += bias
        sig = 1.0 / (1.0 + jnp.exp(-pre))
        act_ref[j] = (pre * sig).astype(BF)
        grad = (cot.astype(F32) * sig * (1.0 + pre * (1.0 - sig))).astype(BF)
        g_ref[k] = grad
        gagg_ref[j] = dot(w_neigh, grad, ((0,), (0,))).astype(BF)


def grads_kernel(ny, nw, g_ref, act_even, act_odd, *refs):
    w_refs, refs = refs[:nw], refs[nw:]
    even, odd, agg = refs[:ny], refs[ny : 2 * ny], refs[2 * ny : 4 * ny]
    back_even, back_odd, *out_refs = refs[4 * ny :]
    w_self, _ = weights(w_refs)
    small, width = w_self.shape
    sub = out_refs[0].shape[1]
    xs = []
    for k in range(2 * ny):
        j = k // 2
        act_ref, back_ref = (act_odd, back_odd) if k % 2 else (act_even, back_even)
        back_ref[j, :width] = dot(w_self, g_ref[k], ((0,), (0,))).astype(BF)
        back_ref[j, width:] = act_ref[j]
        xs.append(odd[j][:width, :] if k % 2 else even[j][small : small + width, :])
    grad = jnp.concatenate([g_ref[k] for k in range(2 * ny)], axis=1)
    own = dot(grad, jnp.concatenate(xs, axis=1), ((1,), (1,))).astype(BF)
    neigh = dot(grad, jnp.concatenate([r[...] for r in agg], axis=1), ((1,), (1,))).astype(BF)
    total = jnp.sum(grad.astype(F32), axis=1, keepdims=True)
    high = total.astype(BF).astype(F32)
    lane = lax.broadcasted_iota(jnp.int32, (small, T), 1)
    both = jnp.where(lane == 0, high, jnp.where(lane == 1, total - high, 0.0)).astype(BF)
    nz = out_refs[0].shape[0]
    for i in range(small // sub):
        rows, out_ref = slice(i * sub, (i + 1) * sub), out_refs[i // nz]
        out_ref[i % nz, :, :width] = own[rows]
        out_ref[i % nz, :, width : 2 * width] = neigh[rows]
        out_ref[i % nz, :, 2 * width :] = both[rows]


def pair_kernel(even_ref, got_ref, *out_refs):
    for j, out_ref in enumerate(out_refs):
        out_ref[...] = (even_ref[j].astype(F32) + got_ref[j].astype(F32)).astype(BF)


def back_pair_kernel(width, even_ref, got_ref, *out_refs):
    for j, out_ref in enumerate(out_refs):
        both = even_ref[j, :width].astype(F32) + got_ref[j, :width].astype(F32)
        small = even_ref.shape[1] - width
        out_ref[:width] = both.astype(BF)
        out_ref[width : width + small] = even_ref[j, width:]
        out_ref[width + small :] = got_ref[j, width:]


def back_pack_kernel(blocks, me_ref, block_ref, *refs):
    *in_refs, out_ref = refs
    groups, chunks, sub, piece = out_ref.shape
    n = chunks // 2
    width = groups * n * sub
    small = groups * sub
    total = in_refs[0][:width].astype(F32)
    for r in in_refs[1:]:
        total += r[:width].astype(F32)
    out_ref[:, :n] = total.astype(BF).reshape(groups, n, sub, piece)
    for k in range(2 * len(in_refs)):
        d = me_ref[0] ^ k
        for i, f in enumerate(blocks):
            at = width + (k % 2) * small + i * sub
            out_ref[block_ref[0] ^ f, n + d] = in_refs[k // 2][at : at + sub]


def wsum_kernel(width, *refs):
    *in_refs, out_ref = refs
    total = in_refs[0][...].astype(F32)
    for r in in_refs[1:]:
        total += r[...].astype(F32)
    out_ref[:, : 2 * width] = total[:, : 2 * width].astype(BF)
    bias = jnp.sum(total[:, 2 * width :], axis=1, keepdims=True)
    high = bias.astype(BF).astype(F32)
    lane = lax.broadcasted_iota(jnp.int32, (total.shape[0], T), 1)
    both = jnp.where(lane == 0, high, jnp.where(lane == 1, bias - high, 0.0))
    out_ref[:, 2 * width :] = both.astype(BF)


def wout_kernel(me_ref, *refs):
    *in_refs, self_ref, neigh_ref, bias_ref = refs
    width = self_ref.shape[2]
    for k, ref in enumerate(in_refs):
        d = me_ref[0] ^ k
        self_ref[d] = ref[:, :width].astype(F32)
        neigh_ref[d] = ref[:, width : 2 * width].astype(F32)
        total = jnp.sum(ref[:, 2 * width :].astype(F32), axis=1, keepdims=True)
        bias_ref[d] = jnp.broadcast_to(total, bias_ref.shape[1:])


def halo_grad_kernel(ga_ref, ext_ref, flat_ref, *out_refs):
    ga = jnp.concatenate([ga_ref[b] for b in range(ga_ref.shape[0])], axis=1)
    flat_ref[...] = ga
    for k, out_ref in enumerate(out_refs):
        span = slice(k * 2 * T, (k + 1) * 2 * T)
        out_ref[...] = dot(ga, ext_ref[:, span], ((1,), (0,))).astype(BF)


def add_returned(total, at, me_ref, send_ref, hub_ref, ret_refs):
    rows = lax.broadcasted_iota(jnp.int32, (total.shape[1], T), 0) + at
    hub = (rows == hub_ref[...]).astype(F32).astype(BF)
    hots, cols, hubs = [], [], 0.0
    for q, ret_ref in enumerate(ret_refs):
        idx = send_ref[pl.ds(me_ref[0] ^ q, 1), :]
        hots.append((rows == idx).astype(F32).astype(BF))
        cols.append(ret_ref[:, :T])
        hubs += ret_ref[:, T:].astype(F32)
    high = hubs.astype(BF)
    cols += [high, (hubs - high.astype(F32)).astype(BF)]
    hots += [hub, hub]
    return total + dot(jnp.concatenate(cols, axis=1), jnp.concatenate(hots, axis=1), ((1,), (1,)))


SPLIT = 4


def times_owned(ga_ref, own_refs):
    depth = own_refs[0].shape[0]
    total = 0.0
    for r, ref in enumerate(own_refs):
        total += dot(ga_ref[:, r * depth : (r + 1) * depth], ref[...], ((1,), (0,)))
    return total


def finish_rest_kernel(top, me_ref, ga_ref, send_ref, hub_ref, *refs):
    own_refs, ret_refs, out_ref = refs[:SPLIT], refs[SPLIT:-1], refs[-1]
    at = (pl.program_id(0) + top) * out_ref.shape[1]
    total = times_owned(ga_ref, own_refs)
    out_ref[...] = add_returned(total, at, me_ref, send_ref, hub_ref, ret_refs)


def finish_dst_kernel(me_ref, ga_ref, send_ref, hub_ref, back_ref, grads_ref, *refs):
    own_refs, ret_refs, out_ref, act_ref = refs[:SPLIT], refs[SPLIT:-2], refs[-2], refs[-1]
    rows = ga_ref.shape[0]
    groups = range(back_ref.shape[0])
    own = jnp.concatenate([back_ref[b, :rows] for b in groups], axis=1).astype(F32)
    act_ref[...] = jnp.concatenate([back_ref[b, rows:] for b in groups], axis=1)
    at = pl.program_id(0) * out_ref.shape[1]
    total = times_owned(ga_ref, own_refs) + own
    out_ref[...] = add_returned(total, at, me_ref, send_ref, hub_ref, ret_refs)


def column(rows, first):
    return pl.BlockSpec((rows, WIDE), lambda i: (0, i + first))


def row_blocks(n_dst, first):
    block = (None, n_dst // SPLIT, WIDE)
    return [pl.BlockSpec(block, lambda i, r=r: (i + first, r, 0)) for r in range(SPLIT)]


def fixed(x):
    return pl.BlockSpec(x.shape, lambda i: (0, 0))


def finish_rest(me, ga, own, ret, sends, hubs, n_dst):
    rows, n, top = ga.shape[0], own.shape[0] * WIDE, n_dst // WIDE
    return pl.pallas_call(
        functools.partial(finish_rest_kernel, top),
        out_shape=shape(rows, n, kind=F32),
        grid=(n // WIDE - top,),
        in_specs=[SMEM, fixed(ga), fixed(sends), fixed(hubs)]
        + row_blocks(n_dst, top)
        + [fixed(r) for r in ret],
        out_specs=column(rows, top),
        compiler_params=pltpu.CompilerParams(vmem_limit_bytes=56 * MIB),
        cost_estimate=pl.CostEstimate(flops=0, bytes_accessed=18000000, transcendentals=0),
        name="finish_rest",
    )(me, ga, sends, hubs, *[own] * SPLIT, *ret)


def finish_dst(me, ga, own, ret, sends, hubs, back, grads):
    rows, n = grads.shape
    groups, _, piece = back.shape
    n_dst = groups * piece
    return pl.pallas_call(
        finish_dst_kernel,
        out_shape=[shape(rows, n, kind=F32), shape(rows, n_dst)],
        grid=(n_dst // WIDE,),
        in_specs=[
            SMEM,
            fixed(ga),
            fixed(sends),
            fixed(hubs),
            pl.BlockSpec((WIDE // piece, 2 * rows, piece), lambda i: (i, 0, 0)),
            pl.BlockSpec(memory_space=pl.ANY),
        ]
        + row_blocks(n_dst, 0)
        + [fixed(r) for r in ret],
        out_specs=[column(rows, 0), column(rows, 0)],
        input_output_aliases={5: 0},
        compiler_params=pltpu.CompilerParams(vmem_limit_bytes=56 * MIB),
        cost_estimate=pl.CostEstimate(flops=0, bytes_accessed=6000000, transcendentals=0),
        name="finish_dst",
    )(me, ga, sends, hubs, back, grads, *[own] * SPLIT, *ret)


def body(
    node_feats,
    send_rows,
    hub_rows,
    tile_dst,
    tile_src,
    tile_count,
    tile_vals,
    w_self,
    w_neigh,
    bias_vec,
    cotangent,
):
    n_dom = lax.axis_size("dom")
    n_feat = lax.axis_size("feat")
    ny, nz = n_dom // 2, n_feat // 2
    rows = node_feats.shape[0]
    own_rows = node_feats.shape[1]
    dst_rows = cotangent.shape[1]
    width = w_self.shape[1]
    n_own, n_dst = own_rows // T, dst_rows // T
    n_src = n_own + 2 * n_dom
    piece = dst_rows // n_feat
    sub = w_self.shape[0] // n_dom
    small = n_feat * sub
    me = lax.axis_index("dom")
    block = lax.axis_index("feat")
    me_s, block_s = me.reshape(1), block.reshape(1)

    def over_dom(x, k):
        return lax.ppermute(x, "dom", [(i, i ^ k) for i in range(n_dom)])

    def over_feat(x, k):
        return lax.ppermute(x, "feat", [(i, i ^ k) for i in range(n_feat)])

    def after(x, *events):
        return lax.optimization_barrier((x, events))[0]

    mine = jnp.stack(
        [
            lax.dynamic_slice_in_dim(w_self, me * sub, sub, axis=0),
            lax.dynamic_slice_in_dim(w_neigh, me * sub, sub, axis=0),
        ]
    )
    w, blocks = [mine[None]], [0]
    for bit in [1 << i for i in range(n_feat.bit_length() - 2, 0, -1)]:
        send = w[0] if len(w) == 1 else jnp.concatenate(w, axis=0)
        w.append(over_feat(send, bit))
        blocks += [k ^ bit for k in blocks]
    blocks += [k ^ 1 for k in blocks]

    sends, hubs = send_rows.reshape(n_dom, T), hub_rows[None, :]
    first, *outgoing = pack(
        me_s, node_feats, cotangent, bias_vec[None, :], sends, hubs, sub, n_feat
    )
    first = after(first, w[1])
    first = lax.all_to_all(first, "feat", 0, 0, tiled=True)
    incoming = [outgoing[0]] + [over_dom(outgoing[k], k) for k in range(1, n_dom)]

    halo_tile = n_own + 2 * ((tile_src - n_own) ^ me)
    hub_tile = n_own + 2 * ((tile_src - n_own - n_dom) ^ me) + 1
    place = jnp.where(
        tile_src < n_own, tile_src, jnp.where(tile_src < n_own + n_dom, halo_tile, hub_tile)
    )
    n_pos = n_dst * n_src
    slot = jnp.arange(tile_dst.shape[0], dtype=jnp.int32)
    key = jnp.where(slot < tile_count[0], tile_dst * n_src + place, n_pos)
    before = (key[None, :] < key[:, None]) | (
        (key[None, :] == key[:, None]) & (slot[None, :] < slot[:, None])
    )
    rank = jnp.sum(before.astype(jnp.int32), axis=1)
    order = jnp.sum(jnp.where(rank[:, None] == slot[None, :], slot[:, None], 0), axis=0)
    order = jnp.concatenate([order, jnp.zeros((2,), jnp.int32)])
    ends = jnp.arange(n_pos + 1, dtype=jnp.int32)
    start = jnp.sum((key[None, :] < ends[:, None]).astype(jnp.int32), axis=1)
    a_own, a_ext, agg = build_dense(
        tile_vals, order, start, node_feats, incoming, n_dst, n_src, n_own, n_feat
    )

    w[-1] = after(w[-1], agg)
    agg = after(agg, first)
    first = after(first, w[-1])
    w.append(over_feat(jnp.concatenate(w, axis=0), 1))
    agg = lax.all_to_all(agg, "feat", 0, 0, tiled=True).reshape(width, piece)

    bias, even, odd, *cross = whole_call(
        functools.partial(split_kernel, blocks, n_dom),
        "split",
        1.5,
        [
            shape(small, T, kind=F32),
            shape(small + width, piece),
            shape(small + width, piece),
        ]
        + [shape(2 * small + width, piece)] * (ny - 1),
        me_s,
        block_s,
        first,
        scalars=2,
    )
    cross = [over_dom(c, 2 * (j + 1)) for j, c in enumerate(cross)]
    evens = [even] + cross
    odds = [over_dom(odd, 1)] + [over_dom(c[small:], 1) for c in cross]
    agg_even = [agg] + [over_dom(agg, 2 * j) for j in range(1, ny)]
    agg_odd = [over_dom(a, 1) for a in agg_even]
    aggs = [a for pair in zip(agg_even, agg_odd) for a in pair]

    grad, act_even, act_odd, gagg_even, gagg_odd = whole_call(
        functools.partial(dense_kernel, ny, len(w)),
        "dense",
        3.0,
        [
            shape(n_dom, small, piece),
            shape(ny, small, piece),
            shape(ny, small, piece),
            shape(ny, width, piece),
            shape(ny, width, piece),
        ],
        bias,
        *w,
        *evens,
        *odds,
        *aggs,
    )

    got = over_dom(gagg_odd, 1)
    pair = whole_call(pair_kernel, "pair", 1.0, [shape(width, piece)] * ny, gagg_even, got)

    back_even, back_odd, parts, parts_odd = whole_call(
        functools.partial(grads_kernel, ny, len(w)),
        "grads",
        3.0,
        [
            shape(ny, width + small, piece),
            shape(ny, width + small, piece),
            shape(nz, sub, 2 * width + T),
            shape(nz, sub, 2 * width + T),
        ],
        grad,
        act_even,
        act_odd,
        *w,
        *evens,
        *odds,
        *aggs,
    )
    parts_odd, back_odd = after(parts_odd, pair), after(back_odd, pair)

    gagg = pair[0].astype(F32)
    for j in range(1, ny):
        gagg += over_dom(pair[j], 2 * j).astype(F32)
    gagg = gagg.astype(BF).reshape(n_feat, rows, piece)
    from_x = over_feat(parts_odd, 1)
    from_core = over_dom(back_odd, 1)
    from_x, from_core = after(from_x, gagg), after(from_core, gagg)

    gagg = lax.all_to_all(gagg, "feat", 0, 0, tiled=True)
    parts = whole_call(pair_kernel, "x_sum", 1.0, [shape(sub, 2 * width + T)] * nz, parts, from_x)
    back = whole_call(
        functools.partial(back_pair_kernel, width),
        "back_pair",
        1.0,
        [shape(width + 2 * small, piece)] * ny,
        back_even,
        from_core,
    )
    back = [back[0]] + [over_dom(back[j], 2 * j) for j in range(1, ny)]
    gagg = after(gagg, parts)
    parts = [parts[0]] + [over_feat(parts[j], blocks[j]) for j in range(1, nz)]

    gagg, *halo_grad = whole_call(
        halo_grad_kernel,
        "halo_grads",
        1.0,
        [shape(rows, dst_rows)] + [shape(rows, 2 * T)] * n_dom,
        gagg,
        a_ext,
    )
    halo_grad = after(halo_grad, back)
    returned = [halo_grad[0]] + [over_dom(halo_grad[k], k) for k in range(1, n_dom)]
    back = after(back, halo_grad, parts)

    back = whole_call(
        functools.partial(back_pack_kernel, blocks),
        "back_pack",
        1.0,
        shape(n_feat, 2 * n_dom, sub, piece),
        me_s,
        block_s,
        *back,
        scalars=2,
    )
    back = after(back, returned[2:])
    back = lax.all_to_all(back, "feat", 0, 0, tiled=True).reshape(n_feat, 2 * rows, piece)
    total = whole_call(
        functools.partial(wsum_kernel, width), "w_sum", 1.0, shape(sub, 2 * width + T), *parts
    )
    whole = [total] + [over_dom(total, 2 * j) for j in range(1, ny)]
    grads = finish_rest(me_s, gagg, a_own, returned, sends, hubs, dst_rows)
    whole[1:] = [after(e, grads) for e in whole[1:]]
    whole = [t for e in whole for t in (e, over_dom(e, 1))]
    grad_self, grad_neigh, grad_bias = whole_call(
        wout_kernel,
        "w_out",
        1.0,
        [
            shape(n_dom, sub, width, kind=F32),
            shape(n_dom, sub, width, kind=F32),
            shape(n_dom, sub, T, kind=F32),
        ],
        me_s,
        *whole,
        scalars=1,
    )

    grad_feats, activations = finish_dst(
        me_s, gagg, a_own, returned, sends, hubs, back, grads
    )
    return (
        activations,
        grad_feats,
        grad_self.reshape(n_dom * sub, width),
        grad_neigh.reshape(n_dom * sub, width),
        grad_bias[:, :, 0].reshape(n_dom * sub),
    )


def solution(mesh):
    return jax.shard_map(
        body,
        mesh=mesh,
        in_specs=(
            P("feat", "dom"),
            P("dom"),
            P("dom"),
            P("dom"),
            P("dom"),
            P("dom"),
            P("dom", None, None),
            P("feat", None),
            P("feat", None),
            P("feat"),
            P("feat", "dom"),
        ),
        out_specs=(P("feat", "dom"), P("feat", "dom"), P("feat", None), P("feat", None), P("feat")),
        check_vma=False,
    )
```

```python
import functools

import jax
import jax.numpy as jnp
from jax import lax
from jax.experimental import pallas as pl
from jax.experimental.pallas import tpu as pltpu
from jax.sharding import PartitionSpec as P

T = 128
BF = jnp.bfloat16
F32 = jnp.float32
MIB = 1 << 20
WIDE = 512
VMEM = pl.BlockSpec(memory_space=pltpu.VMEM)
SMEM = pl.BlockSpec(memory_space=pltpu.SMEM)


def dot(left, right, dims):
    return lax.dot_general(left, right, (dims, ((), ())), preferred_element_type=F32)


def shape(*dims, kind=BF):
    return jax.ShapeDtypeStruct(dims, kind)


def whole_call(kernel, name, micros, out_shape, *args, scalars=0, mib=24):
    many = isinstance(out_shape, (list, tuple))
    return pl.pallas_call(
        kernel,
        out_shape=out_shape,
        in_specs=[SMEM] * scalars + [VMEM] * (len(args) - scalars),
        out_specs=[VMEM] * len(out_shape) if many else VMEM,
        compiler_params=pltpu.CompilerParams(vmem_limit_bytes=mib * MIB),
        cost_estimate=pl.CostEstimate(
            flops=0, bytes_accessed=int(micros * 3.0e6), transcendentals=0
        ),
        name=name,
    )(*args)


def pack_kernel(sub, me_ref, x_ref, cot_ref, bias_ref, send_ref, hub_ref, first_ref, *out_refs):
    groups, chunks, _, piece = first_ref.shape
    n = x_ref.shape[0] // sub
    bias = bias_ref[...]
    high = bias.astype(BF).astype(F32)
    row = lax.broadcasted_iota(jnp.int32, (sub, piece), 0)
    tail = jnp.where(row == 0, high, jnp.where(row == 1, bias - high, 0.0)).astype(BF)
    for b in range(groups):
        cols = slice(b * piece, (b + 1) * piece)
        first_ref[b, :n] = x_ref[:, cols].reshape(n, sub, piece)
        first_ref[b, n : 2 * n] = cot_ref[:, cols].reshape(n, sub, piece)
        first_ref[b, 2 * n] = tail
    x = x_ref[...]
    rows = lax.broadcasted_iota(jnp.int32, (x.shape[1], T), 0)
    readers = len(out_refs)
    for q in range(readers + 1):
        idx = send_ref[pl.ds(me_ref[0] ^ q, 1), :] if q < readers else hub_ref[...]
        hot = (rows == idx).astype(F32).astype(BF)
        got = dot(x, hot, ((1,), (0,))).astype(BF)
        if q < readers:
            out_refs[q][:, :T] = got
        else:
            for r in range(readers):
                out_refs[r][:, T:] = got


def pack(me, x, cot, bias, sends, hubs, sub, n_feat):
    n_dom = sends.shape[0]
    rows = x.shape[0]
    args = (x, cot, bias, sends, hubs)
    outs = [shape(n_feat, 2 * n_dom + 1, sub, cot.shape[1] // n_feat)]
    outs += [shape(rows, 2 * T)] * n_dom
    return pl.pallas_call(
        functools.partial(pack_kernel, sub),
        out_shape=outs,
        grid=(1,),
        in_specs=[SMEM] + [pl.BlockSpec(a.shape, lambda i, n=a.ndim: (0,) * n) for a in args],
        out_specs=[pl.BlockSpec(o.shape, lambda i, n=len(o.shape): (0,) * n) for o in outs],
        compiler_params=pltpu.CompilerParams(vmem_limit_bytes=60 * MIB),
        cost_estimate=pl.CostEstimate(flops=0, bytes_accessed=12000000, transcendentals=0),
        name="pack",
    )(me, *args)


def build_kernel(n_own, order_ref, start_ref, x_ref, vals_hbm, *refs):
    *halo_refs, own_ref, ext_ref, agg_ref, vals, sems = refs
    step = pl.program_id(0)
    slots = vals_hbm.shape[0]
    n_src = n_own + ext_ref.shape[1] // T
    tiles, wide = own_ref.shape[1] // T, own_ref.shape[2]
    chunks = sems.shape[0]
    per = slots // chunks

    def piece(i):
        span = pl.ds(i * per, per)
        return pltpu.make_async_copy(vals_hbm.at[span], vals.at[span], sems.at[i])

    @pl.when(step == 0)
    def _():
        for i in range(chunks):
            piece(i).start()
        vals[slots] = jnp.zeros((T, T), BF)
        for i in range(chunks):
            piece(i).wait()

    for v in range(tiles):
        rows = slice(v * T, (v + 1) * T)
        for s in range(n_src):
            p = (step * tiles + v) * n_src + s
            first, last = start_ref[p], start_ref[p + 1]
            one = jnp.where(last > first, order_ref[first], slots)
            two = jnp.where(last > first + 1, order_ref[first + 1], slots)
            total = vals[one].astype(F32) + vals[two].astype(F32)

            def more(i, total):
                return total + vals[order_ref[i]].astype(F32)

            total = lax.fori_loop(first + 2, last, more, total).astype(BF)
            if s < n_own:
                at = s * T % wide
                own_ref[s * T // wide, rows, at : at + T] = total
            else:
                ext_ref[rows, (s - n_own) * T : (s - n_own + 1) * T] = total
    halo = jnp.concatenate([r[...] for r in halo_refs], axis=1)
    total = 0.0
    for b in range(own_ref.shape[0]):
        total += dot(x_ref[:, b * wide : (b + 1) * wide], own_ref[b], ((1,), (1,)))
    total = (total + dot(halo, ext_ref[...], ((1,), (1,)))).astype(BF)
    piece_n = agg_ref.shape[2]
    for b in range(agg_ref.shape[0]):
        agg_ref[b] = total[:, b * piece_n : (b + 1) * piece_n]


def build_dense(vals, order, start, x, halos, n_dst, n_src, n_own, n_feat):
    rows = x.shape[0]
    piece = n_dst * T // n_feat
    ext = (n_src - n_own) * T
    return pl.pallas_call(
        functools.partial(build_kernel, n_own),
        out_shape=(
            shape(n_own * T // WIDE, n_dst * T, WIDE),
            shape(n_dst * T, ext),
            shape(n_feat, rows, piece),
        ),
        grid_spec=pltpu.PrefetchScalarGridSpec(
            num_scalar_prefetch=2,
            grid=(n_dst // 2,),
            in_specs=[VMEM, pl.BlockSpec(memory_space=pl.ANY)] + [VMEM] * len(halos),
            out_specs=[
                pl.BlockSpec((n_own * T // WIDE, 2 * T, WIDE), lambda u, *_: (0, u, 0)),
                pl.BlockSpec((2 * T, ext), lambda u, *_: (u, 0)),
                pl.BlockSpec((2 * T // piece, rows, piece), lambda u, *_: (u, 0, 0)),
            ],
            scratch_shapes=[
                pltpu.VMEM((vals.shape[0] + 1, T, T), BF),
                pltpu.SemaphoreType.DMA((8,)),
            ],
        ),
        compiler_params=pltpu.CompilerParams(vmem_limit_bytes=58 * MIB),
        cost_estimate=pl.CostEstimate(flops=0, bytes_accessed=30000000, transcendentals=0),
        name="build_dense",
    )(order, start, x, vals, *halos)


def split_kernel(blocks, n_dom, me_ref, block_ref, first_ref, bias_ref, *out_refs):
    _, _, sub, piece = first_ref.shape
    n = (first_ref.shape[1] - 1) // 2
    small = len(blocks) * sub
    width = len(blocks) * n * sub
    x = first_ref[:, :n].reshape(width, piece)
    row = lax.broadcasted_iota(jnp.int32, (sub, piece), 0) + me_ref[0] * sub
    lane = lax.broadcasted_iota(jnp.int32, (sub, piece), 1)
    for i, k in enumerate(blocks):
        b = block_ref[0] ^ k
        both = first_ref[b, 2 * n, 0:1].astype(F32) + first_ref[b, 2 * n, 1:2].astype(F32)
        mine = jnp.sum(jnp.where(row == lane, both, 0.0), axis=1, keepdims=True)
        bias_ref[i * sub : (i + 1) * sub, :] = jnp.broadcast_to(mine, (sub, T))
    even, odd = out_refs[0], out_refs[1]
    even[small:] = x
    odd[:width] = x
    for i, k in enumerate(blocks):
        b = block_ref[0] ^ k
        even[i * sub : (i + 1) * sub] = first_ref[b, n + me_ref[0]]
        odd[width + i * sub : width + (i + 1) * sub] = first_ref[b, n + (me_ref[0] ^ 1)]
    for j in range(1, n_dom // 2):
        ref = out_refs[1 + j]
        ref[small : small + width] = x
        for i, k in enumerate(blocks):
            b = block_ref[0] ^ k
            at = small + width + i * sub
            ref[i * sub : (i + 1) * sub] = first_ref[b, n + (me_ref[0] ^ (2 * j))]
            ref[at : at + sub] = first_ref[b, n + (me_ref[0] ^ (2 * j + 1))]


def weights(refs):
    return [jnp.concatenate([r[g, m] for r in refs for g in range(r.shape[0])]) for m in (0, 1)]


def dense_kernel(ny, nw, bias_ref, *refs):
    w_refs, refs = refs[:nw], refs[nw:]
    even, odd, agg = refs[:ny], refs[ny : 2 * ny], refs[2 * ny : 4 * ny]
    g_ref, act_even, act_odd, gagg_even, gagg_odd = refs[4 * ny :]
    w_self, w_neigh = weights(w_refs)
    small, width = w_self.shape
    bias = bias_ref[:, :1]
    for k in range(2 * ny):
        j = k // 2
        if k % 2 == 0:
            cot, x = even[j][:small, :], even[j][small : small + width, :]
            act_ref, gagg_ref = act_even, gagg_even
        else:
            x, cot = odd[j][:width, :], odd[j][width:, :]
            act_ref, gagg_ref = act_odd, gagg_odd
        pre = dot(w_self, x, ((1,), (0,)))
        pre += dot(w_neigh, agg[k][...], ((1,), (0,)))
        pre += bias
        sig = 1.0 / (1.0 + jnp.exp(-pre))
        act_ref[j] = (pre * sig).astype(BF)
        grad = (cot.astype(F32) * sig * (1.0 + pre * (1.0 - sig))).astype(BF)
        g_ref[k] = grad
        gagg_ref[j] = dot(w_neigh, grad, ((0,), (0,))).astype(BF)


def grads_kernel(ny, nw, g_ref, act_even, act_odd, *refs):
    w_refs, refs = refs[:nw], refs[nw:]
    even, odd, agg = refs[:ny], refs[ny : 2 * ny], refs[2 * ny : 4 * ny]
    back_even, back_odd, *out_refs = refs[4 * ny :]
    w_self, _ = weights(w_refs)
    small, width = w_self.shape
    sub = out_refs[0].shape[1]
    xs = []
    for k in range(2 * ny):
        j = k // 2
        act_ref, back_ref = (act_odd, back_odd) if k % 2 else (act_even, back_even)
        back_ref[j, :width] = dot(w_self, g_ref[k], ((0,), (0,))).astype(BF)
        back_ref[j, width:] = act_ref[j]
        xs.append(odd[j][:width, :] if k % 2 else even[j][small : small + width, :])
    grad = jnp.concatenate([g_ref[k] for k in range(2 * ny)], axis=1)
    own = dot(grad, jnp.concatenate(xs, axis=1), ((1,), (1,))).astype(BF)
    neigh = dot(grad, jnp.concatenate([r[...] for r in agg], axis=1), ((1,), (1,))).astype(BF)
    total = jnp.sum(grad.astype(F32), axis=1, keepdims=True)
    high = total.astype(BF).astype(F32)
    lane = lax.broadcasted_iota(jnp.int32, (small, T), 1)
    both = jnp.where(lane == 0, high, jnp.where(lane == 1, total - high, 0.0)).astype(BF)
    nz = out_refs[0].shape[0]
    for i in range(small // sub):
        rows, out_ref = slice(i * sub, (i + 1) * sub), out_refs[i // nz]
        out_ref[i % nz, :, :width] = own[rows]
        out_ref[i % nz, :, width : 2 * width] = neigh[rows]
        out_ref[i % nz, :, 2 * width :] = both[rows]


def pair_kernel(even_ref, got_ref, *out_refs):
    for j, out_ref in enumerate(out_refs):
        out_ref[...] = (even_ref[j].astype(F32) + got_ref[j].astype(F32)).astype(BF)


def back_pair_kernel(width, even_ref, got_ref, *out_refs):
    for j, out_ref in enumerate(out_refs):
        both = even_ref[j, :width].astype(F32) + got_ref[j, :width].astype(F32)
        small = even_ref.shape[1] - width
        out_ref[:width] = both.astype(BF)
        out_ref[width : width + small] = even_ref[j, width:]
        out_ref[width + small :] = got_ref[j, width:]


def back_pack_kernel(blocks, me_ref, block_ref, *refs):
    *in_refs, out_ref = refs
    groups, chunks, sub, piece = out_ref.shape
    n = chunks // 2
    width = groups * n * sub
    small = groups * sub
    total = in_refs[0][:width].astype(F32)
    for r in in_refs[1:]:
        total += r[:width].astype(F32)
    out_ref[:, :n] = total.astype(BF).reshape(groups, n, sub, piece)
    for k in range(2 * len(in_refs)):
        d = me_ref[0] ^ k
        for i, f in enumerate(blocks):
            at = width + (k % 2) * small + i * sub
            out_ref[block_ref[0] ^ f, n + d] = in_refs[k // 2][at : at + sub]


def wsum_kernel(width, *refs):
    *in_refs, out_ref = refs
    total = in_refs[0][...].astype(F32)
    for r in in_refs[1:]:
        total += r[...].astype(F32)
    out_ref[:, : 2 * width] = total[:, : 2 * width].astype(BF)
    bias = jnp.sum(total[:, 2 * width :], axis=1, keepdims=True)
    high = bias.astype(BF).astype(F32)
    lane = lax.broadcasted_iota(jnp.int32, (total.shape[0], T), 1)
    both = jnp.where(lane == 0, high, jnp.where(lane == 1, bias - high, 0.0))
    out_ref[:, 2 * width :] = both.astype(BF)


def wout_kernel(me_ref, *refs):
    *in_refs, self_ref, neigh_ref, bias_ref = refs
    width = self_ref.shape[2]
    for k, ref in enumerate(in_refs):
        d = me_ref[0] ^ k
        self_ref[d] = ref[:, :width].astype(F32)
        neigh_ref[d] = ref[:, width : 2 * width].astype(F32)
        total = jnp.sum(ref[:, 2 * width :].astype(F32), axis=1, keepdims=True)
        bias_ref[d] = jnp.broadcast_to(total, bias_ref.shape[1:])


def halo_grad_kernel(ga_ref, ext_ref, flat_ref, *out_refs):
    ga = jnp.concatenate([ga_ref[b] for b in range(ga_ref.shape[0])], axis=1)
    flat_ref[...] = ga
    for k, out_ref in enumerate(out_refs):
        span = slice(k * 2 * T, (k + 1) * 2 * T)
        out_ref[...] = dot(ga, ext_ref[:, span], ((1,), (0,))).astype(BF)


def add_returned(total, at, me_ref, send_ref, hub_ref, ret_refs):
    rows = lax.broadcasted_iota(jnp.int32, (total.shape[1], T), 0) + at
    hub = (rows == hub_ref[...]).astype(F32).astype(BF)
    hots, cols, hubs = [], [], 0.0
    for q, ret_ref in enumerate(ret_refs):
        idx = send_ref[pl.ds(me_ref[0] ^ q, 1), :]
        hots.append((rows == idx).astype(F32).astype(BF))
        cols.append(ret_ref[:, :T])
        hubs += ret_ref[:, T:].astype(F32)
    high = hubs.astype(BF)
    cols += [high, (hubs - high.astype(F32)).astype(BF)]
    hots += [hub, hub]
    return total + dot(jnp.concatenate(cols, axis=1), jnp.concatenate(hots, axis=1), ((1,), (1,)))


SPLIT = 4


def times_owned(ga_ref, own_refs):
    depth = own_refs[0].shape[0]
    total = 0.0
    for r, ref in enumerate(own_refs):
        total += dot(ga_ref[:, r * depth : (r + 1) * depth], ref[...], ((1,), (0,)))
    return total


def finish_rest_kernel(me_ref, ga_ref, send_ref, hub_ref, *refs):
    own_refs, ret_refs, out_ref = refs[:SPLIT], refs[SPLIT:-1], refs[-1]
    at = pl.program_id(0) * out_ref.shape[1]
    total = times_owned(ga_ref, own_refs)
    out_ref[...] = add_returned(total, at, me_ref, send_ref, hub_ref, ret_refs)


def finish_dst_kernel(back_ref, grads_ref, out_ref, act_ref):
    rows = out_ref.shape[0]
    groups = range(back_ref.shape[0])
    own = jnp.concatenate([back_ref[b, :rows] for b in groups], axis=1).astype(F32)
    act_ref[...] = jnp.concatenate([back_ref[b, rows:] for b in groups], axis=1)
    out_ref[...] = grads_ref[...] + own


def column(rows, first):
    return pl.BlockSpec((rows, WIDE), lambda i: (0, i + first))


def row_blocks(n_dst, first):
    block = (None, n_dst // SPLIT, WIDE)
    return [pl.BlockSpec(block, lambda i, r=r: (i + first, r, 0)) for r in range(SPLIT)]


def fixed(x):
    return pl.BlockSpec(x.shape, lambda i: (0, 0))


def finish_rest(me, ga, own, ret, sends, hubs, n_dst):
    rows, n = ga.shape[0], own.shape[0] * WIDE
    return pl.pallas_call(
        finish_rest_kernel,
        out_shape=shape(rows, n, kind=F32),
        grid=(n // WIDE,),
        in_specs=[SMEM, fixed(ga), fixed(sends), fixed(hubs)]
        + row_blocks(n_dst, 0)
        + [fixed(r) for r in ret],
        out_specs=column(rows, 0),
        compiler_params=pltpu.CompilerParams(vmem_limit_bytes=56 * MIB),
        cost_estimate=pl.CostEstimate(flops=0, bytes_accessed=18000000, transcendentals=0),
        name="finish_rest",
    )(me, ga, sends, hubs, *[own] * SPLIT, *ret)


def finish_dst(back, grads):
    rows, n = grads.shape
    groups, _, piece = back.shape
    n_dst = groups * piece
    return pl.pallas_call(
        finish_dst_kernel,
        out_shape=[shape(rows, n, kind=F32), shape(rows, n_dst)],
        grid=(n_dst // WIDE,),
        in_specs=[
            pl.BlockSpec((WIDE // piece, 2 * rows, piece), lambda i: (i, 0, 0)),
            column(rows, 0),
        ],
        out_specs=[column(rows, 0), column(rows, 0)],
        input_output_aliases={1: 0},
        compiler_params=pltpu.CompilerParams(vmem_limit_bytes=56 * MIB),
        cost_estimate=pl.CostEstimate(flops=0, bytes_accessed=6000000, transcendentals=0),
        name="finish_dst",
    )(back, grads)


def body(
    node_feats,
    send_rows,
    hub_rows,
    tile_dst,
    tile_src,
    tile_count,
    tile_vals,
    w_self,
    w_neigh,
    bias_vec,
    cotangent,
):
    n_dom = lax.axis_size("dom")
    n_feat = lax.axis_size("feat")
    ny, nz = n_dom // 2, n_feat // 2
    rows = node_feats.shape[0]
    own_rows = node_feats.shape[1]
    dst_rows = cotangent.shape[1]
    width = w_self.shape[1]
    n_own, n_dst = own_rows // T, dst_rows // T
    n_src = n_own + 2 * n_dom
    piece = dst_rows // n_feat
    sub = w_self.shape[0] // n_dom
    small = n_feat * sub
    me = lax.axis_index("dom")
    block = lax.axis_index("feat")
    me_s, block_s = me.reshape(1), block.reshape(1)

    def over_dom(x, k):
        return lax.ppermute(x, "dom", [(i, i ^ k) for i in range(n_dom)])

    def over_feat(x, k):
        return lax.ppermute(x, "feat", [(i, i ^ k) for i in range(n_feat)])

    def after(x, *events):
        return lax.optimization_barrier((x, events))[0]

    mine = jnp.stack(
        [
            lax.dynamic_slice_in_dim(w_self, me * sub, sub, axis=0),
            lax.dynamic_slice_in_dim(w_neigh, me * sub, sub, axis=0),
        ]
    )
    w, blocks = [mine[None]], [0]
    for bit in [1 << i for i in range(n_feat.bit_length() - 2, 0, -1)]:
        send = w[0] if len(w) == 1 else jnp.concatenate(w, axis=0)
        w.append(over_feat(send, bit))
        blocks += [k ^ bit for k in blocks]
    blocks += [k ^ 1 for k in blocks]

    sends, hubs = send_rows.reshape(n_dom, T), hub_rows[None, :]
    first, *outgoing = pack(
        me_s, node_feats, cotangent, bias_vec[None, :], sends, hubs, sub, n_feat
    )
    first = after(first, w[1])
    first = lax.all_to_all(first, "feat", 0, 0, tiled=True)
    incoming = [outgoing[0]] + [over_dom(outgoing[k], k) for k in range(1, n_dom)]

    halo_tile = n_own + 2 * ((tile_src - n_own) ^ me)
    hub_tile = n_own + 2 * ((tile_src - n_own - n_dom) ^ me) + 1
    place = jnp.where(
        tile_src < n_own, tile_src, jnp.where(tile_src < n_own + n_dom, halo_tile, hub_tile)
    )
    n_pos = n_dst * n_src
    slot = jnp.arange(tile_dst.shape[0], dtype=jnp.int32)
    key = jnp.where(slot < tile_count[0], tile_dst * n_src + place, n_pos)
    before = (key[None, :] < key[:, None]) | (
        (key[None, :] == key[:, None]) & (slot[None, :] < slot[:, None])
    )
    rank = jnp.sum(before.astype(jnp.int32), axis=1)
    order = jnp.sum(jnp.where(rank[:, None] == slot[None, :], slot[:, None], 0), axis=0)
    order = jnp.concatenate([order, jnp.zeros((2,), jnp.int32)])
    ends = jnp.arange(n_pos + 1, dtype=jnp.int32)
    start = jnp.sum((key[None, :] < ends[:, None]).astype(jnp.int32), axis=1)
    a_own, a_ext, agg = build_dense(
        tile_vals, order, start, node_feats, incoming, n_dst, n_src, n_own, n_feat
    )

    w[-1] = after(w[-1], agg)
    agg = after(agg, first)
    first = after(first, w[-1])
    w.append(over_feat(jnp.concatenate(w, axis=0), 1))
    agg = lax.all_to_all(agg, "feat", 0, 0, tiled=True).reshape(width, piece)

    bias, even, odd, *cross = whole_call(
        functools.partial(split_kernel, blocks, n_dom),
        "split",
        1.5,
        [
            shape(small, T, kind=F32),
            shape(small + width, piece),
            shape(small + width, piece),
        ]
        + [shape(2 * small + width, piece)] * (ny - 1),
        me_s,
        block_s,
        first,
        scalars=2,
    )
    cross = [over_dom(c, 2 * (j + 1)) for j, c in enumerate(cross)]
    evens = [even] + cross
    odds = [over_dom(odd, 1)] + [over_dom(c[small:], 1) for c in cross]
    agg_even = [agg] + [over_dom(agg, 2 * j) for j in range(1, ny)]
    agg_odd = [over_dom(a, 1) for a in agg_even]
    aggs = [a for pair in zip(agg_even, agg_odd) for a in pair]

    grad, act_even, act_odd, gagg_even, gagg_odd = whole_call(
        functools.partial(dense_kernel, ny, len(w)),
        "dense",
        3.0,
        [
            shape(n_dom, small, piece),
            shape(ny, small, piece),
            shape(ny, small, piece),
            shape(ny, width, piece),
            shape(ny, width, piece),
        ],
        bias,
        *w,
        *evens,
        *odds,
        *aggs,
    )

    got = over_dom(gagg_odd, 1)
    pair = whole_call(pair_kernel, "pair", 1.0, [shape(width, piece)] * ny, gagg_even, got)

    back_even, back_odd, parts, parts_odd = whole_call(
        functools.partial(grads_kernel, ny, len(w)),
        "grads",
        3.0,
        [
            shape(ny, width + small, piece),
            shape(ny, width + small, piece),
            shape(nz, sub, 2 * width + T),
            shape(nz, sub, 2 * width + T),
        ],
        grad,
        act_even,
        act_odd,
        *w,
        *evens,
        *odds,
        *aggs,
    )
    parts_odd, back_odd = after(parts_odd, pair), after(back_odd, pair)

    gagg = pair[0].astype(F32)
    for j in range(1, ny):
        gagg += over_dom(pair[j], 2 * j).astype(F32)
    gagg = gagg.astype(BF).reshape(n_feat, rows, piece)
    from_x = over_feat(parts_odd, 1)
    from_core = over_dom(back_odd, 1)
    from_x, from_core = after(from_x, gagg), after(from_core, gagg)

    gagg = lax.all_to_all(gagg, "feat", 0, 0, tiled=True)
    parts = whole_call(pair_kernel, "x_sum", 1.0, [shape(sub, 2 * width + T)] * nz, parts, from_x)
    back = whole_call(
        functools.partial(back_pair_kernel, width),
        "back_pair",
        1.0,
        [shape(width + 2 * small, piece)] * ny,
        back_even,
        from_core,
    )
    back = [back[0]] + [over_dom(back[j], 2 * j) for j in range(1, ny)]
    gagg = after(gagg, parts)
    parts = [parts[0]] + [over_feat(parts[j], blocks[j]) for j in range(1, nz)]

    gagg, *halo_grad = whole_call(
        halo_grad_kernel,
        "halo_grads",
        1.0,
        [shape(rows, dst_rows)] + [shape(rows, 2 * T)] * n_dom,
        gagg,
        a_ext,
    )
    halo_grad = after(halo_grad, back)
    returned = [halo_grad[0]] + [over_dom(halo_grad[k], k) for k in range(1, n_dom)]
    back = after(back, halo_grad, parts)

    back = whole_call(
        functools.partial(back_pack_kernel, blocks),
        "back_pack",
        1.0,
        shape(n_feat, 2 * n_dom, sub, piece),
        me_s,
        block_s,
        *back,
        scalars=2,
    )
    back = after(back, returned[2:])
    back = lax.all_to_all(back, "feat", 0, 0, tiled=True).reshape(n_feat, 2 * rows, piece)
    total = whole_call(
        functools.partial(wsum_kernel, width), "w_sum", 1.0, shape(sub, 2 * width + T), *parts
    )
    whole = [total] + [over_dom(total, 2 * j) for j in range(1, ny)]
    grads = finish_rest(me_s, gagg, a_own, returned, sends, hubs, dst_rows)
    whole[1:] = [after(e, grads) for e in whole[1:]]
    whole = [t for e in whole for t in (e, over_dom(e, 1))]
    grad_self, grad_neigh, grad_bias = whole_call(
        wout_kernel,
        "w_out",
        1.0,
        [
            shape(n_dom, sub, width, kind=F32),
            shape(n_dom, sub, width, kind=F32),
            shape(n_dom, sub, T, kind=F32),
        ],
        me_s,
        *whole,
        scalars=1,
    )

    grad_feats, activations = finish_dst(back, grads)
    return (
        activations,
        grad_feats,
        grad_self.reshape(n_dom * sub, width),
        grad_neigh.reshape(n_dom * sub, width),
        grad_bias[:, :, 0].reshape(n_dom * sub),
    )


def solution(mesh):
    return jax.shard_map(
        body,
        mesh=mesh,
        in_specs=(
            P("feat", "dom"),
            P("dom"),
            P("dom"),
            P("dom"),
            P("dom"),
            P("dom"),
            P("dom", None, None),
            P("feat", None),
            P("feat", None),
            P("feat"),
            P("feat", "dom"),
        ),
        out_specs=(P("feat", "dom"), P("feat", "dom"), P("feat", None), P("feat", None), P("feat")),
        check_vma=False,
    )
```
